32 devices in a mesh: head: 4 (over y, x), seq: 8 (over z, core).
Axes of the slice: x: 2, y: 2, z: 4, core: 2. Of those that a mesh axis runs over, the one named last changes fastest.
Arguments:
- hidden_in: bfloat16 [2, 8, 512, 1024], P(None, 'seq', 'head'), may hold values from -6 to 6
- lengths: int32 [2], replicated, may hold values from 1024 to 4096, as said below
- cotangent: bfloat16 [2, 8, 512, 1024], P(None, 'seq', 'head'), may hold values from -6 to 6
- input_gain: bfloat16 [1024], P(('head', 'seq')), may hold values from 0.25 to 1.75
- mixer_gate: bfloat16 [1024, 1536], P(('head', 'seq')), may hold values from -0.1875 to 0.1875
- mixer_inputs: bfloat16 [1024, 1536], P(('head', 'seq')), may hold values from -0.1875 to 0.1875
- state_weights: bfloat16 [1024, 256], P(('head', 'seq')), may hold values from -0.09375 to 0.09375
- conv_weight: bfloat16 [1792, 4], P(('head', 'seq')), may hold values from -3 to 3
- step_weight: bfloat16 [1024, 24], P(('head', 'seq')), may hold values from -0.5 to 0.5
- decay_log: float32 [24], replicated, may hold values from -6.2 to 0.7
- step_bias: float32 [24], replicated, may hold values from -4 to -1.5
- skip_gain: float32 [24], replicated, may hold values from 0.5 to 4
- query_weight: bfloat16 [1024, 1024], P(('head', 'seq')), may hold values from -0.4375 to 0.4375
- key_value_weight: bfloat16 [1024, 512], P(('head', 'seq')), may hold values from -0.1875 to 0.1875
- mixer_gain: bfloat16 [1536], P(('head', 'seq')), may hold values from 0.25 to 1.75
- mixer_output: bfloat16 [1536, 1024], P(('head', 'seq')), may hold values from -0.15625 to 0.15625
- attention_out: bfloat16 [1024, 1024], P(('head', 'seq')), may hold values from -0.75 to 0.75
- second_gain: bfloat16 [1024], P(('head', 'seq')), may hold values from 0.25 to 1.75
- gate_weight: bfloat16 [1024, 2048], P(('head', 'seq')), may hold values from -0.1875 to 0.1875
- up_weight: bfloat16 [1024, 2048], P(('head', 'seq')), may hold values from -0.1875 to 0.1875
- down_weight: bfloat16 [2048, 1024], P(('head', 'seq')), may hold values from -0.125 to 0.125
Outputs:
- hidden_out: float32 [2, 8, 512, 1024], P(None, 'seq', 'head')
- grad_hidden: float32 [2, 8, 512, 1024], P(None, 'seq', 'head')
- grad_input_gain: float32 [1024], P(('head', 'seq'))
- grad_mixer_gate: float32 [1024, 1536], P(('head', 'seq'))
- grad_mixer_inputs: float32 [1024, 1536], P(('head', 'seq'))
- grad_state_weights: float32 [1024, 256], P(('head', 'seq'))
- grad_conv_weight: float32 [1792, 4], P(('head', 'seq'))
- grad_step_weight: float32 [1024, 24], P(('head', 'seq'))
- grad_decay_log: float32 [24], replicated
- grad_step_bias: float32 [24], replicated
- grad_skip_gain: float32 [24], replicated
- grad_query_weight: float32 [1024, 1024], P(('head', 'seq'))
- grad_key_value_weight: float32 [1024, 512], P(('head', 'seq'))
- grad_mixer_gain: float32 [1536], P(('head', 'seq'))
- grad_mixer_output: float32 [1536, 1024], P(('head', 'seq'))
- grad_attention_out: float32 [1024, 1024], P(('head', 'seq'))
- grad_second_gain: float32 [1024], P(('head', 'seq'))
- grad_gate_weight: float32 [1024, 2048], P(('head', 'seq'))
- grad_up_weight: float32 [1024, 2048], P(('head', 'seq'))
- grad_down_weight: float32 [2048, 1024], P(('head', 'seq'))
The draws below stay inside these ranges and needn't reach their ends.
Inputs may be any that keep to these rules, and one draw needn't show every extreme that they name: `lengths`: one slot, drawn from the seed, holds a sequence of all 4096 positions.
All inputs are finite; a program needn't handle non-finite values.
Results may differ from the reference program's by a relative error of at most 0.025.
Values may be sent and summed in bfloat16 or wider, within the bound.
No kernel may reach another device: no remote copies, remote signals or barrier semaphores. Data moves between devices by JAX's collectives and lax.ppermute only.
A program may use at most 320 MiB of HBM per device.

```python
import jax
import jax.numpy as jnp
from jax import lax

D = 1024
FF = 2048
QH = 8
KVH = 2
HD = 128
MH = 24
MP = 64
NS = 128
SLOTS = 2
DI = 1536
BLK = 512
LEN = 4096
N_HEAD = 4
N_SEQ = 8


def draw_lengths(key, part):
    key = jax.random.fold_in(key, 11)
    choose_key, length_key = jax.random.split(key)
    full_slot = jax.random.randint(choose_key, (), 0, SLOTS)
    others = jax.random.randint(length_key, (SLOTS,), LEN // 4, LEN + 1)
    return jnp.where(jnp.arange(SLOTS) == full_slot, LEN, others).astype(jnp.int32)


def block_scale(rng, shape, pieces, least, high):
    def one(position, blocks):
        draws = jax.random.uniform(jax.random.fold_in(jax.random.fold_in(rng, 6), position), (blocks,), jnp.float32, least / len(pieces), high / len(pieces))
        return jnp.repeat(jnp.exp(draws), shape[position] // blocks).reshape((-1,) + (1,) * (len(shape) - position - 1))

    factor_of = one(*pieces[0])
    for cut in pieces[1:]:
        factor_of = factor_of * one(*cut)
    return factor_of


def scatter_about(rng, extent, scale, most, shards=(), kind=jnp.bfloat16):
    values = jax.random.normal(rng, extent, jnp.float32) * scale
    if len(shards) > 0:
        values = block_scale(rng, extent, shards, -0.22, 0.18) * values
    return jnp.clip(values, min=-most, max=most).astype(kind)


def setup_inputs(seed: int = 0) -> dict:
    key_of = jax.random.split(jax.random.key(seed), 22)
    hidden_in = scatter_about(key_of[0], (SLOTS, N_SEQ, BLK, D), 1.0, 6.0, ((1, 8), (2, 4)))
    lengths = draw_lengths(jax.random.fold_in(key_of[21], 71), 0)
    cotangent = scatter_about(key_of[2], (SLOTS, N_SEQ, BLK, D), 1.0, 6.0, ((1, 8), (2, 4)))
    input_gain = jnp.clip(1.0 + 0.15 * jax.random.normal(key_of[3], (D,), jnp.float32), 0.25, 1.75).astype(jnp.bfloat16)
    mixer_gate = scatter_about(key_of[4], (D, DI), D ** -0.5, 0.1875, ((0, 32),))
    mixer_inputs = scatter_about(key_of[5], (D, DI), D ** -0.5, 0.1875, ((0, 32),))
    state_weights = scatter_about(key_of[6], (D, 2 * NS), (4 * D) ** -0.5, 0.09375, ((0, 32),))
    conv_weight = scatter_about(key_of[7], (DI + 2 * NS, 4), 4 ** -0.5, 3.0, ((0, 32),))
    step_weight = scatter_about(key_of[8], (D, MH), (D // 9) ** -0.5, 0.5, ((0, 32),))
    decay_log = jnp.clip(jax.random.uniform(key_of[9], (MH,), jnp.float32, -6.2, 0.7), -6.2, 0.7)
    step_bias = jnp.clip(jax.random.uniform(key_of[10], (MH,), jnp.float32, -4.0, -1.5), -4.0, -1.5)
    skip_gain = jnp.clip(jax.random.uniform(key_of[11], (MH,), jnp.float32, 0.5, 4.0), 0.5, 4.0)
    query_weight = scatter_about(key_of[12], (D, QH * HD), (D // 6) ** -0.5, 0.4375, ((0, 32),))
    key_value_weight = scatter_about(key_of[13], (D, 2 * KVH * HD), D ** -0.5, 0.1875, ((0, 32),))
    mixer_gain = jnp.clip(1.0 + 0.15 * jax.random.normal(key_of[14], (DI,), jnp.float32), 0.25, 1.75).astype(jnp.bfloat16)
    mixer_output = scatter_about(key_of[15], (DI, D), DI ** -0.5, 0.15625, ((0, 32),))
    attention_out = scatter_about(key_of[16], (QH * HD, D), (QH * HD // 16) ** -0.5, 0.75, ((0, 32),))
    second_gain = jnp.clip(1.0 + 0.15 * jax.random.normal(key_of[17], (D,), jnp.float32), 0.25, 1.75).astype(jnp.bfloat16)
    gate_weight = scatter_about(key_of[18], (D, FF), D ** -0.5, 0.1875, ((0, 32),))
    up_weight = scatter_about(key_of[19], (D, FF), D ** -0.5, 0.1875, ((0, 32),))
    down_weight = scatter_about(key_of[20], (FF, D), FF ** -0.5, 0.125, ((0, 32),))
    return dict(hidden_in=hidden_in, lengths=lengths, cotangent=cotangent, input_gain=input_gain, mixer_gate=mixer_gate, mixer_inputs=mixer_inputs, state_weights=state_weights, conv_weight=conv_weight, step_weight=step_weight, decay_log=decay_log, step_bias=step_bias, skip_gain=skip_gain, query_weight=query_weight, key_value_weight=key_value_weight, mixer_gain=mixer_gain, mixer_output=mixer_output, attention_out=attention_out, second_gain=second_gain, gate_weight=gate_weight, up_weight=up_weight, down_weight=down_weight)


norm_eps = 1e-05
highest = lax.Precision.HIGHEST

@jax.custom_vjp
def low(v):
    return lax.optimization_barrier(v.astype(jnp.bfloat16)).astype(jnp.float32)

@jax.custom_vjp
def low_back(v):
    return v

def low_keep(v):
    return (low(v), None)

def low_pass(kept, grad):
    return (grad,)

def back_keep(v):
    return (v, None)

def back_low(kept, grad):
    return (low(grad),)
low.defvjp(low_keep, low_pass)
low_back.defvjp(back_keep, back_low)

def rms_norm(values, gain):
    return values * lax.rsqrt(lax.optimization_barrier(jnp.mean(values * values, axis=-1, keepdims=True)) + norm_eps) * gain

def matmul(left_side, right_side):
    return jnp.dot(left_side, right_side, precision=highest)

def short_conv(values, weights):
    length_rows = values.shape[0]
    padded = jnp.concatenate([jnp.zeros((3,) + values.shape[1:], jnp.float32), values], axis=0)
    total = padded[0:length_rows] * weights[:, 0]
    for tap in range(1, 4):
        total = total + padded[tap:tap + length_rows] * weights[:, tap]
    return jax.nn.silu(total)

def ssm_stretch(carried, element, rates, skip_gain):
    channels, writes, reads, step_size = element
    cumulative = jnp.cumsum(-rates[None, :] * step_size, axis=0)
    length_rows = step_size.shape[0]
    lower = jnp.arange(length_rows, dtype=jnp.int32)[:, None] >= jnp.arange(length_rows, dtype=jnp.int32)[None, :]
    gaps = cumulative[:, None, :] - cumulative[None, :, :]
    decays = jnp.exp(jnp.where(lower[:, :, None], gaps, -jnp.inf))
    mixing = jnp.einsum('thn,uhn->tuh', reads, writes, precision=highest) * decays
    within = jnp.einsum('tuh,uh,uhp->thp', mixing, step_size, channels, precision=highest)
    carried_in = jnp.exp(cumulative)[:, :, None] * jnp.einsum('thn,hpn->thp', reads, carried, precision=highest)
    weight_end = jnp.exp(cumulative[-1][None, :] - cumulative) * step_size
    renewed = jnp.exp(cumulative[-1])[:, None, None] * carried + jnp.einsum('uh,uhp,uhn->hpn', weight_end, channels, writes, precision=highest)
    return (renewed, within + carried_in + skip_gain[None, :, None] * channels)

def layer_slot(hidden, seq_length, params):
    gain_first, mixer_gate, mixer_inputs, state_weights, conv_weight, step_weight, decay_log, step_bias, skip_gain, query_weight, key_value_weight, gain_mixer, mixer_output, attention_out, gain_second, gate_weight, up_weight, down_weight = params
    positions = jnp.arange(LEN, dtype=jnp.int32)
    normed = low(rms_norm(hidden, gain_first))
    zgate = low_back(matmul(normed, mixer_gate))
    channels_pre = low_back(low(matmul(normed, mixer_inputs)))
    channels = short_conv(channels_pre, conv_weight[:MH * MP]).reshape(LEN, MH, MP)
    state_in = low_back(low(matmul(normed, state_weights)))
    state_copies = low_back(jnp.broadcast_to(state_in[:, None, :], (LEN, N_HEAD, 2 * NS)))
    state_conv = short_conv(state_copies, conv_weight[MH * MP:])
    state_heads = jnp.repeat(state_conv, MH // N_HEAD, axis=1)
    step_raw = low_back(low(matmul(normed, step_weight)))
    query = low_back(low(matmul(normed, query_weight))).reshape(LEN, QH, HD)
    key_value = low_back(low(matmul(normed, key_value_weight)))
    pairs = jnp.concatenate([key_value[:, :KVH * HD].reshape(LEN, KVH, HD), key_value[:, KVH * HD:].reshape(LEN, KVH, HD)], axis=2)
    copies = low_back(jnp.repeat(pairs, N_HEAD // KVH, axis=1))
    per_query = jnp.repeat(copies, QH // N_HEAD, axis=1)
    block_rows = min(512, LEN)

    def attend(offset):
        query_rows = lax.dynamic_slice_in_dim(query, offset, block_rows, 0)
        scores = low_back(jnp.einsum('qhd,khd->hqk', query_rows, per_query[:, :, :HD], precision=highest) * HD ** (-0.5))
        allowed = positions[None, :] <= (offset + jnp.arange(block_rows, dtype=jnp.int32))[:, None]
        probs = jax.nn.softmax(jnp.where(allowed[None], scores, -jnp.inf), axis=-1)
        return jnp.einsum('hqk,khd->qhd', low(probs), per_query[:, :, HD:], precision=highest)
    attended = lax.map(jax.checkpoint(attend), jnp.arange(LEN // block_rows, dtype=jnp.int32) * block_rows)
    attended = low_back(low(attended.reshape(LEN, QH * HD)))
    step_size = jax.nn.softplus(step_raw + step_bias[None, :])
    rates = jnp.exp(decay_log)
    stretch_rows = min(256, LEN)
    stretches = LEN // stretch_rows
    elements = (channels.reshape(stretches, stretch_rows, MH, MP), state_heads[..., :NS].reshape(stretches, stretch_rows, MH, NS), state_heads[..., NS:].reshape(stretches, stretch_rows, MH, NS), step_size.reshape(stretches, stretch_rows, MH))

    def advance(carried, element):
        return ssm_stretch(carried, element, rates, skip_gain)
    unused, mixed = lax.scan(jax.checkpoint(advance), jnp.zeros((MH, MP, NS), jnp.float32), elements)
    mixed = low_back(low(mixed.reshape(LEN, MH * MP)))
    gated = low(rms_norm(mixed * jax.nn.silu(zgate), gain_mixer))
    resid = hidden + low_back(matmul(gated, mixer_output)) + low_back(matmul(attended, attention_out))
    normed_two = low(rms_norm(resid, gain_second))
    gate_val = low_back(matmul(normed_two, gate_weight))
    up_val = low_back(matmul(normed_two, up_weight))
    acted = low(jax.nn.silu(gate_val) * up_val)
    result = resid + matmul(acted, down_weight)
    return result * (positions < seq_length).astype(jnp.float32)[:, None]

def reference(hidden_in, lengths, cotangent, input_gain, mixer_gate, mixer_inputs, state_weights, conv_weight, step_weight, decay_log, step_bias, skip_gain, query_weight, key_value_weight, mixer_gain, mixer_output, attention_out, second_gain, gate_weight, up_weight, down_weight):
    params = tuple((param.astype(jnp.float32) for param in (input_gain, mixer_gate, mixer_inputs, state_weights, conv_weight, step_weight, decay_log, step_bias, skip_gain, query_weight, key_value_weight, mixer_gain, mixer_output, attention_out, second_gain, gate_weight, up_weight, down_weight)))
    hidden = hidden_in.astype(jnp.float32).reshape(SLOTS, LEN, D)

    def forward(hidden_all, param_all):
        return jnp.stack([layer_slot(hidden_all[slot_number], lengths[slot_number], param_all) for slot_number in range(SLOTS)])
    result, pull = jax.vjp(forward, hidden, params)
    grad_hidden, grads = pull(cotangent.astype(jnp.float32).reshape(SLOTS, LEN, D))
    layout = hidden_in.shape
    return (result.reshape(layout), grad_hidden.reshape(layout), grads[0], grads[1], grads[2], grads[3], grads[4], grads[5], grads[6], grads[7], grads[8], grads[9], grads[10], grads[11], grads[12], grads[13], grads[14], grads[15], grads[16], grads[17])
```

```python
import functools

import jax
import jax.numpy as jnp
from jax import lax
from jax.experimental import pallas as pl
from jax.experimental.pallas import tpu as pltpu
from jax.sharding import PartitionSpec as P

QH = 8
KVH = 2
HD = 128
MH = 24
MP = 64
NS = 128
HEADS = 4
MIX = MH // HEADS
CH = MIX * MP
QD = QH // HEADS * HD
CONV = CH + 2 * NS
STEP_AT = CONV
QUERY_AT = STEP_AT + 128
KEY_AT = QUERY_AT + QD
REST = KEY_AT + HD
TILE = 128
PAIRS = MIX // 2

norm_eps = 1e-05
score_scale = HD ** (-0.5)
highest = lax.Precision.HIGHEST
f32 = jnp.float32
bf16 = jnp.bfloat16
NN = ((1,), (0,))
NT = ((1,), (1,))
TN = ((0,), (0,))
BIG = 1e30


def low(x):
    return x.astype(bf16)


def mul(left, right, sides=NN, precision=None):
    return lax.dot_general(
        left, right, (sides, ((), ())), preferred_element_type=f32, precision=precision
    )


def params(megabytes, **more):
    return pltpu.CompilerParams(vmem_limit_bytes=megabytes * 1024 * 1024, **more)


def iota(shape, dim):
    return lax.broadcasted_iota(jnp.int32, shape, dim)


def tile_of(g, place):
    blocks = TILE * HEADS // TILE
    return ((g % blocks) ^ place[0]) * 2 + ((g // blocks) ^ place[1])


def conv_sums(ext, taps):
    total = ext[5:133, :] * taps[0:1, :]
    for k in range(1, 4):
        total = total + ext[5 + k : 133 + k, :] * taps[k : k + 1, :]
    return total


def step_sizes(raw, heads):
    rows = iota((TILE, TILE), 0)
    cols = iota((TILE, TILE), 1)
    lower = rows >= cols
    moved = raw + heads[1:2, :]
    delta = jnp.maximum(moved, 0.0) + jnp.log1p(jnp.exp(-jnp.abs(moved)))
    cum = mul(lower.astype(f32), heads[0:1, :] * delta, precision=highest)
    return moved, delta, cum, lower


def pair_terms(p, delta, cum, cum_rows, lower, left):
    c0 = jnp.broadcast_to(cum[:, 2 * p : 2 * p + 1], (TILE, TILE))
    c1 = jnp.broadcast_to(cum[:, 2 * p + 1 : 2 * p + 2], (TILE, TILE))
    l0 = jnp.exp(jnp.where(lower, c0 - cum_rows[2 * p : 2 * p + 1, :], -BIG))
    l1 = jnp.exp(jnp.where(lower, c1 - cum_rows[2 * p + 1 : 2 * p + 2, :], -BIG))
    both = jnp.where(left, c0, c1)
    sizes = jnp.where(left, delta[:, 2 * p : 2 * p + 1], delta[:, 2 * p + 1 : 2 * p + 2])
    return l0, l1, both, sizes


def row_pair(values, p, top):
    return jnp.where(top, values[:, 2 * p : 2 * p + 1], values[:, 2 * p + 1 : 2 * p + 2])


def halves(x, left):
    return jnp.concatenate([jnp.where(left, x, 0.0), jnp.where(left, 0.0, x)], axis=0)


def mixer_forward_kernel(
    place, rest, tail, taps, heads, skip, y0, reads_out, carry_out, starts, runs, final, ending,
    ext, state, run,
):
    g = pl.program_id(0)

    @pl.when(g == 0)
    def _():
        state[...] = jnp.zeros_like(state)
        run[...] = jnp.zeros_like(run)
        ext[0:8, :] = tail[...]

    pre = rest[:, :CONV].astype(f32)
    ext[8:136, :] = pre
    total = conv_sums(ext, taps)
    act = total * jax.nn.sigmoid(total)
    ext[0:8, :] = pre[120:128, :]
    writes = low(act[:, CH : CH + NS])
    reads = low(act[:, CH + NS :])
    reads_out[...] = reads
    starts[0] = state[...]
    runs[0] = run[...]
    _, delta, cum, lower = step_sizes(rest[:, STEP_AT : STEP_AT + 128].astype(f32), heads)
    cum_rows = cum.T
    left = iota((TILE, TILE), 1) < MP
    top = iota((TILE, TILE), 0) < MP
    meet = mul(reads, writes, NT)
    run_row = run[0:1, :]
    last_row = cum[127:128, :]
    shrink = jnp.exp(last_row)
    for p in range(PAIRS):
        lanes = slice(TILE * p, TILE * (p + 1))
        l0, l1, both, sizes = pair_terms(p, delta, cum, cum_rows, lower, left)
        x = act[:, lanes]
        xd = x * sizes
        mix = jnp.concatenate([low(meet * l0), low(meet * l1)], axis=1)
        within = mul(mix, low(halves(xd, left)))
        held = state[lanes, :]
        carried = jnp.exp(both) * mul(reads, low(held), NT)
        y0[:, lanes] = within + carried + skip[0:1, lanes] * x
        carry_out[:, lanes] = jnp.exp(both + row_pair(run_row, p, left))
        ended = both[127:128, :]
        xw = low(jnp.exp(ended - both) * xd)
        state[lanes, :] = row_pair(shrink, p, top) * held + mul(xw, writes, TN)
    run[...] = run[...] + last_row
    final[...] = state[...]
    ending[...] = run[...]


def mixer_forward(place, rest, tail, taps, heads, skip):
    rows = rest.shape[0]
    tiles = rows // TILE
    fixed = lambda g, s: (0, 0)
    moved = lambda g, s: (tile_of(g, s), 0)
    by_tile = lambda g, s: (g, 0, 0)
    return pl.pallas_call(
        mixer_forward_kernel,
        grid_spec=pltpu.PrefetchScalarGridSpec(
            num_scalar_prefetch=1,
            grid=(tiles,),
            in_specs=[
                pl.BlockSpec((TILE, QUERY_AT), moved),
                pl.BlockSpec((8, CONV), fixed),
                pl.BlockSpec((8, CONV), fixed),
                pl.BlockSpec((8, 128), fixed),
                pl.BlockSpec((8, CH), fixed),
            ],
            out_specs=[
                pl.BlockSpec((TILE, CH), moved),
                pl.BlockSpec((TILE, NS), moved),
                pl.BlockSpec((TILE, CH), moved),
                pl.BlockSpec((1, CH, NS), by_tile),
                pl.BlockSpec((1, 8, 128), by_tile),
                pl.BlockSpec((CH, NS), fixed),
                pl.BlockSpec((8, 128), fixed),
            ],
            scratch_shapes=[
                pltpu.VMEM((TILE + 8, CONV), f32),
                pltpu.VMEM((CH, NS), f32),
                pltpu.VMEM((8, 128), f32),
            ],
        ),
        out_shape=[
            jax.ShapeDtypeStruct((rows, CH), f32),
            jax.ShapeDtypeStruct((rows, NS), bf16),
            jax.ShapeDtypeStruct((rows, CH), f32),
            jax.ShapeDtypeStruct((tiles, CH, NS), f32),
            jax.ShapeDtypeStruct((tiles, 8, 128), f32),
            jax.ShapeDtypeStruct((CH, NS), f32),
            jax.ShapeDtypeStruct((8, 128), f32),
        ],
        compiler_params=params(32),
        name="mixer_forward",
    )(place, rest, tail, taps, heads, skip)


def mixer_backward_kernel(
    place, rest, before, tail, taps, heads, skip, starts, runs, incoming, grad_y, grad_end,
    grad_pre, first, grad_taps, sums, grad_skip,
    ext, dext, grad_state,
):
    step = pl.program_id(0)
    g = pl.num_programs(0) - 1 - step

    @pl.when(step == 0)
    def _():
        grad_state[...] = grad_end[...]
        dext[128:136, :] = jnp.zeros((8, CONV), f32)
        grad_taps[...] = jnp.zeros_like(grad_taps)
        sums[...] = jnp.zeros_like(sums)
        grad_skip[...] = jnp.zeros_like(grad_skip)

    pre = rest[:, :CONV].astype(f32)
    ext[8:136, :] = pre
    ext[0:8, :] = jnp.where(g == 0, tail[...], before[:, :CONV].astype(f32)[8:16, :])
    total = conv_sums(ext, taps)
    gate = jax.nn.sigmoid(total)
    act = total * gate
    writes = low(act[:, CH : CH + NS])
    reads = low(act[:, CH + NS :])
    moved, delta, cum, lower = step_sizes(rest[:, STEP_AT : STEP_AT + 128].astype(f32), heads)
    cum_rows = cum.T
    rows = iota((TILE, TILE), 0)
    cols = iota((TILE, TILE), 1)
    left = cols < MP
    top = rows < MP
    meet = mul(reads, writes, NT)
    last_row = cum[127:128, :]
    shrink = jnp.exp(last_row)
    grown = jnp.exp(runs[0][0:1, :])
    grad_meet = jnp.zeros((TILE, TILE), f32)
    grad_reads = jnp.zeros((TILE, NS), f32)
    grad_writes = jnp.zeros((TILE, NS), f32)
    grad_cum = jnp.zeros((TILE, 128), f32)
    column_sums = []
    grad_x = []
    parts = [[], [], []]
    lane_row = iota((1, 128), 1)
    last_add = jnp.zeros((1, 128), f32)
    for p in range(PAIRS):
        lanes = slice(TILE * p, TILE * (p + 1))
        l0, l1, both, sizes = pair_terms(p, delta, cum, cum_rows, lower, left)
        x = act[:, lanes]
        xd = x * sizes
        xd_low = low(xd)
        dy = grad_y[:, lanes].astype(f32)
        dy_two = low(halves(dy, left))
        m0 = meet * l0
        m1 = meet * l1
        dm = mul(dy_two, xd_low, NT)
        dm0 = dm[:TILE]
        dm1 = dm[TILE:]
        grad_meet = grad_meet + dm0 * l0 + dm1 * l1
        for one, e in ((2 * p, dm0 * m0), (2 * p + 1, dm1 * m1)):
            grad_cum = grad_cum + jnp.where(cols == one, jnp.sum(e, axis=1, keepdims=True), 0.0)
            column_sums.append(jnp.sum(e, axis=0, keepdims=True))
        held = starts[0, lanes, :] + row_pair(grown, p, top) * incoming[lanes, :]
        held_low = low(held)
        ds = grad_state[lanes, :]
        ds_low = low(ds)
        ended = both[127:128, :]
        to_end = jnp.exp(ended - both)
        from_start = jnp.exp(both)
        mixed = jnp.concatenate([low(m0), low(m1)], axis=0)
        kept = to_end * mul(writes, ds_low, NT)
        dxd = mul(mixed, dy_two, TN) + kept
        grad_x.append(dxd * sizes + skip[0:1, lanes] * dy)
        parts[0].append(dy * from_start * mul(reads, held_low, NT))
        parts[1].append(kept * xd)
        parts[2].append(dxd * x)
        dy_start = low(dy * from_start)
        grad_reads = grad_reads + mul(dy_start, held_low)
        grad_writes = grad_writes + mul(low(xd * to_end), ds_low)
        grad_skip[0:1, lanes] = grad_skip[0:1, lanes] + jnp.sum(dy * x, axis=0, keepdims=True)
        product = held * ds
        for one, part in ((2 * p, product[:MP]), (2 * p + 1, product[MP:])):
            amount = jnp.sum(jnp.sum(part, axis=0, keepdims=True), axis=1, keepdims=True)
            last_add = last_add + jnp.where(lane_row == one, amount, 0.0)
        grad_state[lanes, :] = row_pair(shrink, p, top) * ds + mul(dy_start, reads, TN)
    meet_low = low(grad_meet)
    grad_reads = grad_reads + mul(meet_low, writes)
    grad_writes = grad_writes + mul(meet_low, reads, TN)
    stacked = jnp.concatenate([jnp.concatenate(part, axis=1) for part in parts], axis=0)
    pick = low(iota((CH, 128), 0) // MP == iota((CH, 128), 1))
    high_part = low(stacked)
    low_part = low(stacked - high_part.astype(f32))
    by_head = mul(high_part, pick) + mul(low_part, pick)
    carried = by_head[:TILE]
    ended_part = by_head[TILE : 2 * TILE]
    grad_delta = by_head[2 * TILE :]
    column_block = jnp.concatenate(column_sums + [jnp.zeros((TILE - MIX, TILE), f32)], axis=0)
    last_add = last_add * shrink + jnp.sum(ended_part, axis=0, keepdims=True)
    grad_cum = grad_cum + carried - ended_part - column_block.T
    grad_cum = grad_cum + jnp.where(rows == TILE - 1, last_add, 0.0)
    later = mul((rows <= cols).astype(f32), grad_cum, precision=highest)
    grad_raw = (grad_delta + heads[0:1, :] * later) * jax.nn.sigmoid(moved)
    grad_raw = jnp.where(cols < MIX, grad_raw, 0.0)
    sums[0:1, :] = sums[0:1, :] + heads[0:1, :] * jnp.sum(delta * later, axis=0, keepdims=True)
    sums[1:2, :] = sums[1:2, :] + jnp.sum(grad_raw, axis=0, keepdims=True)
    grad_act = jnp.concatenate(grad_x + [grad_writes, grad_reads], axis=1)
    grad_total = grad_act * (gate * (1.0 + total * (1.0 - gate)))
    dext[0:128, :] = grad_total
    out = dext[3:131, :] * taps[0:1, :]
    for k in range(1, 4):
        out = out + dext[3 - k : 131 - k, :] * taps[k : k + 1, :]
    for k in range(4):
        grad_taps[k : k + 1, :] = grad_taps[k : k + 1, :] + jnp.sum(
            grad_total * ext[5 + k : 133 + k, :], axis=0, keepdims=True
        )
    grad_pre[:, :CONV] = low(out)
    grad_pre[:, STEP_AT:] = low(grad_raw)
    dext[128:136, :] = grad_total[0:8, :]
    first[...] = grad_total[0:8, :]


def mixer_backward(
    place, rest, tail, taps, heads, skip, starts, runs, incoming, grad_y, grad_end
):
    rows = rest.shape[0]
    tiles = rows // TILE
    per = TILE // 16
    fixed = lambda i, s: (0, 0)
    moved = lambda i, s: (tile_of(tiles - 1 - i, s), 0)
    previous = lambda i, s: (
        tile_of(jnp.maximum(tiles - 2 - i, 0), s) * per + per - 1,
        0,
    )
    by_tile = lambda i, s: (tiles - 1 - i, 0, 0)
    return pl.pallas_call(
        mixer_backward_kernel,
        grid_spec=pltpu.PrefetchScalarGridSpec(
            num_scalar_prefetch=1,
            grid=(tiles,),
            in_specs=[
                pl.BlockSpec((TILE, QUERY_AT), moved),
                pl.BlockSpec((16, QUERY_AT), previous),
                pl.BlockSpec((8, CONV), fixed),
                pl.BlockSpec((8, CONV), fixed),
                pl.BlockSpec((8, 128), fixed),
                pl.BlockSpec((8, CH), fixed),
                pl.BlockSpec((1, CH, NS), by_tile),
                pl.BlockSpec((1, 8, 128), by_tile),
                pl.BlockSpec((CH, NS), fixed),
                pl.BlockSpec((TILE, CH), moved),
                pl.BlockSpec((CH, NS), fixed),
            ],
            out_specs=[
                pl.BlockSpec((TILE, QUERY_AT), moved),
                pl.BlockSpec((8, CONV), fixed),
                pl.BlockSpec((8, CONV), fixed),
                pl.BlockSpec((8, 128), fixed),
                pl.BlockSpec((8, CH), fixed),
            ],
            scratch_shapes=[
                pltpu.VMEM((TILE + 8, CONV), f32),
                pltpu.VMEM((TILE + 8, CONV), f32),
                pltpu.VMEM((CH, NS), f32),
            ],
        ),
        out_shape=[
            jax.ShapeDtypeStruct((rows, QUERY_AT), bf16),
            jax.ShapeDtypeStruct((8, CONV), f32),
            jax.ShapeDtypeStruct((8, CONV), f32),
            jax.ShapeDtypeStruct((8, 128), f32),
            jax.ShapeDtypeStruct((8, CH), f32),
        ],
        compiler_params=params(32),
        name="mixer_backward",
    )(place, rest, rest, tail, taps, heads, skip, starts, runs, incoming, grad_y, grad_end)


def tile_number(stored, place):
    return ((stored % 2) ^ place[1]) * HEADS + ((stored // 2) ^ place[0])


def masked(scores, place, query_tile):
    reach = iota((TILE, TILE), 0) - iota((TILE, TILE), 1)
    rows = []
    for i in range(scores.shape[0] // TILE):
        cols = []
        for j in range(scores.shape[1] // TILE):
            gap = (tile_number(query_tile + j, place) - tile_number(i, place)) * TILE
            part = scores[TILE * i : TILE * (i + 1), TILE * j : TILE * (j + 1)]
            cols.append(jnp.where(reach <= gap, part, -BIG))
        rows.append(jnp.concatenate(cols, axis=1))
    return jnp.concatenate(rows, axis=0)


def attend_kernel(diagonal, closing, place, query, mine, other, acc_in, stat_in, *outs):
    columns = query.shape[0]
    if closing:
        attended, logs = outs
    else:
        acc_out, stat_out = outs
    active = place[3] == 1
    odd = place[2] == 1
    first_tile = pl.program_id(0) * (columns // TILE)

    def one_head(j):
        keys = jnp.where(odd, other[...], mine[...])
        vals = jnp.where(odd, mine[...], other[...])
        scores = mul(keys, query[:, HD * j : HD * (j + 1)], NT) * score_scale
        if diagonal:
            scores = masked(scores, place, first_tile)
        new = jnp.max(scores, axis=0, keepdims=True)
        if not diagonal:
            old = stat_in[j, 0:1, :]
            new = jnp.maximum(new, old)
            fade = jnp.exp(old - new)
        probs = jnp.exp(scores - new)
        total = jnp.sum(probs, axis=0, keepdims=True)
        acc = mul(vals, low(probs), TN)
        if not diagonal:
            total = total + stat_in[j, 1:2, :] * fade
            acc = acc + acc_in[j] * fade
        return acc, new, total

    def put(j, acc, new, total):
        if closing:
            attended[:, HD * j : HD * (j + 1)] = low((acc / total).T)
            logs[j] = new + jnp.log(total)
        else:
            acc_out[j] = acc
            stat_out[j, 0:1, :] = new
            stat_out[j, 1:2, :] = total

    if diagonal:
        for j in range(QD // HD):
            put(j, *one_head(j))
    else:

        @pl.when(active)
        def _():
            for j in range(QD // HD):
                put(j, *one_head(j))

        @pl.when(jnp.logical_not(active))
        def _():
            for j in range(QD // HD):
                put(j, acc_in[j], stat_in[j, 0:1, :], stat_in[j, 1:2, :])


def attend(place, rest, mine, other, acc, stat, diagonal, closing, wide=256):
    rows = rest.shape[0]
    heads = QD // HD
    fixed = lambda i, s: (0, 0)
    across = lambda i, s: (0, 0, i)
    in_specs = [
        pl.BlockSpec((wide, QD), lambda i, s: (i, QUERY_AT // QD)),
        pl.BlockSpec((rows, HD), fixed),
        pl.BlockSpec((rows, HD), fixed),
        pl.BlockSpec((heads, HD, wide), across),
        pl.BlockSpec((heads, 8, wide), across),
    ]
    aliases = {}
    if closing:
        out_specs = [
            pl.BlockSpec((wide, QD), lambda i, s: (i, 0)),
            pl.BlockSpec((heads, 1, wide), across),
        ]
        out_shape = [
            jax.ShapeDtypeStruct((rows, QD), bf16),
            jax.ShapeDtypeStruct((heads, 1, rows), f32),
        ]
    else:
        out_specs = [
            pl.BlockSpec((heads, HD, wide), across),
            pl.BlockSpec((heads, 8, wide), across),
        ]
        out_shape = [
            jax.ShapeDtypeStruct((heads, HD, rows), f32),
            jax.ShapeDtypeStruct((heads, 8, rows), f32),
        ]
    args = [place, rest, mine, other, acc, stat]
    body_of = functools.partial(attend_kernel, diagonal, closing)
    if diagonal:
        in_specs = in_specs[:3]
        args = args[:4]
        full = body_of
        body_of = lambda place, query, mine, other, *outs: full(
            place, query, mine, other, None, None, *outs
        )
    return pl.pallas_call(
        body_of,
        grid_spec=pltpu.PrefetchScalarGridSpec(
            num_scalar_prefetch=1,
            grid=(rows // wide,),
            in_specs=in_specs,
            out_specs=out_specs,
        ),
        out_shape=out_shape,
        input_output_aliases=aliases,
        compiler_params=params(32),
        cost_estimate=pl.CostEstimate(
            flops=8 * rows * rows * HD, bytes_accessed=6 * rows * rows, transcendentals=0
        ),
        name="attend",
    )(*args)


def attend_back_kernel(
    diagonal, opening, place, query, grad_out, logs, terms, mine, other, *refs
):
    if opening:
        grad_query, keep, give, keys_sum, vals_sum = refs
    else:
        query_in, grad_query, keep, give, keys_sum, vals_sum = refs
    columns = query.shape[0]
    active = place[3] == 1
    odd = place[2] == 1
    step = pl.program_id(0)
    first_tile = step * (columns // TILE)

    @pl.when(step == 0)
    def _():
        keys_sum[...] = jnp.zeros_like(keys_sum)
        vals_sum[...] = jnp.zeros_like(vals_sum)

    def work():
        keys = jnp.where(odd, other[...], mine[...])
        vals = jnp.where(odd, mine[...], other[...])
        keys_add = []
        vals_add = []
        for j in range(QD // HD):
            lanes = slice(HD * j, HD * (j + 1))
            q = query[:, lanes]
            do = grad_out[:, lanes]
            scores = mul(keys, q, NT) * score_scale
            if diagonal:
                scores = masked(scores, place, first_tile)
            probs = jnp.exp(scores - logs[j])
            grad_probs = mul(vals, do, NT)
            grad_scores = low(probs * (grad_probs - terms[j]))
            vals_add.append(mul(low(probs), do))
            keys_add.append(mul(grad_scores, q))
            add = mul(grad_scores, keys, TN) * score_scale
            if opening:
                grad_query[:, lanes] = add
            else:
                grad_query[:, lanes] = query_in[:, lanes] + add
        keys_sum[...] = keys_sum[...] + sum(keys_add[1:], keys_add[0])
        vals_sum[...] = vals_sum[...] + sum(vals_add[1:], vals_add[0])

    if diagonal:
        work()
    else:
        pl.when(active)(work)

        @pl.when(jnp.logical_not(active))
        def _():
            grad_query[...] = jnp.zeros_like(grad_query) if opening else query_in[...]

    @pl.when(step == pl.num_programs(0) - 1)
    def _():
        grad_keys = low(keys_sum[...] * score_scale)
        grad_vals = low(vals_sum[...])
        keep[...] = jnp.where(odd, grad_vals, grad_keys)
        give[...] = jnp.where(odd, grad_keys, grad_vals)


def attend_back(place, rest, grad_out, logs, terms, mine, other, grad_query, diagonal, wide=256):
    rows = rest.shape[0]
    heads = QD // HD
    fixed = lambda i, s: (0, 0)
    across = lambda i, s: (0, 0, i)
    down = lambda i, s: (i, 0)
    in_specs = [
        pl.BlockSpec((wide, QD), lambda i, s: (i, QUERY_AT // QD)),
        pl.BlockSpec((wide, QD), down),
        pl.BlockSpec((heads, 1, wide), across),
        pl.BlockSpec((heads, 1, wide), across),
        pl.BlockSpec((rows, HD), fixed),
        pl.BlockSpec((rows, HD), fixed),
    ]
    args = [place, rest, grad_out, logs, terms, mine, other]
    opening = grad_query is None
    if not opening:
        in_specs.append(pl.BlockSpec((wide, QD), down))
        args.append(grad_query)
    return pl.pallas_call(
        functools.partial(attend_back_kernel, diagonal, opening),
        grid_spec=pltpu.PrefetchScalarGridSpec(
            num_scalar_prefetch=1,
            grid=(rows // wide,),
            in_specs=in_specs,
            out_specs=[
                pl.BlockSpec((wide, QD), down),
                pl.BlockSpec((rows, HD), fixed),
                pl.BlockSpec((rows, HD), fixed),
            ],
            scratch_shapes=[pltpu.VMEM((rows, HD), f32), pltpu.VMEM((rows, HD), f32)],
        ),
        out_shape=[
            jax.ShapeDtypeStruct((rows, QD), f32),
            jax.ShapeDtypeStruct((rows, HD), bf16),
            jax.ShapeDtypeStruct((rows, HD), bf16),
        ],
        compiler_params=params(32),
        cost_estimate=pl.CostEstimate(
            flops=20 * rows * rows * HD, bytes_accessed=12 * rows * rows, transcendentals=0
        ),
        name="attend_back",
    )(*args)


def to_head(x, mask):
    return lax.ppermute(x, "head", [(i, i ^ mask) for i in range(HEADS)])


def to_seq(x, mask):
    return lax.ppermute(x, "seq", [(i, i ^ mask) for i in range(lax.axis_size("seq"))])


def shifted(x, blocks):
    count = lax.axis_size("seq")
    route = [(i, i + 2 * blocks) for i in range(count) if 0 <= i + 2 * blocks < count]
    return lax.ppermute(x, "seq", route)


def gather_head(x):
    half = x.shape[0] // 2
    one = to_head(x, 1)
    two = to_head(x, 2)
    three_top = to_head(one[:half], 2)
    three_bottom = to_head(two[half:], 1)
    return jnp.concatenate([x, one, two, three_top, three_bottom], axis=0)


def add_low(*terms):
    return low(sum((t.astype(f32) for t in terms[1:]), terms[0].astype(f32)))


def scatter_head(x):
    parts = x.reshape(HEADS, 2, x.shape[0] // HEADS // 2, x.shape[1])
    first = to_head(jnp.stack([parts[1, 0], parts[3, 0]]), 1)
    second = to_head(jnp.stack([parts[2, 1], parts[3, 1]]), 2)
    top = to_head(add_low(parts[2, 0], first[1]), 2)
    bottom = to_head(add_low(parts[1, 1], second[1]), 1)
    return jnp.concatenate(
        [
            parts[0, 0].astype(f32) + first[0].astype(f32) + top.astype(f32),
            parts[0, 1].astype(f32) + second[0].astype(f32) + bottom.astype(f32),
        ],
        axis=0,
    )


def sum_head(x):
    def turned(y, mask):
        return y.reshape(HEADS, -1)[jnp.array([k ^ mask for k in range(HEADS)])].reshape(y.shape)

    received = [turned(to_head(x, mask), mask) for mask in range(1, HEADS)]
    return x + received[0] + received[1] + received[2]


def swap_tiles(x):
    rows = x.shape[0]
    tiled = x.reshape(2, 2, rows // 4, x.shape[1])
    return jnp.concatenate([tiled[:, 1:], tiled[:, :1]], axis=1).reshape(x.shape)


def gather_small(x, head_index, seq_index):
    for axis, index in (("seq", seq_index), ("head", head_index)):
        for bit in range(lax.axis_size(axis).bit_length() - 1):
            got = to_seq(x, 1 << bit) if axis == "seq" else to_head(x, 1 << bit)
            upper = (index >> bit) & 1 == 1
            x = jnp.concatenate([jnp.where(upper, got, x), jnp.where(upper, x, got)], axis=0)
    return x


def sum_all(x):
    for axis in ("seq", "head"):
        for bit in range(lax.axis_size(axis).bit_length() - 1):
            x = x + (to_seq(x, 1 << bit) if axis == "seq" else to_head(x, 1 << bit))
    return x


def state_pack(state, ending):
    total = ending[0:1, :]
    high_part = lax.reduce_precision(total, 8, 7)
    rows = jnp.concatenate([high_part, total - high_part, jnp.zeros((14, 128), f32)], axis=0)
    return jnp.concatenate([low(state), low(rows)], axis=0)


def state_sum(packed, blocks, direction):
    result = jnp.zeros((CH, NS), f32)
    passed = jnp.zeros((MIX,), f32)
    for k in range(1, blocks):
        got = shifted(packed, direction * k).astype(f32)
        factor = jnp.repeat(jnp.exp(passed), MP)[:, None]
        result = result + factor * got[:CH]
        passed = passed + got[CH, :MIX] + got[CH + 1, :MIX]
    return result


def gather_rows(shard):
    return lax.all_gather(shard, "seq", axis=0, tiled=False)


def scatter_rows(x):
    return lax.psum_scatter(x, "seq", scatter_dimension=0, tiled=False)


def exchange_columns(x):
    return lax.all_to_all(x, "head", split_axis=0, concat_axis=0, tiled=True)


def split_columns(x):
    return x.reshape(x.shape[0], HEADS, -1).swapaxes(0, 1)


def join_columns(x):
    return x.swapaxes(0, 1).reshape(x.shape[1], -1).astype(f32)


def body(
    hidden_in,
    lengths,
    cotangent,
    input_gain,
    mixer_gate,
    mixer_inputs,
    state_weights,
    conv_weight,
    step_weight,
    decay_log,
    step_bias,
    skip_gain,
    query_weight,
    key_value_weight,
    mixer_gain,
    mixer_output,
    attention_out,
    second_gain,
    gate_weight,
    up_weight,
    down_weight,
):
    seq_count = lax.axis_size("seq")
    head_index = lax.axis_index("head")
    seq_index = lax.axis_index("seq")
    block = seq_index // 2
    core = seq_index % 2
    blocks = seq_count // 2
    own_rows, features = hidden_in.shape[2], hidden_in.shape[3]
    rows = 2 * own_rows * HEADS
    shard = input_gain.shape[0]
    ff = gate_weight.shape[1] // HEADS
    mix_shard, down_shard = mixer_output.shape[0], down_weight.shape[0]
    conv_shard = conv_weight.shape[0]
    device = head_index * seq_count + seq_index

    pairs = key_value_weight.reshape(shard, 2, KVH, HD).transpose(2, 1, 0, 3)
    steps = jnp.pad(split_columns(step_weight), ((0, 0), (0, 0), (0, 128 - MIX)))
    first_pack = jnp.concatenate(
        [
            split_columns(mixer_gate),
            split_columns(mixer_inputs),
            jnp.broadcast_to(state_weights[None], (HEADS, shard, 2 * NS)),
            steps,
            split_columns(query_weight),
            pairs.reshape(HEADS, shard, HD),
        ],
        axis=2,
    )
    wide = first_pack.shape[2]
    first_all = gather_rows(exchange_columns(first_pack))
    weights_in = first_all.swapaxes(0, 1).reshape(features, wide)
    second_pack = jnp.concatenate([split_columns(gate_weight), split_columns(up_weight)], axis=2)
    out_all = gather_rows(jnp.concatenate([mixer_output, attention_out], axis=0))
    weights_out = jnp.concatenate(
        [
            out_all[:, :mix_shard].reshape(CH, features),
            out_all[:, mix_shard:].reshape(QD, features),
        ],
        axis=0,
    )
    ff_all = gather_rows(
        jnp.concatenate(
            [exchange_columns(second_pack).reshape(HEADS * shard, 2 * ff), down_weight], axis=0
        )
    )
    weights_ff = (
        ff_all[:, : HEADS * shard]
        .reshape(seq_count, HEADS, shard, 2 * ff)
        .swapaxes(0, 1)
        .reshape(features, 2 * ff)
    )
    weights_down = ff_all[:, HEADS * shard :].reshape(ff, features)

    small = jnp.concatenate([input_gain, second_gain, mixer_gain, conv_weight.reshape(-1)])
    small = gather_small(small[None], head_index, seq_index).astype(f32)
    at = 2 * shard + mix_shard
    gain_in = small[:, :shard].reshape(1, features)
    gain_two = small[:, shard : 2 * shard].reshape(1, features)
    gain_mix = lax.dynamic_slice_in_dim(
        small[:, 2 * shard : at].reshape(1, MH * MP), head_index * CH, CH, 1
    )
    taps_all = small[:, at:].reshape(MH * MP + 2 * NS, 4)
    taps = jnp.concatenate(
        [lax.dynamic_slice_in_dim(taps_all, head_index * CH, CH, 0), taps_all[MH * MP :]], axis=0
    )
    taps = jnp.pad(taps.T, ((0, 4), (0, 0)))

    both = jnp.stack([hidden_in[:, 0], cotangent[:, 0]], axis=1)
    keep = lax.dynamic_index_in_dim(both, core, 0, keepdims=False)
    give = lax.dynamic_index_in_dim(both, 1 - core, 0, keepdims=False)
    got = to_seq(give, 1)
    tokens = 2 * own_rows
    hidden = jnp.concatenate([keep[0], got[0]], axis=0).astype(f32)
    cot = jnp.concatenate([keep[1], got[1]], axis=0)
    block_rows = own_rows * HEADS
    spot = jnp.arange(tokens)
    positions = (
        (2 * block + ((spot // own_rows) ^ core)) * block_rows
        + head_index * own_rows
        + spot % own_rows
    )
    length = lax.dynamic_index_in_dim(lengths, core, 0, keepdims=False)
    valid = (positions < length).astype(f32)[:, None]
    grad_result_own = cot.astype(f32) * valid

    scale_in = lax.rsqrt(jnp.mean(hidden * hidden, axis=-1, keepdims=True) + norm_eps)
    normed = gather_head(low(hidden * scale_in * gain_in))
    grad_result = gather_head(low(grad_result_own))

    place = jnp.stack([head_index, core, head_index % 2, jnp.int32(1)]).astype(jnp.int32)
    end_row = ((head_index ^ (HEADS - 1)) * 2 + (1 ^ core)) * TILE + TILE - 16
    normed_tail = shifted(lax.dynamic_slice_in_dim(normed, end_row, 16, 0), 1)
    weights_rest = weights_in[:, CH:]
    rest = low(mul(normed, weights_rest))
    tail = low(mul(normed_tail, weights_rest[:, :CONV])).astype(f32)[8:]
    zgate = mul(normed, weights_in[:, :CH])

    mine = [rest[:, KEY_AT:]]
    for k in range(1, blocks):
        mine.append(shifted(mine[-1], 1))
    other = [swap_tiles(to_head(m, 1)) for m in mine]

    decay_part = lax.dynamic_slice_in_dim(-jnp.exp(decay_log), head_index * MIX, MIX)
    bias_part = lax.dynamic_slice_in_dim(step_bias, head_index * MIX, MIX)
    skip_part = lax.dynamic_slice_in_dim(skip_gain, head_index * MIX, MIX)
    heads = jnp.pad(jnp.stack([decay_part, bias_part]), ((0, 6), (0, 128 - MIX)))
    skip = jnp.broadcast_to(jnp.repeat(skip_part, MP)[None], (8, CH))
    y0, reads, carry, starts, runs, final, ending = mixer_forward(
        place, rest, tail, taps, heads, skip
    )
    incoming = state_sum(state_pack(final, ending), blocks, 1)

    def step_place(k):
        return place.at[3].set((block >= k).astype(jnp.int32))

    acc = stat = None
    for k in range(blocks):
        acc, stat = attend(
            step_place(k), rest, mine[k], other[k], acc, stat, k == 0, k == blocks - 1
        )
    attended, logs = acc, stat

    mixed = low(y0 + carry * mul(reads, low(incoming), NT)).astype(f32)
    gate_sig = jax.nn.sigmoid(zgate)
    silu_z = zgate * gate_sig
    inner = mixed * silu_z
    square = sum_head(jnp.sum(inner * inner, axis=1))
    scale_mix = lax.rsqrt(square / (MH * MP) + norm_eps)[:, None]
    gated = low(inner * scale_mix * gain_mix)
    branch = jnp.concatenate([gated, attended], axis=1)
    resid = hidden + scatter_head(low(mul(branch, weights_out)))

    scale_two = lax.rsqrt(jnp.mean(resid * resid, axis=-1, keepdims=True) + norm_eps)
    norm_two = resid * scale_two
    normed_two = gather_head(low(norm_two * gain_two))
    grad_acted = mul(grad_result, weights_down, NT)
    inner_ff = mul(normed_two, weights_ff)
    gate_val, up_val = inner_ff[:, :ff], inner_ff[:, ff:]
    sig = jax.nn.sigmoid(gate_val)
    silu_gate = gate_val * sig
    acted = low(silu_gate * up_val)
    grad_gate = grad_acted * up_val * (sig * (1.0 + gate_val * (1.0 - sig)))
    grad_inner = jnp.concatenate([low(grad_gate), low(grad_acted * silu_gate)], axis=1)
    grad_two = scatter_head(low(mul(grad_inner, weights_ff, NT)))
    grad_gain_two = jnp.sum(grad_two * norm_two, axis=0)
    grad_two = grad_two * gain_two
    grad_resid = grad_result_own + scale_two * (
        grad_two - norm_two * jnp.mean(grad_two * norm_two, axis=-1, keepdims=True)
    )
    grad_branch = gather_head(low(grad_resid))

    grad_ff = low(mul(normed_two, grad_inner, TN)).reshape(HEADS, seq_count, shard, 2 * ff)
    grad_down = low(mul(acted, grad_result, TN)).reshape(seq_count, down_shard, features)
    ff_sum = scatter_rows(
        jnp.concatenate(
            [grad_ff.swapaxes(0, 1).reshape(seq_count, HEADS * shard, 2 * ff), grad_down], axis=1
        )
    )
    ff_cols = exchange_columns(ff_sum[: HEADS * shard].reshape(HEADS, shard, 2 * ff))
    result = resid + scatter_head(low(mul(acted, weights_down)))
    result = result * valid

    grad_heads = mul(grad_branch, weights_out, NT)
    grad_attended = low(grad_heads[:, CH:])
    grad_gated = grad_heads[:, :CH]
    grad_out_w = low(mul(branch, grad_branch, TN))
    out_sum = scatter_rows(
        jnp.concatenate(
            [
                grad_out_w[:CH].reshape(seq_count, mix_shard, features),
                grad_out_w[CH:].reshape(seq_count, shard, features),
            ],
            axis=1,
        )
    )
    unit = inner * scale_mix
    grad_gain_mix = jnp.sum(grad_gated * unit, axis=0)
    grad_unit = grad_gated * gain_mix
    mean_mix = sum_head(jnp.sum(grad_unit * unit, axis=1))[:, None] / (MH * MP)
    grad_inner_mix = scale_mix * (grad_unit - unit * mean_mix)
    grad_mixed = low(grad_inner_mix * silu_z)
    grad_z = low(grad_inner_mix * mixed * (gate_sig * (1.0 + zgate * (1.0 - gate_sig))))

    leaving = mul(low(grad_mixed.astype(f32) * carry), reads, TN)
    grad_end = state_sum(state_pack(leaving, ending), blocks, -1)
    grad_pre, first, grad_taps, sums, grad_skip = mixer_backward(
        place, rest, tail, taps, heads, skip, starts, runs, incoming, grad_mixed, grad_end
    )
    from_next = shifted(first, -1)
    fixes = []
    for d in range(3):
        part = jnp.zeros((1, CONV), f32)
        for k in range(d + 1):
            part = part + from_next[d - k : d - k + 1] * taps[k : k + 1]
        fixes.append(part)
    fix = jnp.concatenate([jnp.zeros((13, CONV), f32)] + fixes, axis=0)
    ends = lax.dynamic_slice(grad_pre, (end_row, 0), (16, CONV))
    grad_pre = lax.dynamic_update_slice(grad_pre, low(ends.astype(f32) + fix), (end_row, 0))

    terms = jnp.sum(
        (grad_attended.astype(f32) * attended.astype(f32)).reshape(rows, QD // HD, HD), axis=2
    ).T[:, None, :]
    grad_query = None
    chain = None
    for k in reversed(range(blocks)):
        grad_query, kept, given = attend_back(
            step_place(k), rest, grad_attended, logs, terms, mine[k], other[k], grad_query, k == 0
        )
        arrived = swap_tiles(to_head(given, 1))
        if chain is None:
            chain = add_low(kept, arrived)
        else:
            chain = add_low(kept, arrived, shifted(chain, -1))
    grad_late = jnp.concatenate([low(grad_query), chain], axis=1)

    grad_early = jnp.concatenate([grad_z, grad_pre], axis=1)
    early = CH + QUERY_AT
    partial = mul(grad_early, weights_in[:, :early], NT) + mul(
        grad_late, weights_in[:, early:], NT
    )
    grad_normed = scatter_head(low(partial))
    grad_gain_in = jnp.sum(partial * normed.astype(f32), axis=0) / gain_in[0]

    def scatter_in(grads):
        piece = low(mul(normed, grads, TN)).reshape(HEADS, seq_count, shard, grads.shape[1])
        reduced = scatter_rows(piece.swapaxes(0, 1))
        return exchange_columns(reduced)

    early_cols = scatter_in(grad_early)
    late_cols = scatter_in(grad_late)

    unit_in = hidden * scale_in
    grad_normed = grad_normed * gain_in
    grad_hidden = grad_resid + scale_in * (
        grad_normed - unit_in * jnp.mean(grad_normed * unit_in, axis=-1, keepdims=True)
    )

    def back(x):
        x = x.reshape(2, own_rows, features)
        arrived = to_seq(x[1], 1)
        return jnp.stack(
            [jnp.where(core == 0, x[0], arrived), jnp.where(core == 0, arrived, x[0])]
        )[:, None]

    taps_full = lax.dynamic_update_slice_in_dim(
        jnp.zeros((4, MH * MP), f32), grad_taps[:4, :CH], head_index * CH, 1
    )
    taps_full = jnp.concatenate([taps_full, grad_taps[:4, CH:]], axis=1)
    skip_sums = jnp.sum(grad_skip[0].reshape(MIX, MP), axis=1)
    head_sums = lax.dynamic_update_slice_in_dim(
        jnp.zeros((3, MH), f32),
        jnp.stack([sums[0, :MIX], sums[1, :MIX], skip_sums]),
        head_index * MIX,
        1,
    )
    mix_full = lax.dynamic_update_slice_in_dim(
        jnp.zeros((MH * MP,), f32), grad_gain_mix, head_index * CH, 0
    )
    vector = jnp.concatenate(
        [grad_gain_two, mix_full, taps_full.T.reshape(-1), head_sums.reshape(-1)]
    )
    vector = sum_all(jnp.pad(vector, (0, -vector.shape[0] % 128)).reshape(-1, 128)).reshape(-1)
    grad_gain_in = sum_all(grad_gain_in.reshape(-1, 128)).reshape(-1)
    spot_mix = features
    spot_taps = spot_mix + MH * MP
    spot_heads = spot_taps + (MH * MP + 2 * NS) * 4
    out_heads = vector[spot_heads : spot_heads + 3 * MH].reshape(3, MH)

    def own(x, size):
        return lax.dynamic_slice_in_dim(x, device * size, size, 0)

    key_values = late_cols[:, :, QD:].reshape(KVH, 2, shard, HD).transpose(2, 1, 0, 3)
    at_state = 2 * CH
    return (
        back(result),
        back(grad_hidden),
        own(grad_gain_in, shard),
        join_columns(early_cols[:, :, :CH]),
        join_columns(early_cols[:, :, CH : 2 * CH]),
        jnp.sum(early_cols[:, :, at_state : at_state + 2 * NS].astype(f32), axis=0),
        own(vector[spot_taps:spot_heads], conv_shard * 4).reshape(conv_shard, 4),
        join_columns(early_cols[:, :, CH + STEP_AT : CH + STEP_AT + MIX]),
        out_heads[0],
        out_heads[1],
        out_heads[2],
        join_columns(late_cols[:, :, :QD]),
        key_values.reshape(shard, 2 * KVH * HD).astype(f32),
        own(vector[spot_mix:spot_taps], mix_shard),
        out_sum[:mix_shard].astype(f32),
        out_sum[mix_shard:].astype(f32),
        own(vector[:features], shard),
        join_columns(ff_cols[:, :, :ff]),
        join_columns(ff_cols[:, :, ff:]),
        ff_sum[HEADS * shard :].astype(f32),
    )


def solution(mesh):
    tokens = P(None, "seq", "head", None)
    split = P(("head", "seq"), None)
    line = P(("head", "seq"))
    whole = P()
    in_specs = (
        tokens, whole, tokens, line, split, split, split, split, split, whole, whole, whole,
        split, split, line, split, split, line, split, split, split,
    )
    out_specs = (
        tokens, tokens, line, split, split, split, split, split, whole, whole, whole, split,
        split, line, split, split, line, split, split, split,
    )
    return jax.shard_map(body, mesh=mesh, in_specs=in_specs, out_specs=out_specs, check_vma=False)
```

```python
import functools

import jax
import jax.numpy as jnp
from jax import lax
from jax.experimental import pallas as pl
from jax.experimental.pallas import tpu as pltpu
from jax.sharding import PartitionSpec as P

QH = 8
KVH = 2
HD = 128
MH = 24
MP = 64
NS = 128
HEADS = 4
MIX = MH // HEADS
CH = MIX * MP
QD = QH // HEADS * HD
CONV = CH + 2 * NS
STEP_AT = CONV
QUERY_AT = STEP_AT + 128
GATE_AT = QUERY_AT + QD
KEY_AT = GATE_AT + CH
TILE = 128
GAIN_LANE = 8
PAIRS = MIX // 2

norm_eps = 1e-05
score_scale = HD ** (-0.5)
exponent_scale = score_scale * 1.4426950408889634
highest = lax.Precision.HIGHEST
f32 = jnp.float32
bf16 = jnp.bfloat16
NN = ((1,), (0,))
NT = ((1,), (1,))
TN = ((0,), (0,))
BIG = 1e30
VMEM = 24


def low(x):
    return x.astype(bf16)


def mul(left, right, sides=NN, precision=None):
    return lax.dot_general(
        left, right, (sides, ((), ())), preferred_element_type=f32, precision=precision
    )


def params(megabytes, **more):
    return pltpu.CompilerParams(vmem_limit_bytes=megabytes * 1024 * 1024, **more)


def taking(micros):
    micros = micros * 0.02
    return pl.CostEstimate(
        flops=int(micros * 1.1e9), bytes_accessed=int(micros * 3.6e6), transcendentals=0
    )


def unread(deps):
    return [pl.BlockSpec(memory_space=pl.ANY)] * len(deps)


def iota(shape, dim):
    return lax.broadcasted_iota(jnp.int32, shape, dim)


def tile_of(g, place):
    blocks = TILE * HEADS // TILE
    return ((g % blocks) ^ place[0]) * 2 + ((g // blocks) ^ place[1])


def conv_sums(ext, taps):
    total = ext[5:133, :] * taps[0:1, :]
    for k in range(1, 4):
        total = total + ext[5 + k : 133 + k, :] * taps[k : k + 1, :]
    return total


def step_sizes(raw, heads):
    rows = iota((TILE, TILE), 0)
    cols = iota((TILE, TILE), 1)
    lower = rows >= cols
    moved = raw + heads[1:2, :]
    delta = jnp.maximum(moved, 0.0) + jnp.log1p(jnp.exp(-jnp.abs(moved)))
    cum = mul(lower.astype(f32), heads[0:1, :] * delta, precision=highest)
    return moved, delta, cum, lower


def pair_terms(p, delta, cum, cum_rows, lower, left):
    c0 = jnp.broadcast_to(cum[:, 2 * p : 2 * p + 1], (TILE, TILE))
    c1 = jnp.broadcast_to(cum[:, 2 * p + 1 : 2 * p + 2], (TILE, TILE))
    l0 = jnp.exp(jnp.where(lower, c0 - cum_rows[2 * p : 2 * p + 1, :], -BIG))
    l1 = jnp.exp(jnp.where(lower, c1 - cum_rows[2 * p + 1 : 2 * p + 2, :], -BIG))
    both = jnp.where(left, c0, c1)
    sizes = jnp.where(left, delta[:, 2 * p : 2 * p + 1], delta[:, 2 * p + 1 : 2 * p + 2])
    return l0, l1, both, sizes


def row_pair(values, p, top):
    return jnp.where(top, values[:, 2 * p : 2 * p + 1], values[:, 2 * p + 1 : 2 * p + 2])


def halves(x, left):
    return jnp.concatenate([jnp.where(left, x, 0.0), jnp.where(left, 0.0, x)], axis=0)


def tile_rows(g, place):
    return pl.ds(pl.multiple_of(tile_of(g, place) * TILE, TILE), TILE)


def pack_rows(state, total):
    high_part = low(total).astype(f32)
    rows = jnp.concatenate([high_part, total - high_part, jnp.zeros((14, 128), f32)], axis=0)
    return jnp.concatenate([low(state), low(rows)], axis=0)


def sum_packs(packs, out):
    top = iota((TILE, NS), 0) < MP
    out[...] = jnp.zeros_like(out)
    passed = jnp.zeros((1, 128), f32)
    for pack in packs:
        factor = jnp.exp(passed)
        for p in range(PAIRS):
            lanes = slice(TILE * p, TILE * (p + 1))
            out[lanes, :] = out[lanes, :] + row_pair(factor, p, top) * pack[lanes, :].astype(f32)
        ends = pack[CH : CH + 16, :].astype(f32)
        passed = passed + ends[0:1, :] + ends[1:2, :]


def mixer_forward_kernel(
    place, rest, tail, taps, heads, skip, y0, reads_out, cums, starts, runs, packed,
    ext, state, run,
):
    state[...] = jnp.zeros_like(state)
    run[...] = jnp.zeros_like(run)
    ext[0:8, :] = tail[...].astype(f32)[8:16, :]

    def one_tile(g, unused):
        here = tile_rows(g, place)
        pre = rest[here, :CONV].astype(f32)
        ext[8:136, :] = pre
        total = conv_sums(ext, taps)
        act = total * jax.nn.sigmoid(total)
        ext[0:8, :] = pre[120:128, :]
        writes = low(act[:, CH : CH + NS])
        reads = low(act[:, CH + NS :])
        reads_out[here, :] = reads
        starts[g] = low(state[...])
        runs[g] = run[...]
        _, delta, cum, lower = step_sizes(rest[here, STEP_AT:].astype(f32), heads)
        cum_rows = cum.T
        left = iota((TILE, TILE), 1) < MP
        top = iota((TILE, TILE), 0) < MP
        meet = mul(reads, writes, NT)
        run_row = run[0:1, :]
        cums[:, here] = (cum + run_row).T[0:8, :]
        last_row = cum[127:128, :]
        shrink = jnp.exp(last_row)
        for p in range(PAIRS):
            lanes = slice(TILE * p, TILE * (p + 1))
            l0, l1, both, sizes = pair_terms(p, delta, cum, cum_rows, lower, left)
            x = act[:, lanes]
            xd = x * sizes
            mix = jnp.concatenate([low(meet * l0), low(meet * l1)], axis=1)
            within = mul(mix, low(halves(xd, left)))
            held = state[lanes, :]
            carried = jnp.exp(both) * mul(reads, low(held), NT)
            y0[here, lanes] = within + carried + skip[0:1, lanes] * x
            ended = both[127:128, :]
            xw = low(jnp.exp(ended - both) * xd)
            state[lanes, :] = row_pair(shrink, p, top) * held + mul(xw, writes, TN)
        run[...] = run[...] + last_row
        return unused

    lax.fori_loop(0, rest.shape[0] // TILE, one_tile, 0)
    packed[...] = pack_rows(state[...], run[0:1, :])


def skipping(kernel, before, count):
    def run(*refs):
        kernel(*refs[:before], *refs[before + count :])

    return run


def whole_block(*shape):
    return pl.BlockSpec(shape, lambda *i: (0,) * len(shape))


def whole_call(kernel, place, args, outs, scratch, megabytes, micros, deps, name):
    count = 0 if place is None else 1
    before = len(args) + count
    specs = [whole_block(*a.shape) if hasattr(a, "shape") else a[1] for a in args]
    args = [a if hasattr(a, "shape") else a[0] for a in args]
    return pl.pallas_call(
        skipping(kernel, before, len(deps)),
        grid_spec=pltpu.PrefetchScalarGridSpec(
            num_scalar_prefetch=count,
            grid=(1,),
            in_specs=specs + unread(deps),
            out_specs=[whole_block(*o.shape) for o in outs],
            scratch_shapes=scratch,
        ),
        out_shape=outs,
        compiler_params=params(megabytes),
        cost_estimate=taking(micros),
        name=name,
    )(*([] if place is None else [place]), *args, *deps)


def like(shape, kind):
    return jax.ShapeDtypeStruct(shape, kind)


def mixer_forward(place, rest, tail, taps, heads, skip, deps=()):
    rows = rest.shape[0]
    tiles = rows // TILE
    return whole_call(
        mixer_forward_kernel,
        place,
        [rest, tail, taps, heads, skip],
        [
            like((rows, CH), f32),
            like((rows, NS), bf16),
            like((8, rows), f32),
            like((tiles, CH, NS), bf16),
            like((tiles, 8, 128), f32),
            like((CH + 16, NS), bf16),
        ],
        [
            pltpu.VMEM((TILE + 8, CONV), f32),
            pltpu.VMEM((CH, NS), f32),
            pltpu.VMEM((8, 128), f32),
        ],
        20,
        6,
        deps,
        "mixer_forward",
    )


def mixer_backward_kernel(
    count, place, rest, tail, taps, heads, skip, starts, runs, incoming, grad_y, *refs
):
    packs = refs[:count]
    grad_pre, first, grad_taps, sums, grad_skip, ext, dext, grad_state = refs[count:]
    sum_packs(packs, grad_state)
    dext[128:136, :] = jnp.zeros((8, CONV), f32)
    grad_taps[...] = jnp.zeros_like(grad_taps)
    sums[...] = jnp.zeros_like(sums)
    grad_skip[...] = jnp.zeros_like(grad_skip)
    tiles = rest.shape[0] // TILE

    def one_tile(step, unused):
        g = tiles - 1 - step
        here = tile_rows(g, place)
        before = tile_of(jnp.maximum(g - 1, 0), place) * TILE + TILE - 16
        before = rest[pl.ds(pl.multiple_of(before, 16), 16), :CONV].astype(f32)
        ext[8:136, :] = rest[here, :CONV].astype(f32)
        ext[0:8, :] = jnp.where(g == 0, tail[...].astype(f32), before)[8:16, :]
        total = conv_sums(ext, taps)
        gate = jax.nn.sigmoid(total)
        act = total * gate
        writes = low(act[:, CH : CH + NS])
        reads = low(act[:, CH + NS :])
        moved, delta, cum, lower = step_sizes(rest[here, STEP_AT:].astype(f32), heads)
        cum_rows = cum.T
        rows = iota((TILE, TILE), 0)
        cols = iota((TILE, TILE), 1)
        left = cols < MP
        top = rows < MP
        meet = mul(reads, writes, NT)
        last_row = cum[127:128, :]
        shrink = jnp.exp(last_row)
        grown = jnp.exp(runs[g][0:1, :])
        grad_meet = jnp.zeros((TILE, TILE), f32)
        grad_reads = jnp.zeros((TILE, NS), f32)
        grad_writes = jnp.zeros((TILE, NS), f32)
        row_parts = []
        column_sums = []
        grad_x = []
        parts = [[], [], []]
        lane_row = iota((1, 128), 1)
        last_add = jnp.zeros((1, 128), f32)
        for p in range(PAIRS):
            lanes = slice(TILE * p, TILE * (p + 1))
            l0, l1, both, sizes = pair_terms(p, delta, cum, cum_rows, lower, left)
            x = act[:, lanes]
            xd = x * sizes
            xd_low = low(xd)
            dy = grad_y[here, lanes].astype(f32)
            dy_two = low(halves(dy, left))
            m0 = meet * l0
            m1 = meet * l1
            dm = mul(dy_two, xd_low, NT)
            dm0 = dm[:TILE]
            dm1 = dm[TILE:]
            grad_meet = grad_meet + dm0 * l0 + dm1 * l1
            for one, e in ((2 * p, dm0 * m0), (2 * p + 1, dm1 * m1)):
                row_parts.append(e)
                column_sums.append(jnp.sum(e, axis=0, keepdims=True))
            held = starts[g, lanes, :].astype(f32) + row_pair(grown, p, top) * incoming[lanes, :]
            held_low = low(held)
            ds = grad_state[lanes, :]
            ds_low = low(ds)
            ended = both[127:128, :]
            to_end = jnp.exp(ended - both)
            from_start = jnp.exp(both)
            mixed = jnp.concatenate([low(m0), low(m1)], axis=0)
            kept = to_end * mul(writes, ds_low, NT)
            dxd = mul(mixed, dy_two, TN) + kept
            grad_x.append(dxd * sizes + skip[0:1, lanes] * dy)
            parts[0].append(dy * from_start * mul(reads, held_low, NT))
            parts[1].append(kept * xd)
            parts[2].append(dxd * x)
            dy_start = low(dy * from_start)
            grad_reads = grad_reads + mul(dy_start, held_low)
            grad_writes = grad_writes + mul(low(xd * to_end), ds_low)
            grad_skip[0:1, lanes] = grad_skip[0:1, lanes] + jnp.sum(dy * x, axis=0, keepdims=True)
            product = held * ds
            for one, part in ((2 * p, product[:MP]), (2 * p + 1, product[MP:])):
                amount = jnp.sum(jnp.sum(part, axis=0, keepdims=True), axis=1, keepdims=True)
                last_add = last_add + jnp.where(lane_row == one, amount, 0.0)
            grad_state[lanes, :] = row_pair(shrink, p, top) * ds + mul(dy_start, reads, TN)
        meet_low = low(grad_meet)
        grad_reads = grad_reads + mul(meet_low, writes)
        grad_writes = grad_writes + mul(meet_low, reads, TN)
        stacked = jnp.concatenate([jnp.concatenate(part, axis=1) for part in parts], axis=0)
        pick = low(iota((CH, 128), 0) // MP == iota((CH, 128), 1))
        high_part = low(stacked)
        low_part = low(stacked - high_part.astype(f32))
        by_head = mul(high_part, pick) + mul(low_part, pick)
        meets = jnp.concatenate(row_parts, axis=1)
        pick = low(iota((MIX * TILE, 128), 0) // TILE == iota((MIX * TILE, 128), 1))
        high_part = low(meets)
        low_part = low(meets - high_part.astype(f32))
        grad_cum = mul(high_part, pick) + mul(low_part, pick)
        carried = by_head[:TILE]
        ended_part = by_head[TILE : 2 * TILE]
        grad_delta = by_head[2 * TILE :]
        column_block = jnp.concatenate(column_sums + [jnp.zeros((TILE - MIX, TILE), f32)], axis=0)
        last_add = last_add * shrink + jnp.sum(ended_part, axis=0, keepdims=True)
        grad_cum = grad_cum + carried - ended_part - column_block.T
        grad_cum = grad_cum + jnp.where(rows == TILE - 1, last_add, 0.0)
        later = mul((rows <= cols).astype(f32), grad_cum, precision=highest)
        grad_raw = (grad_delta + heads[0:1, :] * later) * jax.nn.sigmoid(moved)
        grad_raw = jnp.where(cols < MIX, grad_raw, 0.0)
        sums[0:1, :] = sums[0:1, :] + heads[0:1, :] * jnp.sum(delta * later, axis=0, keepdims=True)
        sums[1:2, :] = sums[1:2, :] + jnp.sum(grad_raw, axis=0, keepdims=True)
        grad_act = jnp.concatenate(grad_x + [grad_writes, grad_reads], axis=1)
        grad_total = grad_act * (gate * (1.0 + total * (1.0 - gate)))
        dext[0:128, :] = grad_total
        out = dext[3:131, :] * taps[0:1, :]
        for k in range(1, 4):
            out = out + dext[3 - k : 131 - k, :] * taps[k : k + 1, :]
        for k in range(4):
            grad_taps[k : k + 1, :] = grad_taps[k : k + 1, :] + jnp.sum(
                grad_total * ext[5 + k : 133 + k, :], axis=0, keepdims=True
            )
        grad_pre[here, :CONV] = low(out)
        grad_pre[here, STEP_AT:] = low(grad_raw)
        dext[128:136, :] = grad_total[0:8, :]
        first[...] = grad_total[0:8, :]
        return unused

    lax.fori_loop(0, tiles, one_tile, 0)


def mixer_backward(
    place, rest, tail, taps, heads, skip, starts, runs, incoming, grad_y, packs, deps=()
):
    rows = rest.shape[0]
    return whole_call(
        functools.partial(mixer_backward_kernel, len(packs)),
        place,
        [rest, tail, taps, heads, skip, starts, runs, incoming, grad_y, *packs],
        [
            like((rows, QUERY_AT), bf16),
            like((8, CONV), f32),
            like((8, CONV), f32),
            like((8, 128), f32),
            like((8, CH), f32),
        ],
        [
            pltpu.VMEM((TILE + 8, CONV), f32),
            pltpu.VMEM((TILE + 8, CONV), f32),
            pltpu.VMEM((CH, NS), f32),
        ],
        24,
        13,
        deps,
        "mixer_backward",
    )


def fix_ends(place, grad_pre, from_next, taps):
    def kernel(place, grad_pre, from_next, taps, out):
        fixed = jnp.zeros((16, CONV), f32)
        rows = iota((16, CONV), 0)
        for d in range(3):
            part = from_next[0:1, :] * taps[d : d + 1, :]
            for k in range(d):
                part = part + from_next[d - k : d - k + 1, :] * taps[k : k + 1, :]
            fixed = fixed + jnp.where(rows == 13 + d, part, 0.0)
        out[:, :CONV] = low(grad_pre[:, :CONV].astype(f32) + fixed)
        out[:, CONV:] = grad_pre[:, CONV:]

    block = pl.BlockSpec((16, QUERY_AT), lambda i, s: (s[3], 0))
    return pl.pallas_call(
        kernel,
        grid_spec=pltpu.PrefetchScalarGridSpec(
            num_scalar_prefetch=1,
            grid=(1,),
            in_specs=[block, whole_block(8, CONV), whole_block(8, CONV)],
            out_specs=block,
        ),
        out_shape=like(grad_pre.shape, bf16),
        input_output_aliases={1: 0},
        compiler_params=params(8),
        cost_estimate=taking(1),
        name="fix_ends",
    )(place, grad_pre, from_next, taps)


def tile_number(stored, place):
    return ((stored % 2) ^ place[1]) * HEADS + ((stored // 2) ^ place[0])


def masked(scores, place, query_tile):
    reach = iota((TILE, TILE), 0) - iota((TILE, TILE), 1)
    rows = []
    for i in range(scores.shape[0] // TILE):
        cols = []
        for j in range(scores.shape[1] // TILE):
            gap = (tile_number(query_tile + j, place) - tile_number(i, place)) * TILE
            part = scores[TILE * i : TILE * (i + 1), TILE * j : TILE * (j + 1)]
            cols.append(jnp.where(reach <= gap, part, -BIG))
        rows.append(jnp.concatenate(cols, axis=1))
    return jnp.concatenate(rows, axis=0)


def attend_kernel(diagonal, closing, count, place, *refs):
    query, pair = refs[:2]
    refs = refs[2:]
    if not diagonal:
        acc_in, stat_in = refs[:2]
        refs = refs[2:]
    refs = refs[count:]
    if closing:
        attended, logs = refs
    else:
        acc_out, stat_out = refs
    wide = 256
    columns = query.shape[0]
    items = [
        (j, slice(wide * i, wide * (i + 1))) for i in range(columns // wide) for j in range(QD // HD)
    ]

    def put(j, cols, acc, new, total):
        if closing:
            attended[cols, HD * j : HD * (j + 1)] = low((acc / total).T)
            logs[j, :, cols] = new + jnp.log2(total)
        else:
            acc_out[j, :, cols] = acc
            stat_out[j, 0:1, cols] = new
            stat_out[j, 1:2, cols] = total

    def work():
        keys = pair[:, :HD]
        vals = pair[:, HD:]

        def start(j, cols):
            scores = mul(keys, query[cols, HD * j : HD * (j + 1)], NT)
            return masked(scores, place, cols.start // TILE) if diagonal else scores

        def weigh(scores, j, cols):
            new = jnp.max(scores, axis=0, keepdims=True) * exponent_scale
            if not diagonal:
                new = jnp.maximum(new, stat_in[j, 0:1, cols])
            probs = jnp.exp2(scores * exponent_scale - new)
            return low(probs), jnp.sum(probs, axis=0, keepdims=True), new

        def finish(probs, total, new, j, cols):
            acc = mul(vals, probs, TN)
            if not diagonal:
                fade = jnp.exp2(stat_in[j, 0:1, cols] - new)
                total = total + stat_in[j, 1:2, cols] * fade
                acc = acc + acc_in[j, :, cols] * fade
            put(j, cols, acc, new, total)

        scores = start(*items[0])
        pending = None
        for n, item in enumerate(items):
            following = start(*items[n + 1]) if n + 1 < len(items) else None
            weighed = weigh(scores, *item)
            if pending is not None:
                finish(*pending)
            pending = weighed + item
            scores = following
        finish(*pending)

    if diagonal:
        work()
    else:
        active = place[2] == 1
        pl.when(active)(work)

        @pl.when(jnp.logical_not(active))
        def _():
            for j, cols in items:
                put(j, cols, acc_in[j, :, cols], stat_in[j, 0:1, cols], stat_in[j, 1:2, cols])


def attend(place, query, pair, carried, diagonal, closing, deps=()):
    rows = query.shape[0]
    heads = QD // HD
    whole = lambda *shape: pl.BlockSpec(shape, lambda i, s: (0,) * len(shape))
    in_specs = [
        whole(rows, QD),
        whole(rows, 2 * HD),
    ]
    running = [whole(heads, HD, rows), whole(heads, 8, rows)]
    if not diagonal:
        in_specs += running
    if closing:
        out_specs = [whole(rows, QD), whole(heads, 1, rows)]
        out_shape = [
            jax.ShapeDtypeStruct((rows, QD), bf16),
            jax.ShapeDtypeStruct((heads, 1, rows), f32),
        ]
    else:
        out_specs = running
        out_shape = [
            jax.ShapeDtypeStruct((heads, HD, rows), f32),
            jax.ShapeDtypeStruct((heads, 8, rows), f32),
        ]
    return pl.pallas_call(
        functools.partial(attend_kernel, diagonal, closing, len(deps)),
        grid_spec=pltpu.PrefetchScalarGridSpec(
            num_scalar_prefetch=1,
            grid=(1,),
            in_specs=in_specs + unread(deps),
            out_specs=out_specs,
        ),
        out_shape=out_shape,
        compiler_params=params(16),
        cost_estimate=taking(5),
        name="attend",
    )(place, query, pair, *(() if diagonal else carried), *deps)


def attend_back_kernel(diagonal, opening, count, place, *refs):
    query, grad_out, logs, terms, pair = refs[:5]
    refs = refs[5:]
    if not opening:
        grad_in = refs[0]
        refs = refs[1:]
    grad_query, grad_pair = refs[count:]
    wide = 512

    def work():
        keys = pair[:, :HD]
        vals = pair[:, HD:]
        keys_sum = None
        for i in range(query.shape[0] // wide):
            cols = slice(wide * i, wide * (i + 1))
            for j in range(QD // HD):
                lanes = slice(HD * j, HD * (j + 1))
                q = query[cols, lanes]
                do = grad_out[cols, lanes]
                scores = mul(keys, q, NT)
                if diagonal:
                    scores = masked(scores, place, cols.start // TILE)
                probs = jnp.exp2(scores * exponent_scale - logs[j, :, cols])
                grad_probs = mul(vals, do, NT)
                grad_scores = low(probs * (grad_probs - terms[j, :, cols]))
                vals_add = mul(low(probs), do)
                keys_add = mul(grad_scores, q)
                add = mul(keys, grad_scores, TN)
                if not opening:
                    add = add + grad_in[j, :, cols]
                if diagonal:
                    grad_query[cols, lanes] = low((add * score_scale).T)
                else:
                    grad_query[j, :, cols] = add
                if keys_sum is None:
                    keys_sum, vals_sum = keys_add, vals_add
                else:
                    keys_sum, vals_sum = keys_sum + keys_add, vals_sum + vals_add
        grad_pair[:, :HD] = low(keys_sum * score_scale)
        grad_pair[:, HD:] = low(vals_sum)

    if diagonal:
        work()
    else:
        active = place[2] == 1
        pl.when(active)(work)

        @pl.when(jnp.logical_not(active))
        def _():
            grad_query[...] = jnp.zeros_like(grad_query) if opening else grad_in[...]
            grad_pair[...] = jnp.zeros_like(grad_pair)


def attend_back(place, query, grad_out, logs, terms, pair, grad_query, diagonal, deps=()):
    rows = query.shape[0]
    heads = QD // HD
    whole = lambda *shape: pl.BlockSpec(shape, lambda i, s: (0,) * len(shape))
    in_specs = [
        whole(rows, QD),
        whole(rows, QD),
        whole(heads, 1, rows),
        whole(heads, 1, rows),
        whole(rows, 2 * HD),
    ]
    args = [place, query, grad_out, logs, terms, pair]
    opening = grad_query is None
    if not opening:
        in_specs.append(whole(heads, HD, rows))
        args.append(grad_query)
    if diagonal:
        query_spec = whole(rows, QD)
        query_shape = jax.ShapeDtypeStruct((rows, QD), bf16)
    else:
        query_spec = whole(heads, HD, rows)
        query_shape = jax.ShapeDtypeStruct((heads, HD, rows), f32)
    return pl.pallas_call(
        functools.partial(attend_back_kernel, diagonal, opening, len(deps)),
        grid_spec=pltpu.PrefetchScalarGridSpec(
            num_scalar_prefetch=1,
            grid=(1,),
            in_specs=in_specs + unread(deps),
            out_specs=[query_spec, whole(rows, 2 * HD)],
        ),
        out_shape=[
            query_shape,
            jax.ShapeDtypeStruct((rows, 2 * HD), bf16),
        ],
        compiler_params=params(VMEM),
        cost_estimate=taking(7),
        name="attend_back",
    )(*args, *deps)


def ring(i):
    j = (i + 1) % HEADS
    return j ^ (j // 2)


def load_piece(i, pieces, held, which=None):
    half = pieces[0].shape[-2]
    if which is not None:
        pieces = [p.at[which] for p in pieces]
    for at, k in enumerate((1, 3, 2, 0)):

        @pl.when(i == at)
        def _(k=k):
            held[:half, :] = pieces[2 * k][...]
            held[half:, :] = pieces[2 * k + 1][...]

    return held[...]


def piece_specs(pieces):
    return [fixed_block(*p.shape) for p in pieces]


def put_scatter(i, value, refs):
    send_one, send_two, keep_one, keep_two, own = refs
    half = keep_one.shape[0]
    top, bottom = low(value[:half]), low(value[half:])

    @pl.when(i == 0)
    def _():
        send_one[0] = top
        keep_two[...] = bottom

    @pl.when(i == 1)
    def _():
        send_one[0] = top
        send_two[0] = bottom

    @pl.when(i == 2)
    def _():
        keep_one[...] = top
        send_two[0] = bottom

    @pl.when(i == 3)
    def _():
        own[...] = value


def scatter_outs(half, columns):
    specs = [
        pl.BlockSpec((1, half, columns), lambda i: (jnp.minimum(i, 1), 0, 0)),
        pl.BlockSpec((1, half, columns), lambda i: (jnp.clip(i - 1, 0, 1), 0, 0)),
        pl.BlockSpec((half, columns), lambda i: (0, 0)),
        pl.BlockSpec((half, columns), lambda i: (0, 0)),
        pl.BlockSpec((2 * half, columns), lambda i: (0, 0)),
    ]
    shapes = [
        jax.ShapeDtypeStruct((2, half, columns), bf16),
        jax.ShapeDtypeStruct((2, half, columns), bf16),
        jax.ShapeDtypeStruct((half, columns), bf16),
        jax.ShapeDtypeStruct((half, columns), bf16),
        jax.ShapeDtypeStruct((2 * half, columns), f32),
    ]
    return specs, shapes


def scatter_parts(parts):
    send_one, send_two, keep_one, keep_two, own = parts
    first = to_head(send_one, 1)
    second = to_head(send_two, 2)
    top = to_head(add_low(keep_one, first[1]), 2)
    bottom = to_head(add_low(keep_two, second[0]), 1)
    half = keep_one.shape[0]
    return jnp.concatenate(
        [
            own[:half] + first[0].astype(f32) + top.astype(f32),
            own[half:] + second[1].astype(f32) + bottom.astype(f32),
        ],
        axis=0,
    )


def by_ring(*block):
    return pl.BlockSpec(block, lambda i: (ring(i), 0))


def row_sums(x):
    ones = jnp.ones((8, x.shape[1]), bf16)
    high_part = low(x)
    low_part = low(x - high_part.astype(f32))
    return (mul(ones, high_part, NT) + mul(ones, low_part, NT))[0:1, :]


def column_of(row, width):
    column = jnp.broadcast_to(row, (128, row.shape[1])).T
    return jnp.concatenate([column] * (width // 128), axis=1)


def fixed_block(*shape):
    return pl.BlockSpec(shape, lambda i: (0,) * len(shape), pipeline_mode=pl.Buffered(1))


def tiled_call(kernel, steps, in_specs, out_specs, out_shape, scratch, micros, deps, name):
    count = len(deps)
    ins = len(in_specs)

    def run(*refs):
        kernel(*refs[:ins], *refs[ins + count :])

    return pl.pallas_call(
        run,
        grid=(steps,),
        in_specs=in_specs + unread(deps),
        out_specs=out_specs,
        out_shape=out_shape,
        scratch_shapes=scratch,
        compiler_params=params(32 if name == "feed_forward" else VMEM),
        cost_estimate=taking(micros),
        name=name,
    )


def weight_rows(normed, grads, seq_count, extra=(), deps=()):
    rows, features = normed.shape
    wide = features // HEADS
    shard = wide // seq_count
    columns = sum(g.shape[1] for g in grads) + 128 * len(extra)

    def kernel(*refs):
        normed, grads, out = refs[0], refs[1 : 1 + len(grads_in)], refs[-1]
        at = 0
        for e in refs[1 + len(grads_in) : -1]:
            filled = jnp.concatenate(
                [e[...], jnp.zeros((128 - e.shape[0], wide), f32)], axis=0
            ).T
            out[:, :, :, columns - 128 :] = low(filled.reshape(seq_count, 1, shard, 128))
        for g in grads:
            value = mul(normed[...], g[...], TN).reshape(seq_count, 1, shard, g.shape[1])
            out[:, :, :, at : at + g.shape[1]] = low(value)
            at += g.shape[1]

    grads_in = grads
    out = tiled_call(
        kernel,
        HEADS,
        [pl.BlockSpec((rows, wide), lambda i: (0, i))]
        + [fixed_block(*g.shape) for g in grads]
        + [pl.BlockSpec((e.shape[0], wide), lambda i: (0, i)) for e in extra],
        [pl.BlockSpec((seq_count, 1, shard, columns), lambda i: (0, i, 0, 0))],
        [jax.ShapeDtypeStruct((seq_count, HEADS, shard, columns), bf16)],
        [],
        columns / 300,
        deps,
        "weight_rows",
    )(normed, *grads, *extra, *deps)[0]
    return out.reshape(seq_count, HEADS * shard, columns)


def fetch_weights(source, held, sems, place):
    return [
        pltpu.make_async_copy(source.at[:, place[0] ^ j], held.at[j], sems.at[j])
        for j in range(HEADS)
    ]


def project_all(place, tokens, weights, spots, deps=()):
    half, features = tokens[0].shape[1:]
    rows = 2 * half * HEADS
    seq_count, _, shard, columns = weights.shape
    devices = HEADS * seq_count
    ANY = pl.BlockSpec(memory_space=pl.ANY)

    def kernel(place, *refs):
        tokens, spots, source = refs[:8], refs[8], refs[9]
        normed, mix_in, query, z, pair, small, taps, gain_mix, held, sems = refs[10:]
        copies = fetch_weights(source, held, sems, place)
        for copy in copies:
            copy.start()

        def scaled(x):
            x = x.astype(f32)
            return x * lax.rsqrt(jnp.mean(x * x, axis=1, keepdims=True) + norm_eps)

        for copy in copies:
            copy.wait()

        def take(start, stop):
            part = held[:, :, :, start:stop]
            if shard % 16 != 0:
                part = part.astype(f32)
            return low(part.reshape(features, stop - start))

        turned = take(STEP_AT, STEP_AT + 128).astype(f32).T
        small_rows = turned[GAIN_LANE : GAIN_LANE + 16, :]
        small[...] = small_rows
        gain = small_rows[0:1, :]
        sources = iota((features, spots.shape[1]), 0)
        main = low(sources == spots[0:1, :])
        rest = low(sources == spots[1:2, :])
        small_low = low(small_rows)
        mains, rests = mul(small_low, main), mul(small_low, rest)
        gain_mix[...] = mains[2:3, CONV:] + rests[3:4, CONV:]
        taps[0:4, :] = mains[4:8, :CONV] + rests[8:12, :CONV]
        taps[4:8, :] = jnp.zeros((4, CONV), f32)
        for t in range(2 * HEADS):
            normed[half * t : half * (t + 1), :] = low(scaled(tokens[t][0]) * gain)
        x = normed[...]
        pair[...] = low(mul(x, take(KEY_AT, KEY_AT + 2 * HD)))
        mix_in[:, :CH] = low(mul(x, take(0, CH)))
        mix_in[:, CH:] = low(mul(x, take(CH, QUERY_AT)))
        query[...] = low(mul(x, take(QUERY_AT, GATE_AT)))
        z[...] = low(mul(x, take(GATE_AT, KEY_AT)))

    token_block = pl.BlockSpec((1, half, features), lambda *i: (0, 0, 0))
    return whole_call(
        kernel,
        place,
        [(t, token_block) for t in tokens] + [spots, (weights, ANY)],
        [
            like((rows, features), bf16),
            like((rows, QUERY_AT), bf16),
            like((rows, QD), bf16),
            like((rows, CH), bf16),
            like((rows, 2 * HD), bf16),
            like((16, features), f32),
            like((8, CONV), f32),
            like((1, CH), f32),
        ],
        [
            pltpu.VMEM((HEADS, seq_count, shard, columns), bf16),
            pltpu.SemaphoreType.DMA((HEADS,)),
        ],
        60,
        8,
        deps,
        "project_all",
    )


def pack_weights(place, state, steps, split, pairs, late):
    shard = state.shape[0]
    counts = [w.shape[1] // HEADS for w in split + late]
    columns = 2 * NS + 128 + sum(counts) + 2 * HD
    group = HEADS // KVH

    def kernel(place, *refs):
        outs = refs[-HEADS:]
        state, steps, pairs = refs[0], refs[1], refs[2]
        inputs, query, gate, ff_gate, ff_up = refs[3:-HEADS]
        for m in range(HEADS):
            j = place[0] ^ m

            def cut(ref, wide, at=0, spot=j):
                return ref[:, pl.ds(pl.multiple_of(at + spot * wide, 128), wide)]

            both = j // group
            blocks = [
                cut(inputs, CH), state[...], steps[j], cut(query, QD), cut(gate, CH),
                cut(pairs, HD, 0, both), cut(pairs, HD, KVH * HD, both),
                cut(ff_gate, counts[3]), cut(ff_up, counts[4]),
            ]
            at = 0
            for block in blocks:
                outs[m][:, at : at + block.shape[1]] = block
                at += block.shape[1]

    return whole_call(
        kernel,
        place,
        [state, steps, pairs] + split + late,
        [like((shard, columns), bf16)] * HEADS,
        [],
        60,
        2,
        (),
        "pack_weights",
    )


def gate_of(z_tile):
    z = z_tile.astype(f32)
    return z, jax.nn.sigmoid(z)


def lanes_of(rows, p):
    left = iota((rows.shape[1], TILE), 1) < MP
    first, second = rows[2 * p : 2 * p + 1, :], rows[2 * p + 1 : 2 * p + 2, :]
    return jnp.where(left, column_of(first, TILE), column_of(second, TILE))


def mix_tokens(y0, cums, reads, packs, z, deps=()):
    rows = y0.shape[0]
    wide = rows // HEADS
    count = len(packs)

    def kernel(y0, cums, reads, z, *refs):
        packs, (mixed_out, squares, incoming) = refs[:count], refs[count:]
        sum_packs(packs, incoming)
        for t in range(HEADS):
            here = slice(wide * t, wide * (t + 1))
            met = mul(reads[here, :], low(incoming[...]), NT)
            growth = jnp.exp(cums[:, here])
            grown = jnp.concatenate([lanes_of(growth, p) for p in range(PAIRS)], axis=1)
            mixed = low(y0[here, :] + grown * met)
            mixed_out[here, :] = mixed
            gate, sig = gate_of(z[here, :])
            inner = mixed.astype(f32) * gate * sig
            squares[:, here] = row_sums(inner * inner)

    return whole_call(
        kernel,
        None,
        [y0, cums, reads, z, *packs],
        [like((rows, CH), bf16), like((1, rows), f32), like((CH, NS), f32)],
        [],
        20,
        3,
        deps,
        "mix_tokens",
    )


def branch_out(mixed, z, scale, gain, attended, weights, deps=()):
    rows, features = mixed.shape[0], weights.shape[1]
    wide = rows // HEADS
    specs, shapes = scatter_outs(wide // 2, features)

    def kernel(mixed, z, scale, gain, attended, weights, gated_out, *parts):
        gate, sig = gate_of(z[...])
        inner = mixed[...].astype(f32) * gate * sig
        gated = low(inner * column_of(scale[...], CH) * gain[...])
        gated_out[...] = gated
        value = mul(gated, weights[:CH, :]) + mul(attended[...], weights[CH:, :])
        put_scatter(pl.program_id(0), value, parts)

    outs = tiled_call(
        kernel,
        HEADS,
        [
            by_ring(wide, CH),
            by_ring(wide, CH),
            pl.BlockSpec((1, wide), lambda i: (0, ring(i))),
            pl.BlockSpec((1, CH), lambda i: (0, 0)),
            by_ring(wide, QD),
            fixed_block(CH + QD, features),
        ],
        [by_ring(wide, CH)] + specs,
        [jax.ShapeDtypeStruct((rows, CH), bf16)] + shapes,
        [],
        3,
        deps,
        "branch_out",
    )(mixed, z, scale, gain, attended, weights, *deps)
    return outs[0], outs[1:]


def feed_forward(tokens, grads, weights, weights_down, deps=()):
    wide, features = 2 * tokens[0].shape[0], tokens[0].shape[1]
    rows = wide * HEADS
    ff = weights_down.shape[0]
    specs, shapes = scatter_outs(wide // 2, features)

    def kernel(*refs):
        tokens, grads = refs[:8], refs[8:16]
        weights, weights_down, tokens_out, grads_out, acted_out, inner_out = refs[16:22]
        parts, held, held_grads = refs[22:27], refs[27], refs[28]
        i = pl.program_id(0)
        x = load_piece(i, tokens, held)
        g = load_piece(i, grads, held_grads, 1)
        tokens_out[...] = x
        grads_out[...] = g
        inner = mul(x, weights[...])
        grad_acted = mul(g, weights_down[...], NT)
        gate, up = inner[:, :ff], inner[:, ff:]
        sig = jax.nn.sigmoid(gate)
        silu = gate * sig
        acted_out[...] = low(silu * up)
        grad_gate = low(grad_acted * up * (sig * (1.0 + gate * (1.0 - sig))))
        grad_inner = jnp.concatenate([grad_gate, low(grad_acted * silu)], axis=1)
        inner_out[...] = grad_inner
        put_scatter(i, mul(grad_inner, weights[...], NT), parts)

    outs = tiled_call(
        kernel,
        HEADS,
        piece_specs(tokens)
        + piece_specs(grads)
        + [
            fixed_block(features, 2 * ff),
            fixed_block(ff, features),
        ],
        [by_ring(wide, features), by_ring(wide, features), by_ring(wide, ff), by_ring(wide, 2 * ff)]
        + specs,
        [
            jax.ShapeDtypeStruct((rows, features), bf16),
            jax.ShapeDtypeStruct((rows, features), bf16),
            jax.ShapeDtypeStruct((rows, ff), bf16),
            jax.ShapeDtypeStruct((rows, 2 * ff), bf16),
        ]
        + shapes,
        [pltpu.VMEM((wide, features), bf16), pltpu.VMEM((wide, features), bf16)],
        7,
        deps,
        "feed_forward",
    )(*tokens, *grads, weights, weights_down, *deps)
    return outs[0], outs[1], outs[2], outs[3], outs[4:]


def scattered_product(left, weights, deps=()):
    rows, depth = left.shape
    features = weights.shape[1]
    wide = rows // HEADS
    specs, shapes = scatter_outs(wide // 2, features)

    def kernel(left, weights, *parts):
        put_scatter(pl.program_id(0), mul(left[...], weights[...]), parts)

    return tiled_call(
        kernel,
        HEADS,
        [by_ring(wide, depth), fixed_block(depth, features)],
        specs,
        shapes,
        [],
        2,
        deps,
        "scattered_product",
    )(left, weights, *deps)


def branch_back(grads, weights, attended, mixed, z, scale, gain, deps=()):
    wide, features = 2 * grads[0].shape[0], grads[0].shape[1]
    rows = wide * HEADS
    heads = QD // HD

    def kernel(*refs):
        grads = refs[:8]
        weights, attended, mixed, z, scale, gain = refs[8:14]
        grads_out, grad_att, terms, grad_gated, sums, held = refs[14:]
        i = pl.program_id(0)
        g = load_piece(i, grads, held)
        grads_out[...] = g
        both = mul(g, weights[...], NT)
        att = low(both[:, CH:])
        grad_att[...] = att
        product = att.astype(f32) * attended[...].astype(f32)
        for j in range(heads):
            terms[j] = row_sums(product[:, HD * j : HD * (j + 1)])
        gate, sig = gate_of(z[...])
        unit = mixed[...].astype(f32) * gate * sig * column_of(scale[...], CH)
        gated = both[:, :CH]
        grad_gated[...] = low(gated)
        scaled = gated * unit
        sums[...] = row_sums(scaled * gain[...])

    return tiled_call(
        kernel,
        HEADS,
        piece_specs(grads)
        + [
            fixed_block(CH + QD, features),
            by_ring(wide, QD),
            by_ring(wide, CH),
            by_ring(wide, CH),
            pl.BlockSpec((1, wide), lambda i: (0, ring(i))),
            pl.BlockSpec((1, CH), lambda i: (0, 0)),
        ],
        [
            by_ring(wide, features),
            by_ring(wide, QD),
            pl.BlockSpec((heads, 1, wide), lambda i: (0, 0, ring(i))),
            by_ring(wide, CH),
            pl.BlockSpec((1, wide), lambda i: (0, ring(i))),
        ],
        [
            jax.ShapeDtypeStruct((rows, features), bf16),
            jax.ShapeDtypeStruct((rows, QD), bf16),
            jax.ShapeDtypeStruct((heads, 1, rows), f32),
            jax.ShapeDtypeStruct((rows, CH), bf16),
            jax.ShapeDtypeStruct((1, rows), f32),
        ],
        [pltpu.VMEM((wide, features), bf16)],
        4,
        deps,
        "branch_back",
    )(*grads, weights, attended, mixed, z, scale, gain, *deps)


def gate_back(grad_gated, mixed, z, scale, mean, gain, cums, reads, packed, deps=()):
    rows = mixed.shape[0]
    wide = rows // HEADS

    def kernel(
        grad_gated, mixed, z, scale, mean, gain, cums, reads, packed, grad_mixed, grad_z, leaving
    ):
        total = None
        for t in range(HEADS):
            here = slice(wide * t, wide * (t + 1))
            gate, sig = gate_of(z[here, :])
            silu = gate * sig
            value = mixed[here, :].astype(f32)
            factor = column_of(scale[:, here], CH)
            unit = value * silu * factor
            inner = grad_gated[here, :].astype(f32) * gain[...]
            inner = (inner - unit * column_of(mean[:, here], CH)) * factor
            out = low(inner * silu)
            grad_mixed[here, :] = out
            grad_z[here, :] = low(inner * value * (sig * (1.0 + gate * (1.0 - sig))))
            growth = jnp.exp(cums[:, here])
            grown = jnp.concatenate([lanes_of(growth, p) for p in range(PAIRS)], axis=1)
            part = mul(low(out.astype(f32) * grown), reads[here, :], TN)
            total = part if total is None else total + part
        leaving[:CH, :] = low(total)
        leaving[CH:, :] = packed[CH:, :]

    return whole_call(
        kernel,
        None,
        [grad_gated, mixed, z, scale, mean, gain, cums, reads, packed],
        [like((rows, CH), bf16), like((rows, CH), bf16), like((CH + 16, NS), bf16)],
        [],
        20,
        3,
        deps,
        "gate_back",
    )


def normed_back(place, grad_pre, grad_z, grad_query, grad_pair, weights, deps=()):
    rows = grad_pre.shape[0]
    wide = rows // HEADS
    half = wide // 2
    seq_count, _, shard, columns = weights.shape
    features = HEADS * seq_count * shard
    ANY = pl.BlockSpec(memory_space=pl.ANY)

    def kernel(place, grad_pre, grad_query, grad_z, grad_pair, source, *refs):
        send_one, send_two, keep_one, keep_two, own, held, sems = refs
        copies = fetch_weights(source, held, sems, place)
        for copy in copies:
            copy.start()
        for copy in copies:
            copy.wait()
        for k in (1, 3, 2, 0):
            here = slice(wide * k, wide * (k + 1))
            grads = jnp.concatenate(
                [grad_pre[here, :], grad_query[here, :], grad_z[here, :], grad_pair[here, :]],
                axis=1,
            )
            parts = []
            for j in range(HEADS):
                part = held[j]
                if shard % 16 != 0:
                    part = part.astype(f32)
                parts.append(mul(grads, low(part.reshape(seq_count * shard, columns)), NT))
            value = jnp.concatenate(parts, axis=1)
            top, bottom = low(value[:half]), low(value[half:])
            if k == 1:
                send_one[0] = top
                keep_two[...] = bottom
            elif k == 3:
                send_one[1] = top
                send_two[0] = bottom
            elif k == 2:
                keep_one[...] = top
                send_two[1] = bottom
            else:
                own[...] = value

    shapes = scatter_outs(half, features)[1]
    return whole_call(
        kernel,
        place,
        [grad_pre, grad_query, grad_z, grad_pair, (weights, ANY)],
        shapes,
        [
            pltpu.VMEM((HEADS, seq_count, shard, columns), bf16),
            pltpu.SemaphoreType.DMA((HEADS,)),
        ],
        40,
        6,
        deps,
        "normed_back",
    )


def to_head(x, mask):
    return lax.ppermute(x, "head", [(i, i ^ mask) for i in range(HEADS)])


def to_seq(x, mask):
    return lax.ppermute(x, "seq", [(i, i ^ mask) for i in range(lax.axis_size("seq"))])


def shifted(x, blocks):
    count = lax.axis_size("seq")
    route = [(i, i + 2 * blocks) for i in range(count) if 0 <= i + 2 * blocks < count]
    return lax.ppermute(x, "seq", route)


def gather_head(top, bottom):
    one_top = to_head(top, 1)
    two_bottom = to_head(bottom, 2)
    one_bottom = to_head(bottom, 1)
    two_top = to_head(top, 2)
    three_top = to_head(one_top, 2)
    three_bottom = to_head(two_bottom, 1)
    return top, bottom, one_top, one_bottom, two_top, two_bottom, three_top, three_bottom


def gather_rows_low(x):
    half = x.shape[0] // 2
    return gather_head(low(x[:half]), low(x[half:]))


def pin(x, *deps):
    return lax.optimization_barrier((x,) + deps)[0]


def add_low(*terms):
    return low(sum((t.astype(f32) for t in terms[1:]), terms[0].astype(f32)))


def sum_head(row):
    wide = row.shape[1] // HEADS
    total = row
    for mask in range(1, HEADS):
        got = to_head(row, mask)
        total = total + jnp.concatenate(
            [got[:, wide * (k ^ mask) : wide * ((k ^ mask) + 1)] for k in range(HEADS)], axis=1
        )
    return total


def send_packs(packed, blocks, direction):
    return [shifted(packed, direction * k) for k in range(1, blocks)]


def gather_rows(shard):
    return lax.all_gather(shard, "seq", axis=0, tiled=False)


def scatter_rows(x):
    return lax.psum_scatter(x, "seq", scatter_dimension=0, tiled=False)


def exchange_columns(x, head_index):
    pick = lambda m: lax.dynamic_index_in_dim(x, head_index ^ m, 0, keepdims=False)
    return [pick(0)] + [to_head(pick(m), m) for m in range(1, HEADS)]


def in_order(pieces, index):
    bit = 1
    while bit < len(pieces):
        upper = (index & bit) != 0
        pieces = [jnp.where(upper, pieces[j ^ bit], pieces[j]) for j in range(len(pieces))]
        bit *= 2
    return pieces


def ordered_rows(x, head_index):
    parts = [
        lax.dynamic_index_in_dim(x, head_index ^ j, 1, keepdims=False) for j in range(HEADS)
    ]
    return jnp.stack(parts).reshape(-1, x.shape[-1])


def scatter_direct(x, core, block):
    blocks = x.shape[0] // 2
    x = x.reshape((blocks, 2) + x.shape[1:])
    pick = lambda c: lax.dynamic_index_in_dim(x, c, 1, keepdims=False)
    x = add_low(pick(core), to_seq(pick(1 - core), 1))
    parts = [lax.dynamic_index_in_dim(x, block, 0, keepdims=False)]
    for k in range(1, blocks):
        part = lax.dynamic_index_in_dim(x, block ^ k, 0, keepdims=False)
        parts.append(to_seq(part, 2 * k))
    main = add_low(*[p[:, :-128] for p in parts])
    small = add_low(*in_order([p[:, -128:] for p in parts], block))
    return jnp.concatenate([main, small], axis=1)


def split_columns(x):
    return x.reshape(x.shape[0], HEADS, -1).swapaxes(0, 1)


def joined(pieces, start, stop):
    return jnp.concatenate([p[:, start:stop].astype(f32) for p in pieces], axis=1)


def body(
    hidden_in,
    lengths,
    cotangent,
    input_gain,
    mixer_gate,
    mixer_inputs,
    state_weights,
    conv_weight,
    step_weight,
    decay_log,
    step_bias,
    skip_gain,
    query_weight,
    key_value_weight,
    mixer_gain,
    mixer_output,
    attention_out,
    second_gain,
    gate_weight,
    up_weight,
    down_weight,
):
    seq_count = lax.axis_size("seq")
    head_index = lax.axis_index("head")
    seq_index = lax.axis_index("seq")
    block = seq_index // 2
    core = seq_index % 2
    blocks = seq_count // 2
    own_rows, features = hidden_in.shape[2], hidden_in.shape[3]
    rows = 2 * own_rows * HEADS
    shard = input_gain.shape[0]
    ff = gate_weight.shape[1] // HEADS
    mix_shard, down_shard = mixer_output.shape[0], down_weight.shape[0]
    conv_shard = conv_weight.shape[0]
    device = head_index * seq_count + seq_index

    def in_columns(x):
        x = x.reshape(x.shape[0], -1)
        rest = jnp.pad(x[shard:], ((0, 2 * shard - x.shape[0]), (0, 0)))
        return [x[:shard], rest]

    small = [input_gain[:, None], second_gain[:, None]]
    small = small + in_columns(mixer_gain) + in_columns(conv_weight)
    small = jnp.concatenate(small, axis=1)
    small = jnp.pad(small, ((0, 0), (0, 128 - GAIN_LANE - small.shape[1])))
    steps = jnp.pad(split_columns(step_weight), ((0, 0), (0, 0), (0, GAIN_LANE - MIX)))
    steps = jnp.concatenate([steps, jnp.broadcast_to(small[None], (HEADS,) + small.shape)], axis=2)
    end_row = ((head_index ^ (HEADS - 1)) * 2 + (1 ^ core)) * TILE + TILE - 16
    place = jnp.stack([head_index, core, jnp.int32(1), end_row // 16]).astype(jnp.int32)
    packs = pack_weights(
        place, state_weights, steps, [mixer_inputs, query_weight, mixer_gate], key_value_weight,
        [gate_weight, up_weight],
    )
    wide = packs[0].shape[1] - 2 * ff
    pieces = [packs[0]] + [to_head(packs[m], m) for m in range(1, HEADS)]

    both = jnp.stack([hidden_in[:, 0], cotangent[:, 0]], axis=1)
    keep = lax.dynamic_index_in_dim(both, core, 0, keepdims=False)
    give = lax.dynamic_index_in_dim(both, 1 - core, 0, keepdims=False)
    got = to_seq(give, 1)
    hidden = jnp.concatenate([keep[0], got[0]], axis=0).astype(f32)
    cot = jnp.concatenate([keep[1], got[1]], axis=0)
    first_own = pin(pieces[0], got)
    weights_in = gather_rows(
        jnp.stack([first_own[:, :wide]] + [p[:, :wide] for p in pieces[1:]])
    )
    tokens = 2 * own_rows
    block_rows = own_rows * HEADS
    spot = jnp.arange(tokens)
    positions = (
        (2 * block + ((spot // own_rows) ^ core)) * block_rows
        + head_index * own_rows
        + spot % own_rows
    )
    length = lax.dynamic_index_in_dim(lengths, core, 0, keepdims=False)
    valid = (positions < length).astype(f32)[:, None]
    grad_result_own = cot.astype(f32) * valid
    grad_low = low(grad_result_own)
    both_all = gather_head(
        jnp.stack([keep[0], grad_low[:own_rows]]), jnp.stack([got[0], grad_low[own_rows:]])
    )

    out_pack = jnp.concatenate([mixer_output, attention_out], axis=0)
    out_all = gather_rows(pin(out_pack, *pieces))
    ff_pack = jnp.concatenate([p[:, wide:] for p in pieces] + [down_weight], axis=0)

    def sources(channels, size):
        owner, offset = channels // size, channels % size
        main = jnp.where(offset < shard, owner * shard + offset, -1)
        return jnp.stack([main, jnp.where(offset < shard, -1, owner * shard + offset - shard)])

    spread = jnp.arange(CONV)
    spread = jnp.where(spread < CH, spread + head_index * CH, spread + (MH * MP - CH))
    spots = jnp.concatenate(
        [sources(spread, conv_shard), sources(jnp.arange(CH) + head_index * CH, mix_shard)], axis=1
    )
    spots = jnp.pad(spots, ((0, 6), (0, 0))).astype(jnp.int32)
    (normed, mix_in, query, z, own_pair, small, taps, gain_mix) = project_all(
        place, both_all, weights_in, spots
    )
    tail = shifted(lax.dynamic_slice(mix_in, (end_row, 0), (16, CONV)), 1)
    gain_in, gain_two = small[0:1], small[1:2]
    scale_in = lax.rsqrt(jnp.mean(hidden * hidden, axis=-1, keepdims=True) + norm_eps)
    unit_in = hidden * scale_in

    pair = [own_pair, shifted(own_pair, 1)]

    def step_place(k):
        return place.at[2].set((block >= k).astype(jnp.int32))

    decay_part = lax.dynamic_slice_in_dim(-jnp.exp(decay_log), head_index * MIX, MIX)
    bias_part = lax.dynamic_slice_in_dim(step_bias, head_index * MIX, MIX)
    skip_part = lax.dynamic_slice_in_dim(skip_gain, head_index * MIX, MIX)
    heads = jnp.pad(jnp.stack([decay_part, bias_part]), ((0, 6), (0, 128 - MIX)))
    skip = jnp.broadcast_to(jnp.repeat(skip_part, MP)[None], (8, CH))
    running = attend(place, query, pair[0], None, True, False)
    pair.append(shifted(pin(pair[1], running[1], tail), 1))
    y0, reads, cums, starts, runs, packed = mixer_forward(
        place, mix_in, tail, taps, heads, skip, deps=(running[1], pair[1])
    )
    packs = send_packs(packed, blocks, 1)
    for k in range(3, blocks):
        pair.append(shifted(pin(pair[-1], *packs), 1))
    out_all = pin(out_all, packed)
    weights_out = jnp.concatenate(
        [
            out_all[:, :mix_shard].reshape(CH, features),
            out_all[:, mix_shard:].reshape(QD, features),
        ],
        axis=0,
    )
    for k in range(1, blocks):
        running = attend(
            step_place(k), query, pair[k], running, False, k == blocks - 1,
            deps=(packed, pair[2]) if k == 1 else (squares,),
        )
        if k == 1:
            mixed, squares, incoming = mix_tokens(y0, cums, reads, packs, z, deps=(running[1],))
            ff_all = gather_rows(pin(ff_pack, squares, pair[-1]))
    attended, logs = running
    ff_all = pin(ff_all, attended)
    weights_ff = ordered_rows(
        ff_all[:, : HEADS * shard].reshape(seq_count, HEADS, shard, 2 * ff), head_index
    )
    weights_down = ff_all[:, HEADS * shard :].reshape(ff, features)
    scale_mix = lax.rsqrt(sum_head(squares) / (MH * MP) + norm_eps)
    gated, parts = branch_out(mixed, z, scale_mix, gain_mix, attended, weights_out)
    resid = hidden + scatter_parts(parts)

    scale_two = lax.rsqrt(jnp.mean(resid * resid, axis=-1, keepdims=True) + norm_eps)
    norm_two = resid * scale_two
    normed_two, grad_result, acted, grad_inner, parts = feed_forward(
        gather_rows_low(norm_two * gain_two), both_all, weights_ff, weights_down
    )
    grad_down = low(mul(acted, grad_result, TN)).reshape(seq_count, down_shard, features)
    ff_rows = jnp.concatenate(
        [weight_rows(normed_two, [grad_inner], seq_count), grad_down], axis=1
    )
    ff_sum = scatter_rows(ff_rows)

    down_parts = scattered_product(acted, weights_down)
    grad_two = scatter_parts(parts)
    grad_two = grad_two * gain_two
    grad_resid = grad_result_own + scale_two * (
        grad_two - norm_two * jnp.mean(grad_two * norm_two, axis=-1, keepdims=True)
    )

    grad_branch, grad_attended, terms, grad_gated, sums_mix = branch_back(
        gather_rows_low(pin(grad_resid, ff_rows, down_parts[0])), weights_out, attended, mixed, z, scale_mix, gain_mix,
    )
    mean_mix = sum_head(sums_mix) / (MH * MP)
    down_parts = [pin(p, terms) for p in down_parts]
    result = resid + scatter_parts(down_parts)
    result = result * valid

    out_rows = jnp.concatenate(
        [
            low(mul(gated, grad_branch, TN)).reshape(seq_count, mix_shard, features),
            low(mul(attended, grad_branch, TN)).reshape(seq_count, shard, features),
        ],
        axis=1,
    )
    out_sum = scatter_rows(out_rows)

    chain = None
    grad_query = None

    def back_step(k, grad_query, chain, deps):
        grad_query, kept = attend_back(
            step_place(k), query, grad_attended, logs, terms, pair[k], grad_query, k == 0,
            deps=deps,
        )
        if chain is None:
            return grad_query, kept
        return grad_query, add_low(kept, chain)

    steps_left = list(reversed(range(blocks)))
    k = steps_left.pop(0)
    grad_query, chain = back_step(k, grad_query, chain, ())
    chain = shifted(chain, -1)
    grad_mixed, grad_z, leaving = gate_back(
        grad_gated, mixed, z, scale_mix, mean_mix, gain_mix, cums, reads, packed,
        deps=(grad_query,),
    )
    back_packs = send_packs(leaving, blocks, -1)
    for k in steps_left[:-2]:
        grad_query, chain = back_step(k, grad_query, chain, (leaving, out_rows))
        previous, chain = chain, shifted(chain, -1)
    steps_left = steps_left[-2:]
    grad_pre, first, grad_taps, sums, grad_skip = mixer_backward(
        place, mix_in, tail, taps, heads, skip, starts, runs, incoming, grad_mixed, back_packs,
        deps=(grad_query, previous),
    )
    from_next = shifted(first, -1)
    if len(steps_left) > 1:
        grad_query, chain = back_step(steps_left[0], grad_query, chain, (sums, chain))
        chain = shifted(chain, -1)
    grad_pre = fix_ends(place, grad_pre, from_next, taps)
    def placed(x, at):
        shape = (x.shape[0], x.shape[1] * HEADS)
        return lax.dynamic_update_slice_in_dim(jnp.zeros(shape, f32), x, at, 1)

    devices = HEADS * seq_count
    taps_part = jnp.concatenate(
        [placed(grad_taps[:4, :CH], head_index * CH), grad_taps[:4, CH:]], axis=1
    ).reshape(4, devices, conv_shard)
    taps_rest = jnp.pad(taps_part[:, :, shard:], ((0, 0), (0, 0), (0, 2 * shard - conv_shard)))
    skip_part = jnp.sum(grad_skip[0].reshape(MIX, MP), axis=1)
    head_part = jnp.stack([sums[0, :MIX], sums[1, :MIX], skip_part])
    head_part = jnp.pad(placed(head_part, head_index * MIX), ((0, 0), (0, -MH % shard)))
    head_part = head_part.reshape(-1, 1, shard)
    head_part = jnp.broadcast_to(head_part, (head_part.shape[0], devices, shard))
    small_part = [p.reshape(-1, features) for p in (taps_part[:, :, :shard], taps_rest, head_part)]
    small_part = jnp.concatenate(small_part, axis=0)
    small_part = jnp.pad(small_part, ((0, -small_part.shape[0] % 16), (0, 0)))
    early_rows = weight_rows(normed, [grad_pre, grad_z], seq_count, deps=(grad_query,))
    early_sum = scatter_rows(early_rows)
    grad_query, chain = back_step(steps_left[-1], grad_query, chain, (early_rows, result))

    late_rows = weight_rows(normed, [grad_query, chain], seq_count, extra=(small_part,))
    late_sum = scatter_direct(late_rows, core, block)
    parts = normed_back(
        place, grad_pre, grad_z, grad_query, chain, weights_in, deps=(late_rows,)
    )
    grad_normed = scatter_parts(parts) * gain_in
    all_cols = jnp.concatenate([late_sum, early_sum, ff_sum[: HEADS * shard]], axis=1)
    all_cols = exchange_columns(all_cols.reshape(HEADS, shard, -1), head_index)
    all_cols = in_order(all_cols, head_index)
    late_wide = QD + 2 * HD
    early_wide = CH + QUERY_AT
    late_cols = [p[:, :late_wide] for p in all_cols]
    early_cols = [p[:, late_wide + 128 : late_wide + 128 + early_wide] for p in all_cols]
    ff_cols = [p[:, late_wide + 128 + early_wide :] for p in all_cols]
    grad_hidden = grad_resid + scale_in * (
        grad_normed - unit_in * jnp.mean(grad_normed * unit_in, axis=-1, keepdims=True)
    )

    def back(x):
        x = x.reshape(2, own_rows, features)
        arrived = to_seq(x[1], 1)
        return jnp.stack(
            [jnp.where(core == 0, x[0], arrived), jnp.where(core == 0, arrived, x[0])]
        )[:, None]

    small_sum = sum(p[:, late_wide : late_wide + 128].astype(f32) for p in all_cols).T
    head_rows = 3 * (-(-MH // shard))
    head_sums = small_sum[8 : 8 + head_rows].reshape(3, -1)[:, :MH]
    taps_sum = jnp.concatenate([small_sum[0:4], small_sum[4:8, : conv_shard - shard]], axis=1)
    group = HEADS // KVH
    copies = [
        sum(p[:, QD : QD + 2 * HD].astype(f32) for p in late_cols[group * i : group * (i + 1)])
        for i in range(KVH)
    ]
    key_values = jnp.concatenate(
        [copy[:, HD * j : HD * (j + 1)] for j in range(2) for copy in copies], axis=1
    )
    states = sum(p[:, CH : CH + 2 * NS].astype(f32) for p in early_cols)
    grad_gate = joined(early_cols, QUERY_AT, QUERY_AT + CH)
    grad_inputs = joined(early_cols, 0, CH)
    grad_steps = joined(early_cols, STEP_AT, STEP_AT + MIX)
    grad_queries = joined(late_cols, 0, QD)
    grad_ff_gate = joined(ff_cols, 0, ff)
    grad_ff_up = joined(ff_cols, ff, 2 * ff)
    grad_mixer_output = out_sum[:mix_shard].astype(f32)

    def gain_grad(gain, *both):
        total = sum(jnp.sum(w.astype(f32) * g, axis=1) for w, g in both)
        return total / gain.astype(f32)

    return (
        back(result),
        back(grad_hidden),
        gain_grad(
            input_gain,
            (mixer_gate, grad_gate),
            (mixer_inputs, grad_inputs),
            (state_weights, states),
            (step_weight, grad_steps),
            (query_weight, grad_queries),
            (key_value_weight, key_values),
        ),
        grad_gate,
        grad_inputs,
        states,
        taps_sum.T,
        grad_steps,
        head_sums[0],
        head_sums[1],
        head_sums[2],
        grad_queries,
        key_values,
        gain_grad(mixer_gain, (mixer_output, grad_mixer_output)),
        grad_mixer_output,
        out_sum[mix_shard:].astype(f32),
        gain_grad(second_gain, (gate_weight, grad_ff_gate), (up_weight, grad_ff_up)),
        grad_ff_gate,
        grad_ff_up,
        ff_sum[HEADS * shard :].astype(f32),
    )


def solution(mesh):
    tokens = P(None, "seq", "head", None)
    split = P(("head", "seq"), None)
    line = P(("head", "seq"))
    whole = P()
    in_specs = (
        tokens, whole, tokens, line, split, split, split, split, split, whole, whole, whole,
        split, split, line, split, split, line, split, split, split,
    )
    out_specs = (
        tokens, tokens, line, split, split, split, split, split, whole, whole, whole, split,
        split, line, split, split, line, split, split, split,
    )
    return jax.shard_map(body, mesh=mesh, in_specs=in_specs, out_specs=out_specs, check_vma=False)
```

```python
import functools

import jax
import jax.numpy as jnp
from jax import lax
from jax.experimental import pallas as pl
from jax.experimental.pallas import tpu as pltpu
from jax.sharding import PartitionSpec as P

QH = 8
KVH = 2
HD = 128
MH = 24
MP = 64
NS = 128
HEADS = 4
MIX = MH // HEADS
CH = MIX * MP
QD = QH // HEADS * HD
CONV = CH + 2 * NS
STEP_AT = CONV
QUERY_AT = STEP_AT + 128
GATE_AT = QUERY_AT + QD
KEY_AT = GATE_AT + CH
TILE = 128
GAIN_LANE = 8
PAIRS = MIX // 2

norm_eps = 1e-05
score_scale = HD ** (-0.5)
exponent_scale = score_scale * 1.4426950408889634
highest = lax.Precision.HIGHEST
f32 = jnp.float32
bf16 = jnp.bfloat16
NN = ((1,), (0,))
NT = ((1,), (1,))
TN = ((0,), (0,))
BIG = 1e30
VMEM = 24


def low(x):
    return x.astype(bf16)


def mul(left, right, sides=NN, precision=None):
    return lax.dot_general(
        left, right, (sides, ((), ())), preferred_element_type=f32, precision=precision
    )


def params(megabytes, **more):
    return pltpu.CompilerParams(vmem_limit_bytes=megabytes * 1024 * 1024, **more)


def taking(micros):
    micros = micros * 0.02
    return pl.CostEstimate(
        flops=int(micros * 1.1e9), bytes_accessed=int(micros * 3.6e6), transcendentals=0
    )


def unread(deps):
    return [pl.BlockSpec(memory_space=pl.ANY)] * len(deps)


def iota(shape, dim):
    return lax.broadcasted_iota(jnp.int32, shape, dim)


def tile_of(g, place):
    blocks = TILE * HEADS // TILE
    return ((g % blocks) ^ place[0]) * 2 + ((g // blocks) ^ place[1])


def conv_sums(ext, taps):
    total = ext[5:133, :] * taps[0:1, :]
    for k in range(1, 4):
        total = total + ext[5 + k : 133 + k, :] * taps[k : k + 1, :]
    return total


def mul_exact(picks, values):
    high_part = low(values)
    low_part = low(values - high_part.astype(f32))
    return mul(picks, high_part) + mul(picks, low_part)


def step_sizes(raw, heads):
    rows = iota((TILE, TILE), 0)
    cols = iota((TILE, TILE), 1)
    lower = rows >= cols
    moved = raw + heads[1:2, :]
    delta = jnp.maximum(moved, 0.0) + jnp.log1p(jnp.exp(-jnp.abs(moved)))
    cum = mul_exact(low(lower), heads[0:1, :] * delta)
    return moved, delta, cum, lower


def head_terms(delta, cum, lower, left):
    cum_rows = cum.T
    decays, both, sizes = [], [], []
    for p in range(PAIRS):
        columns = []
        for h in (2 * p, 2 * p + 1):
            column = jnp.broadcast_to(cum[:, h : h + 1], (TILE, TILE))
            decays.append(jnp.exp(jnp.where(lower, column - cum_rows[h : h + 1, :], -BIG)))
            columns.append(column)
        both.append(jnp.where(left, columns[0], columns[1]))
        sizes.append(jnp.where(left, delta[:, 2 * p : 2 * p + 1], delta[:, 2 * p + 1 : 2 * p + 2]))
    return decays, jnp.concatenate(both, axis=1), jnp.concatenate(sizes, axis=1)


def head_rows(values, top):
    return jnp.concatenate([row_pair(values, p, top) for p in range(PAIRS)], axis=0)


def row_pair(values, p, top):
    return jnp.where(top, values[:, 2 * p : 2 * p + 1], values[:, 2 * p + 1 : 2 * p + 2])


def halves(x, left):
    none = jnp.zeros_like(x)
    return jnp.concatenate([jnp.where(left, x, none), jnp.where(left, none, x)], axis=0)


def tile_rows(g, place):
    return pl.ds(pl.multiple_of(tile_of(g, place) * TILE, TILE), TILE)


def pack_rows(state, total):
    high_part = low(total).astype(f32)
    rows = jnp.concatenate([high_part, total - high_part, jnp.zeros((14, 128), f32)], axis=0)
    return jnp.concatenate([low(state), low(rows)], axis=0)


def sum_packs(packs, out):
    top = iota((TILE, NS), 0) < MP
    out[...] = jnp.zeros_like(out)
    passed = jnp.zeros((1, 128), f32)
    for pack in packs:
        factor = jnp.exp(passed)
        for p in range(PAIRS):
            lanes = slice(TILE * p, TILE * (p + 1))
            out[lanes, :] = out[lanes, :] + row_pair(factor, p, top) * pack[lanes, :].astype(f32)
        ends = pack[CH : CH + 16, :].astype(f32)
        passed = passed + ends[0:1, :] + ends[1:2, :]


def mixer_forward_kernel(
    place, rest, tail, taps, heads, skip, y0, reads_out, cums, starts, runs, packed,
    ext, state, run,
):
    state[...] = jnp.zeros_like(state)
    run[...] = jnp.zeros_like(run)
    ext[0:8, :] = tail[...].astype(f32)[8:16, :]

    def one_tile(g, unused):
        here = tile_rows(g, place)
        pre = rest[here, :CONV].astype(f32)
        ext[8:136, :] = pre
        total = conv_sums(ext, taps)
        act = total * jax.nn.sigmoid(total)
        ext[0:8, :] = pre[120:128, :]
        writes = low(act[:, CH : CH + NS])
        reads = low(act[:, CH + NS :])
        reads_out[here, :] = reads
        starts[g] = low(state[...])
        runs[g] = run[...]
        _, delta, cum, lower = step_sizes(rest[here, STEP_AT:].astype(f32), heads)
        left = iota((TILE, TILE), 1) < MP
        top = iota((TILE, TILE), 0) < MP
        meet = mul(reads, writes, NT)
        cums[:, here] = (cum + run[0:1, :]).T[0:8, :]
        last_row = cum[127:128, :]
        decays, both, sizes = head_terms(delta, cum, lower, left)
        x = act[:, :CH]
        xd = x * sizes
        held = state[...]
        carried = jnp.exp(both) * mul(reads, low(held), NT)
        out = []
        for p in range(PAIRS):
            lanes = slice(TILE * p, TILE * (p + 1))
            mix = jnp.concatenate([low(meet * d) for d in decays[2 * p : 2 * p + 2]], axis=1)
            out.append(mul(mix, low(halves(xd[:, lanes], left))))
        y0[here, :] = jnp.concatenate(out, axis=1) + carried + skip[0:1, :] * x
        xw = low(jnp.exp(both[127:128, :] - both) * xd)
        state[...] = head_rows(jnp.exp(last_row), top) * held + mul(xw, writes, TN)
        run[...] = run[...] + last_row
        return unused

    lax.fori_loop(0, rest.shape[0] // TILE, one_tile, 0, unroll=2)
    packed[...] = pack_rows(state[...], run[0:1, :])


def skipping(kernel, before, count):
    def run(*refs):
        kernel(*refs[:before], *refs[before + count :])

    return run


def whole_block(*shape):
    return pl.BlockSpec(shape, lambda *i: (0,) * len(shape))


def whole_call(kernel, place, args, outs, scratch, megabytes, micros, deps, name):
    count = 0 if place is None else 1
    before = len(args) + count
    specs = [whole_block(*a.shape) if hasattr(a, "shape") else a[1] for a in args]
    args = [a if hasattr(a, "shape") else a[0] for a in args]
    return pl.pallas_call(
        skipping(kernel, before, len(deps)),
        grid_spec=pltpu.PrefetchScalarGridSpec(
            num_scalar_prefetch=count,
            grid=(1,),
            in_specs=specs + unread(deps),
            out_specs=[whole_block(*o.shape) for o in outs],
            scratch_shapes=scratch,
        ),
        out_shape=outs,
        compiler_params=params(megabytes),
        cost_estimate=taking(micros),
        name=name,
    )(*([] if place is None else [place]), *args, *deps)


def like(shape, kind):
    return jax.ShapeDtypeStruct(shape, kind)


def mixer_forward(place, rest, tail, taps, heads, skip, deps=()):
    rows = rest.shape[0]
    tiles = rows // TILE
    return whole_call(
        mixer_forward_kernel,
        place,
        [rest, tail, taps, heads, skip],
        [
            like((rows, CH), f32),
            like((rows, NS), bf16),
            like((8, rows), f32),
            like((tiles, CH, NS), bf16),
            like((tiles, 8, 128), f32),
            like((CH + 16, NS), bf16),
        ],
        [
            pltpu.VMEM((TILE + 8, CONV), f32),
            pltpu.VMEM((CH, NS), f32),
            pltpu.VMEM((8, 128), f32),
        ],
        20,
        6,
        deps,
        "mixer_forward",
    )


def mixer_backward_kernel(
    count, place, rest, tail, taps, heads, skip, starts, runs, incoming, grad_y, *refs
):
    packs = refs[:count]
    grad_pre, first, grad_taps, sums, grad_skip, ext, dext, grad_state = refs[count:]
    sum_packs(packs, grad_state)
    dext[128:136, :] = jnp.zeros((8, CONV), f32)
    grad_taps[...] = jnp.zeros_like(grad_taps)
    sums[...] = jnp.zeros_like(sums)
    grad_skip[...] = jnp.zeros_like(grad_skip)
    tiles = rest.shape[0] // TILE

    def one_tile(step, unused):
        g = tiles - 1 - step
        here = tile_rows(g, place)
        before = tile_of(jnp.maximum(g - 1, 0), place) * TILE + TILE - 16
        before = rest[pl.ds(pl.multiple_of(before, 16), 16), :CONV].astype(f32)
        ext[8:136, :] = rest[here, :CONV].astype(f32)
        ext[0:8, :] = jnp.where(g == 0, tail[...].astype(f32), before)[8:16, :]
        total = conv_sums(ext, taps)
        gate = jax.nn.sigmoid(total)
        act = total * gate
        writes = low(act[:, CH : CH + NS])
        reads = low(act[:, CH + NS :])
        moved, delta, cum, lower = step_sizes(rest[here, STEP_AT:].astype(f32), heads)
        rows = iota((TILE, TILE), 0)
        cols = iota((TILE, TILE), 1)
        left = cols < MP
        top = rows < MP
        meet = mul(reads, writes, NT)
        last_row = cum[127:128, :]
        shrink = jnp.exp(last_row)
        decays, both, sizes = head_terms(delta, cum, lower, left)
        x = act[:, :CH]
        xd = x * sizes
        xd_low = low(xd)
        dy_low = grad_y[here, :]
        dy = dy_low.astype(f32)
        held = starts[g].astype(f32) + head_rows(jnp.exp(runs[g][0:1, :]), top) * incoming[...]
        held_low = low(held)
        ds = grad_state[...]
        ds_low = low(ds)
        from_start = jnp.exp(both)
        to_end = jnp.exp(both[127:128, :] - both)
        carried = from_start * mul(reads, held_low, NT)
        kept = to_end * mul(writes, ds_low, NT)
        dy_start = low(dy * from_start)
        grad_reads = mul(dy_start, held_low)
        grad_writes = mul(low(xd * to_end), ds_low)
        grad_meet = jnp.zeros((TILE, TILE), f32)
        within, backs = [], []
        for p in range(PAIRS):
            lanes = slice(TILE * p, TILE * (p + 1))
            l0, l1 = decays[2 * p : 2 * p + 2]
            dy_two = halves(dy_low[:, lanes], left)
            m0, m1 = low(meet * l0), low(meet * l1)
            dm = mul(dy_two, xd_low[:, lanes], NT)
            grad_meet = grad_meet + dm[:TILE] * l0 + dm[TILE:] * l1
            mix = jnp.concatenate([m0, m1], axis=1)
            within.append(mul(mix, halves(xd_low[:, lanes], left)))
            backs.append(mul(jnp.concatenate([m0, m1], axis=0), dy_two, TN))
        within = jnp.concatenate(within, axis=1)
        backs = jnp.concatenate(backs, axis=1)
        dxd = backs + kept
        grad_x = dxd * sizes + skip[0:1, :] * dy
        kept_part = kept * xd
        along = dy * (within + carried) - kept_part - xd_low.astype(f32) * backs
        grad_skip[0:1, :] = grad_skip[0:1, :] + jnp.sum(dy * x, axis=0, keepdims=True)
        product = held * ds
        ends = [jnp.sum(kept_part, axis=0, keepdims=True)]
        head_of = iota((CH, 128), 0) // MP == iota((CH, 128), 1)
        pick = low(head_of)
        by_row = jnp.sum(product, axis=1, keepdims=True)
        state_part = jnp.sum(jnp.where(head_of, by_row, 0.0), axis=0, keepdims=True)
        grad_state[...] = head_rows(shrink, top) * ds + mul(dy_start, reads, TN)
        meet_low = low(grad_meet)
        grad_reads = grad_reads + mul(meet_low, writes)
        grad_writes = grad_writes + mul(meet_low, reads, TN)
        ends.append(jnp.zeros((7, CH), f32))
        stacked = jnp.concatenate([along, dxd * x] + ends, axis=0)
        high_part = low(stacked)
        low_part = low(stacked - high_part.astype(f32))
        by_head = mul(high_part, pick) + mul(low_part, pick)
        grad_cum = by_head[:TILE]
        grad_delta = by_head[TILE : 2 * TILE]
        last_add = state_part * shrink + by_head[2 * TILE : 2 * TILE + 1]
        grad_cum = grad_cum + jnp.where(rows == TILE - 1, last_add, 0.0)
        later = mul_exact(low(rows <= cols), grad_cum)
        grad_raw = (grad_delta + heads[0:1, :] * later) * jax.nn.sigmoid(moved)
        grad_raw = jnp.where(cols < MIX, grad_raw, 0.0)
        sums[0:1, :] = sums[0:1, :] + heads[0:1, :] * jnp.sum(delta * later, axis=0, keepdims=True)
        sums[1:2, :] = sums[1:2, :] + jnp.sum(grad_raw, axis=0, keepdims=True)
        grad_act = jnp.concatenate([grad_x, grad_writes, grad_reads], axis=1)
        grad_total = grad_act * (gate * (1.0 + total * (1.0 - gate)))
        dext[0:128, :] = grad_total
        out = dext[3:131, :] * taps[0:1, :]
        for k in range(1, 4):
            out = out + dext[3 - k : 131 - k, :] * taps[k : k + 1, :]
        for k in range(4):
            grad_taps[k : k + 1, :] = grad_taps[k : k + 1, :] + jnp.sum(
                grad_total * ext[5 + k : 133 + k, :], axis=0, keepdims=True
            )
        grad_pre[here, :CONV] = low(out)
        grad_pre[here, STEP_AT:] = low(grad_raw)
        dext[128:136, :] = grad_total[0:8, :]
        first[...] = grad_total[0:8, :]
        return unused

    lax.fori_loop(0, tiles, one_tile, 0, unroll=2)


def mixer_backward(
    place, rest, tail, taps, heads, skip, starts, runs, incoming, grad_y, packs, deps=()
):
    rows = rest.shape[0]
    return whole_call(
        functools.partial(mixer_backward_kernel, len(packs)),
        place,
        [rest, tail, taps, heads, skip, starts, runs, incoming, grad_y, *packs],
        [
            like((rows, QUERY_AT), bf16),
            like((8, CONV), f32),
            like((8, CONV), f32),
            like((8, 128), f32),
            like((8, CH), f32),
        ],
        [
            pltpu.VMEM((TILE + 8, CONV), f32),
            pltpu.VMEM((TILE + 8, CONV), f32),
            pltpu.VMEM((CH, NS), f32),
        ],
        24,
        13,
        deps,
        "mixer_backward",
    )


def fix_ends(place, grad_pre, from_next, taps):
    def kernel(place, grad_pre, from_next, taps, out):
        fixed = jnp.zeros((16, CONV), f32)
        rows = iota((16, CONV), 0)
        for d in range(3):
            part = from_next[0:1, :] * taps[d : d + 1, :]
            for k in range(d):
                part = part + from_next[d - k : d - k + 1, :] * taps[k : k + 1, :]
            fixed = fixed + jnp.where(rows == 13 + d, part, 0.0)
        out[:, :CONV] = low(grad_pre[:, :CONV].astype(f32) + fixed)
        out[:, CONV:] = grad_pre[:, CONV:]

    block = pl.BlockSpec((16, QUERY_AT), lambda i, s: (s[3], 0))
    return pl.pallas_call(
        kernel,
        grid_spec=pltpu.PrefetchScalarGridSpec(
            num_scalar_prefetch=1,
            grid=(1,),
            in_specs=[block, whole_block(8, CONV), whole_block(8, CONV)],
            out_specs=block,
        ),
        out_shape=like(grad_pre.shape, bf16),
        input_output_aliases={1: 0},
        compiler_params=params(8),
        cost_estimate=taking(1),
        name="fix_ends",
    )(place, grad_pre, from_next, taps)


def tile_number(stored, place):
    return ((stored % 2) ^ place[1]) * HEADS + ((stored // 2) ^ place[0])


def masked(scores, place, query_tile):
    reach = iota((TILE, TILE), 0) - iota((TILE, TILE), 1)
    rows = []
    for i in range(scores.shape[0] // TILE):
        cols = []
        for j in range(scores.shape[1] // TILE):
            gap = (tile_number(query_tile + j, place) - tile_number(i, place)) * TILE
            part = scores[TILE * i : TILE * (i + 1), TILE * j : TILE * (j + 1)]
            cols.append(jnp.where(reach <= gap, part, -BIG))
        rows.append(jnp.concatenate(cols, axis=1))
    return jnp.concatenate(rows, axis=0)


def attend_kernel(back, closing, count, place, *refs):
    diagonal = back == 0
    query, pair = refs[:2]
    refs = refs[2:]
    if not diagonal:
        acc_in, stat_in = refs[:2]
        refs = refs[2:]
    refs = refs[count:]
    if closing:
        attended, logs = refs
    else:
        acc_out, stat_out = refs
    wide = 256
    columns = query.shape[0]
    items = [
        (j, slice(wide * i, wide * (i + 1))) for i in range(columns // wide) for j in range(QD // HD)
    ]

    def put(j, cols, acc, new, total):
        if closing:
            attended[cols, HD * j : HD * (j + 1)] = low((acc / total).T)
            logs[j, :, cols] = new + jnp.log2(total)
        else:
            acc_out[j, :, cols] = acc
            stat_out[j, 0:1, cols] = new
            stat_out[j, 1:2, cols] = total

    def work():
        keys = pair[:, :HD]
        vals = pair[:, HD:]

        def start(j, cols):
            scores = mul(keys, query[cols, HD * j : HD * (j + 1)], NT)
            return masked(scores, place, cols.start // TILE) if diagonal else scores

        def weigh(scores, j, cols):
            new = jnp.max(scores, axis=0, keepdims=True) * exponent_scale
            if not diagonal:
                new = jnp.maximum(new, stat_in[j, 0:1, cols])
            probs = jnp.exp2(scores * exponent_scale - new)
            return low(probs), jnp.sum(probs, axis=0, keepdims=True), new

        def finish(probs, total, new, j, cols):
            acc = mul(vals, probs, TN)
            if not diagonal:
                fade = jnp.exp2(stat_in[j, 0:1, cols] - new)
                total = total + stat_in[j, 1:2, cols] * fade
                acc = acc + acc_in[j, :, cols] * fade
            put(j, cols, acc, new, total)

        scores = start(*items[0])
        pending = None
        for n, item in enumerate(items):
            following = start(*items[n + 1]) if n + 1 < len(items) else None
            weighed = weigh(scores, *item)
            if pending is not None:
                finish(*pending)
            pending = weighed + item
            scores = following
        finish(*pending)

    if diagonal:
        work()
    else:
        active = place[2] >= back
        pl.when(active)(work)

        @pl.when(jnp.logical_not(active))
        def _():
            for j, cols in items:
                put(j, cols, acc_in[j, :, cols], stat_in[j, 0:1, cols], stat_in[j, 1:2, cols])


def attend(place, query, pair, back, carried, closing, deps=()):
    diagonal = back == 0
    rows = query.shape[0]
    heads = QD // HD
    whole = lambda *shape: pl.BlockSpec(shape, lambda i, s: (0,) * len(shape))
    in_specs = [
        whole(rows, QD),
        whole(rows, 2 * HD),
    ]
    running = [whole(heads, HD, rows), whole(heads, 8, rows)]
    if not diagonal:
        in_specs += running
    if closing:
        out_specs = [whole(rows, QD), whole(heads, 1, rows)]
        out_shape = [
            jax.ShapeDtypeStruct((rows, QD), bf16),
            jax.ShapeDtypeStruct((heads, 1, rows), f32),
        ]
    else:
        out_specs = running
        out_shape = [
            jax.ShapeDtypeStruct((heads, HD, rows), f32),
            jax.ShapeDtypeStruct((heads, 8, rows), f32),
        ]
    return pl.pallas_call(
        functools.partial(attend_kernel, back, closing, len(deps)),
        grid_spec=pltpu.PrefetchScalarGridSpec(
            num_scalar_prefetch=1,
            grid=(1,),
            in_specs=in_specs + unread(deps),
            out_specs=out_specs,
        ),
        out_shape=out_shape,
        compiler_params=params(16),
        cost_estimate=taking(5),
        name="attend",
    )(place, query, pair, *(() if diagonal else carried), *deps)


def attend_back_kernel(back, opening, count, place, *refs):
    diagonal = back == 0
    query, grad_out, logs, terms, pair = refs[:5]
    refs = refs[5:]
    if not opening:
        grad_in = refs[0]
        refs = refs[1:]
    grad_query, grad_pair = refs[count:]
    wide = 512

    def work():
        keys = pair[:, :HD]
        vals = pair[:, HD:]
        keys_sum = None
        for i in range(query.shape[0] // wide):
            cols = slice(wide * i, wide * (i + 1))
            for j in range(QD // HD):
                lanes = slice(HD * j, HD * (j + 1))
                q = query[cols, lanes]
                do = grad_out[cols, lanes]
                scores = mul(keys, q, NT)
                if diagonal:
                    scores = masked(scores, place, cols.start // TILE)
                probs = jnp.exp2(scores * exponent_scale - logs[j, :, cols])
                grad_probs = mul(vals, do, NT)
                grad_scores = low(probs * (grad_probs - terms[j, :, cols]))
                vals_add = mul(low(probs), do)
                keys_add = mul(grad_scores, q)
                add = mul(keys, grad_scores, TN)
                if not opening:
                    add = add + grad_in[j, :, cols]
                if diagonal:
                    grad_query[cols, lanes] = low((add * score_scale).T)
                else:
                    grad_query[j, :, cols] = add
                if keys_sum is None:
                    keys_sum, vals_sum = keys_add, vals_add
                else:
                    keys_sum, vals_sum = keys_sum + keys_add, vals_sum + vals_add
        grad_pair[:, :HD] = low(keys_sum * score_scale)
        grad_pair[:, HD:] = low(vals_sum)

    if diagonal:
        work()
    else:
        active = place[2] >= back
        pl.when(active)(work)

        @pl.when(jnp.logical_not(active))
        def _():
            grad_query[...] = jnp.zeros_like(grad_query) if opening else grad_in[...]
            grad_pair[...] = jnp.zeros_like(grad_pair)


def attend_back(place, query, grad_out, logs, terms, pair, grad_query, back, deps=()):
    diagonal = back == 0
    rows = query.shape[0]
    heads = QD // HD
    whole = lambda *shape: pl.BlockSpec(shape, lambda i, s: (0,) * len(shape))
    in_specs = [
        whole(rows, QD),
        whole(rows, QD),
        whole(heads, 1, rows),
        whole(heads, 1, rows),
        whole(rows, 2 * HD),
    ]
    args = [place, query, grad_out, logs, terms, pair]
    opening = grad_query is None
    if not opening:
        in_specs.append(whole(heads, HD, rows))
        args.append(grad_query)
    if diagonal:
        query_spec = whole(rows, QD)
        query_shape = jax.ShapeDtypeStruct((rows, QD), bf16)
    else:
        query_spec = whole(heads, HD, rows)
        query_shape = jax.ShapeDtypeStruct((heads, HD, rows), f32)
    return pl.pallas_call(
        functools.partial(attend_back_kernel, back, opening, len(deps)),
        grid_spec=pltpu.PrefetchScalarGridSpec(
            num_scalar_prefetch=1,
            grid=(1,),
            in_specs=in_specs + unread(deps),
            out_specs=[query_spec, whole(rows, 2 * HD)],
        ),
        out_shape=[
            query_shape,
            jax.ShapeDtypeStruct((rows, 2 * HD), bf16),
        ],
        compiler_params=params(VMEM),
        cost_estimate=taking(7),
        name="attend_back",
    )(*args, *deps)


def ring(i):
    j = (i + 1) % HEADS
    return j ^ (j // 2)


def load_piece(i, pieces, held, which=None):
    half = pieces[0].shape[-2]
    if which is not None:
        pieces = [p.at[which] for p in pieces]
    for at, k in enumerate((1, 3, 2, 0)):

        @pl.when(i == at)
        def _(k=k):
            held[:half, :] = pieces[2 * k][...]
            held[half:, :] = pieces[2 * k + 1][...]

    return held[...]


def piece_specs(pieces):
    return [fixed_block(*p.shape) for p in pieces]


def put_scatter(i, value, refs):
    send_one, send_two, keep_one, keep_two, own = refs
    half = keep_one.shape[0]
    top, bottom = low(value[:half]), low(value[half:])

    @pl.when(i == 0)
    def _():
        send_one[0] = top
        keep_two[...] = bottom

    @pl.when(i == 1)
    def _():
        send_one[0] = top
        send_two[0] = bottom

    @pl.when(i == 2)
    def _():
        keep_one[...] = top
        send_two[0] = bottom

    @pl.when(i == 3)
    def _():
        own[...] = value


def scatter_outs(half, columns):
    specs = [
        pl.BlockSpec((1, half, columns), lambda i: (jnp.minimum(i, 1), 0, 0)),
        pl.BlockSpec((1, half, columns), lambda i: (jnp.clip(i - 1, 0, 1), 0, 0)),
        pl.BlockSpec((half, columns), lambda i: (0, 0)),
        pl.BlockSpec((half, columns), lambda i: (0, 0)),
        pl.BlockSpec((2 * half, columns), lambda i: (0, 0)),
    ]
    shapes = [
        jax.ShapeDtypeStruct((2, half, columns), bf16),
        jax.ShapeDtypeStruct((2, half, columns), bf16),
        jax.ShapeDtypeStruct((half, columns), bf16),
        jax.ShapeDtypeStruct((half, columns), bf16),
        jax.ShapeDtypeStruct((2 * half, columns), f32),
    ]
    return specs, shapes


def scatter_parts(parts, marks=()):
    send_one, send_two, keep_one, keep_two, own = parts
    first = pin(to_head(send_one, 1), *marks)
    second = pin(to_head(send_two, 2), *marks)
    top = to_head(add_low(keep_one, first[1]), 2)
    bottom = to_head(add_low(keep_two, second[0]), 1)
    half = keep_one.shape[0]
    return jnp.concatenate(
        [
            own[:half] + first[0].astype(f32) + top.astype(f32),
            own[half:] + second[1].astype(f32) + bottom.astype(f32),
        ],
        axis=0,
    )


def by_ring(*block):
    return pl.BlockSpec(block, lambda i: (ring(i), 0))


def row_sums(x):
    ones = jnp.ones((8, x.shape[1]), bf16)
    high_part = low(x)
    low_part = low(x - high_part.astype(f32))
    return (mul(ones, high_part, NT) + mul(ones, low_part, NT))[0:1, :]


def column_of(row, width):
    column = jnp.broadcast_to(row, (128, row.shape[1])).T
    return jnp.concatenate([column] * (width // 128), axis=1)


def fixed_block(*shape):
    return pl.BlockSpec(shape, lambda i: (0,) * len(shape), pipeline_mode=pl.Buffered(1))


def tiled_call(kernel, steps, in_specs, out_specs, out_shape, scratch, micros, deps, name):
    count = len(deps)
    ins = len(in_specs)

    def run(*refs):
        kernel(*refs[:ins], *refs[ins + count :])

    return pl.pallas_call(
        run,
        grid=(steps,),
        in_specs=in_specs + unread(deps),
        out_specs=out_specs,
        out_shape=out_shape,
        scratch_shapes=scratch,
        compiler_params=params(32 if name == "feed_forward" else VMEM),
        cost_estimate=taking(micros),
        name=name,
    )


def weight_rows(normed, grads, seq_count, extra=(), deps=()):
    rows, features = normed.shape
    wide = features // HEADS
    shard = wide // seq_count
    columns = sum(g.shape[1] for g in grads) + 128 * len(extra)

    def kernel(*refs):
        normed, grads, out = refs[0], refs[1 : 1 + len(grads_in)], refs[-1]
        at = 0
        for e in refs[1 + len(grads_in) : -1]:
            filled = jnp.concatenate(
                [e[...], jnp.zeros((128 - e.shape[0], wide), f32)], axis=0
            ).T
            out[:, :, :, columns - 128 :] = low(filled.reshape(seq_count, 1, shard, 128))
        for g in grads:
            value = mul(normed[...], g[...], TN).reshape(seq_count, 1, shard, g.shape[1])
            out[:, :, :, at : at + g.shape[1]] = low(value)
            at += g.shape[1]

    grads_in = grads
    out = tiled_call(
        kernel,
        HEADS,
        [pl.BlockSpec((rows, wide), lambda i: (0, i))]
        + [fixed_block(*g.shape) for g in grads]
        + [pl.BlockSpec((e.shape[0], wide), lambda i: (0, i)) for e in extra],
        [pl.BlockSpec((seq_count, 1, shard, columns), lambda i: (0, i, 0, 0))],
        [jax.ShapeDtypeStruct((seq_count, HEADS, shard, columns), bf16)],
        [],
        columns / 300,
        deps,
        "weight_rows",
    )(normed, *grads, *extra, *deps)[0]
    return out.reshape(seq_count, HEADS * shard, columns)


def fetch_weights(source, held, sems, place):
    return [
        pltpu.make_async_copy(source.at[:, place[0] ^ j], held.at[j], sems.at[j])
        for j in range(HEADS)
    ]


def project_all(place, tokens, weights, spots, deps=()):
    half, features = tokens[0].shape[1:]
    rows = 2 * half * HEADS
    seq_count, _, shard, columns = weights.shape
    devices = HEADS * seq_count
    ANY = pl.BlockSpec(memory_space=pl.ANY)

    def kernel(place, *refs):
        tokens, spots, source = refs[:8], refs[8], refs[9]
        normed, mix_in, query, z, pair, small, taps, gain_mix, held, sems = refs[10:]
        copies = fetch_weights(source, held, sems, place)
        for copy in copies:
            copy.start()

        def scaled(x):
            x = x.astype(f32)
            return x * lax.rsqrt(jnp.mean(x * x, axis=1, keepdims=True) + norm_eps)

        for copy in copies:
            copy.wait()

        def take(start, stop):
            part = held[:, :, :, start:stop]
            if shard % 16 != 0:
                part = part.astype(f32)
            return low(part.reshape(features, stop - start))

        turned = take(STEP_AT, STEP_AT + 128).astype(f32).T
        small_rows = turned[GAIN_LANE : GAIN_LANE + 16, :]
        small[...] = small_rows
        gain = small_rows[0:1, :]
        sources = iota((features, spots.shape[1]), 0)
        main = low(sources == spots[0:1, :])
        rest = low(sources == spots[1:2, :])
        small_low = low(small_rows)
        mains, rests = mul(small_low, main), mul(small_low, rest)
        gain_mix[...] = mains[2:3, CONV:] + rests[3:4, CONV:]
        taps[0:4, :] = mains[4:8, :CONV] + rests[8:12, :CONV]
        taps[4:8, :] = jnp.zeros((4, CONV), f32)
        for t in range(2 * HEADS):
            normed[half * t : half * (t + 1), :] = low(scaled(tokens[t][0]) * gain)
        x = normed[...]
        pair[...] = low(mul(x, take(KEY_AT, KEY_AT + 2 * HD)))
        mix_in[:, :CH] = low(mul(x, take(0, CH)))
        mix_in[:, CH:] = low(mul(x, take(CH, QUERY_AT)))
        query[...] = low(mul(x, take(QUERY_AT, GATE_AT)))
        z[...] = low(mul(x, take(GATE_AT, KEY_AT)))

    token_block = pl.BlockSpec((1, half, features), lambda *i: (0, 0, 0))
    return whole_call(
        kernel,
        place,
        [(t, token_block) for t in tokens] + [spots, (weights, ANY)],
        [
            like((rows, features), bf16),
            like((rows, QUERY_AT), bf16),
            like((rows, QD), bf16),
            like((rows, CH), bf16),
            like((rows, 2 * HD), bf16),
            like((16, features), f32),
            like((8, CONV), f32),
            like((1, CH), f32),
        ],
        [
            pltpu.VMEM((HEADS, seq_count, shard, columns), bf16),
            pltpu.SemaphoreType.DMA((HEADS,)),
        ],
        60,
        8,
        deps,
        "project_all",
    )


def exact(values, picks):
    high_part = low(values)
    low_part = low(values - high_part.astype(f32))
    return mul(high_part, picks) + mul(low_part, picks)


def small_rows(place, grad_taps, sums, grad_skip, spots, shard, features, deps=()):
    spans = -(-MH // shard)
    total = 8 + 3 * spans
    rows = -(-total // 16) * 16

    def kernel(place, grad_taps, sums, grad_skip, spots, out):
        places = iota((CONV, features), 1)
        turned = spots[...].T
        for half in range(2):
            picks = low(places == turned[:CONV, half : half + 1])
            out[4 * half : 4 * half + 4, :] = exact(grad_taps[...], picks)[0:4, :]
        by_head = low(iota((CH, 128), 0) // MP == iota((CH, 128), 1))
        skips = exact(grad_skip[...], by_head)[0:1, :]
        values = jnp.concatenate([sums[0:2, :], skips, jnp.zeros((5, 128), f32)], axis=0)
        within = iota((128, features), 1) % shard - place[0] * MIX
        head = iota((128, features), 0)
        for j in range(spans):
            spread = exact(values, low((head == within + shard * j) & (head < MIX)))
            for i in range(3):
                at = 8 + i * spans + j
                out[at : at + 1, :] = spread[i : i + 1, :]
        out[total:, :] = jnp.zeros((rows - total, features), f32)

    return whole_call(
        kernel,
        place,
        [grad_taps, sums, grad_skip, spots],
        [like((rows, features), f32)],
        [],
        16,
        2,
        deps,
        "small_rows",
    )[0]


def pack_weights(place, state, steps, split, pairs, late):
    shard = state.shape[0]
    counts = [w.shape[1] // HEADS for w in split + late]
    columns = 2 * NS + 128 + sum(counts) + 2 * HD
    group = HEADS // KVH

    def kernel(place, *refs):
        outs = refs[-HEADS:]
        state, steps, pairs = refs[0], refs[1], refs[2]
        inputs, query, gate, ff_gate, ff_up = refs[3:-HEADS]
        for m in range(HEADS):
            j = place[0] ^ m

            def cut(ref, wide, at=0, spot=j):
                return ref[:, pl.ds(pl.multiple_of(at + spot * wide, 128), wide)]

            both = j // group
            blocks = [
                cut(inputs, CH), state[...], steps[j], cut(query, QD), cut(gate, CH),
                cut(pairs, HD, 0, both), cut(pairs, HD, KVH * HD, both),
                cut(ff_gate, counts[3]), cut(ff_up, counts[4]),
            ]
            at = 0
            for block in blocks:
                outs[m][:, at : at + block.shape[1]] = block
                at += block.shape[1]

    return whole_call(
        kernel,
        place,
        [state, steps, pairs] + split + late,
        [like((shard, columns), bf16)] * HEADS,
        [],
        60,
        2,
        (),
        "pack_weights",
    )


def gate_of(z_tile):
    z = z_tile.astype(f32)
    return z, jax.nn.sigmoid(z)


def lanes_of(rows, p):
    left = iota((rows.shape[1], TILE), 1) < MP
    first, second = rows[2 * p : 2 * p + 1, :], rows[2 * p + 1 : 2 * p + 2, :]
    return jnp.where(left, column_of(first, TILE), column_of(second, TILE))


def mix_tokens(y0, cums, reads, packs, z, deps=()):
    rows = y0.shape[0]
    wide = rows // HEADS
    count = len(packs)

    def kernel(y0, cums, reads, z, *refs):
        packs, (mixed_out, squares, incoming) = refs[:count], refs[count:]
        sum_packs(packs, incoming)
        for t in range(HEADS):
            here = slice(wide * t, wide * (t + 1))
            met = mul(reads[here, :], low(incoming[...]), NT)
            growth = jnp.exp(cums[:, here])
            grown = jnp.concatenate([lanes_of(growth, p) for p in range(PAIRS)], axis=1)
            mixed = low(y0[here, :] + grown * met)
            mixed_out[here, :] = mixed
            gate, sig = gate_of(z[here, :])
            inner = mixed.astype(f32) * gate * sig
            squares[:, here] = row_sums(inner * inner)

    return whole_call(
        kernel,
        None,
        [y0, cums, reads, z, *packs],
        [like((rows, CH), bf16), like((1, rows), f32), like((CH, NS), f32)],
        [],
        20,
        3,
        deps,
        "mix_tokens",
    )


def branch_out(mixed, z, scale, gain, attended, weights, deps=()):
    rows, features = mixed.shape[0], weights.shape[1]
    wide = rows // HEADS
    specs, shapes = scatter_outs(wide // 2, features)

    def kernel(mixed, z, scale, gain, attended, weights, gated_out, *parts):
        gate, sig = gate_of(z[...])
        inner = mixed[...].astype(f32) * gate * sig
        gated = low(inner * column_of(scale[...], CH) * gain[...])
        gated_out[...] = gated
        value = mul(gated, weights[:CH, :]) + mul(attended[...], weights[CH:, :])
        put_scatter(pl.program_id(0), value, parts)

    outs = tiled_call(
        kernel,
        HEADS,
        [
            by_ring(wide, CH),
            by_ring(wide, CH),
            pl.BlockSpec((1, wide), lambda i: (0, ring(i))),
            pl.BlockSpec((1, CH), lambda i: (0, 0)),
            by_ring(wide, QD),
            fixed_block(CH + QD, features),
        ],
        [by_ring(wide, CH)] + specs,
        [jax.ShapeDtypeStruct((rows, CH), bf16)] + shapes,
        [],
        3,
        deps,
        "branch_out",
    )(mixed, z, scale, gain, attended, weights, *deps)
    return outs[0], outs[1:]


def feed_forward(tokens, grads, weights, weights_down, deps=()):
    wide, features = 2 * tokens[0].shape[0], tokens[0].shape[1]
    rows = wide * HEADS
    ff = weights_down.shape[0]
    specs, shapes = scatter_outs(wide // 2, features)

    def kernel(*refs):
        tokens, grads = refs[:8], refs[8:16]
        weights, weights_down, tokens_out, grads_out, acted_out, inner_out = refs[16:22]
        parts, held, held_grads = refs[22:27], refs[27], refs[28]
        i = pl.program_id(0)
        x = load_piece(i, tokens, held)
        g = load_piece(i, grads, held_grads, 1)
        tokens_out[...] = x
        grads_out[...] = g
        inner = mul(x, weights[...])
        grad_acted = mul(g, weights_down[...], NT)
        gate, up = inner[:, :ff], inner[:, ff:]
        sig = jax.nn.sigmoid(gate)
        silu = gate * sig
        acted_out[...] = low(silu * up)
        grad_gate = low(grad_acted * up * (sig * (1.0 + gate * (1.0 - sig))))
        grad_inner = jnp.concatenate([grad_gate, low(grad_acted * silu)], axis=1)
        inner_out[...] = grad_inner
        put_scatter(i, mul(grad_inner, weights[...], NT), parts)

    outs = tiled_call(
        kernel,
        HEADS,
        piece_specs(tokens)
        + piece_specs(grads)
        + [
            fixed_block(features, 2 * ff),
            fixed_block(ff, features),
        ],
        [by_ring(wide, features), by_ring(wide, features), by_ring(wide, ff), by_ring(wide, 2 * ff)]
        + specs,
        [
            jax.ShapeDtypeStruct((rows, features), bf16),
            jax.ShapeDtypeStruct((rows, features), bf16),
            jax.ShapeDtypeStruct((rows, ff), bf16),
            jax.ShapeDtypeStruct((rows, 2 * ff), bf16),
        ]
        + shapes,
        [pltpu.VMEM((wide, features), bf16), pltpu.VMEM((wide, features), bf16)],
        7,
        deps,
        "feed_forward",
    )(*tokens, *grads, weights, weights_down, *deps)
    return outs[0], outs[1], outs[2], outs[3], outs[4:]


def scattered_product(left, weights, deps=()):
    rows, depth = left.shape
    features = weights.shape[1]
    wide = rows // HEADS
    specs, shapes = scatter_outs(wide // 2, features)

    def kernel(left, weights, *parts):
        put_scatter(pl.program_id(0), mul(left[...], weights[...]), parts)

    return tiled_call(
        kernel,
        HEADS,
        [by_ring(wide, depth), fixed_block(depth, features)],
        specs,
        shapes,
        [],
        2,
        deps,
        "scattered_product",
    )(left, weights, *deps)


def branch_back(grads, weights, attended, mixed, z, scale, gain, deps=()):
    wide, features = 2 * grads[0].shape[0], grads[0].shape[1]
    rows = wide * HEADS
    heads = QD // HD

    def kernel(*refs):
        grads = refs[:8]
        weights, attended, mixed, z, scale, gain = refs[8:14]
        grads_out, grad_att, terms, grad_gated, sums, held = refs[14:]
        i = pl.program_id(0)
        g = load_piece(i, grads, held)
        grads_out[...] = g
        both = mul(g, weights[...], NT)
        att = low(both[:, CH:])
        grad_att[...] = att
        product = att.astype(f32) * attended[...].astype(f32)
        for j in range(heads):
            terms[j] = row_sums(product[:, HD * j : HD * (j + 1)])
        gate, sig = gate_of(z[...])
        unit = mixed[...].astype(f32) * gate * sig * column_of(scale[...], CH)
        gated = both[:, :CH]
        grad_gated[...] = low(gated)
        scaled = gated * unit
        sums[...] = row_sums(scaled * gain[...])

    return tiled_call(
        kernel,
        HEADS,
        piece_specs(grads)
        + [
            fixed_block(CH + QD, features),
            by_ring(wide, QD),
            by_ring(wide, CH),
            by_ring(wide, CH),
            pl.BlockSpec((1, wide), lambda i: (0, ring(i))),
            pl.BlockSpec((1, CH), lambda i: (0, 0)),
        ],
        [
            by_ring(wide, features),
            by_ring(wide, QD),
            pl.BlockSpec((heads, 1, wide), lambda i: (0, 0, ring(i))),
            by_ring(wide, CH),
            pl.BlockSpec((1, wide), lambda i: (0, ring(i))),
        ],
        [
            jax.ShapeDtypeStruct((rows, features), bf16),
            jax.ShapeDtypeStruct((rows, QD), bf16),
            jax.ShapeDtypeStruct((heads, 1, rows), f32),
            jax.ShapeDtypeStruct((rows, CH), bf16),
            jax.ShapeDtypeStruct((1, rows), f32),
        ],
        [pltpu.VMEM((wide, features), bf16)],
        4,
        deps,
        "branch_back",
    )(*grads, weights, attended, mixed, z, scale, gain, *deps)


def gate_back(grad_gated, mixed, z, scale, mean, gain, cums, reads, packed, deps=()):
    rows = mixed.shape[0]
    wide = rows // HEADS

    def kernel(
        grad_gated, mixed, z, scale, mean, gain, cums, reads, packed, grad_mixed, grad_z, leaving
    ):
        total = None
        for t in range(HEADS):
            here = slice(wide * t, wide * (t + 1))
            gate, sig = gate_of(z[here, :])
            silu = gate * sig
            value = mixed[here, :].astype(f32)
            factor = column_of(scale[:, here], CH)
            unit = value * silu * factor
            inner = grad_gated[here, :].astype(f32) * gain[...]
            inner = (inner - unit * column_of(mean[:, here], CH)) * factor
            out = low(inner * silu)
            grad_mixed[here, :] = out
            grad_z[here, :] = low(inner * value * (sig * (1.0 + gate * (1.0 - sig))))
            growth = jnp.exp(cums[:, here])
            grown = jnp.concatenate([lanes_of(growth, p) for p in range(PAIRS)], axis=1)
            part = mul(low(out.astype(f32) * grown), reads[here, :], TN)
            total = part if total is None else total + part
        leaving[:CH, :] = low(total)
        leaving[CH:, :] = packed[CH:, :]

    return whole_call(
        kernel,
        None,
        [grad_gated, mixed, z, scale, mean, gain, cums, reads, packed],
        [like((rows, CH), bf16), like((rows, CH), bf16), like((CH + 16, NS), bf16)],
        [],
        20,
        3,
        deps,
        "gate_back",
    )


def normed_back(place, grad_pre, grad_z, grad_query, grad_pair, weights, deps=()):
    rows = grad_pre.shape[0]
    wide = rows // HEADS
    half = wide // 2
    seq_count, _, shard, columns = weights.shape
    features = HEADS * seq_count * shard
    ANY = pl.BlockSpec(memory_space=pl.ANY)

    def kernel(place, grad_pre, grad_query, grad_z, grad_pair, source, *refs):
        send_one, send_two, keep_one, keep_two, own, held, sems = refs
        copies = fetch_weights(source, held, sems, place)
        for copy in copies:
            copy.start()
        for copy in copies:
            copy.wait()
        for k in (1, 3, 2, 0):
            here = slice(wide * k, wide * (k + 1))
            grads = jnp.concatenate(
                [grad_pre[here, :], grad_query[here, :], grad_z[here, :], grad_pair[here, :]],
                axis=1,
            )
            parts = []
            for j in range(HEADS):
                part = held[j]
                if shard % 16 != 0:
                    part = part.astype(f32)
                parts.append(mul(grads, low(part.reshape(seq_count * shard, columns)), NT))
            value = jnp.concatenate(parts, axis=1)
            top, bottom = low(value[:half]), low(value[half:])
            if k == 1:
                send_one[0] = top
                keep_two[...] = bottom
            elif k == 3:
                send_one[1] = top
                send_two[0] = bottom
            elif k == 2:
                keep_one[...] = top
                send_two[1] = bottom
            else:
                own[...] = value

    shapes = scatter_outs(half, features)[1]
    return whole_call(
        kernel,
        place,
        [grad_pre, grad_query, grad_z, grad_pair, (weights, ANY)],
        shapes,
        [
            pltpu.VMEM((HEADS, seq_count, shard, columns), bf16),
            pltpu.SemaphoreType.DMA((HEADS,)),
        ],
        40,
        6,
        deps,
        "normed_back",
    )


def to_head(x, mask):
    return lax.ppermute(x, "head", [(i, i ^ mask) for i in range(HEADS)])


def to_seq(x, mask):
    return lax.ppermute(x, "seq", [(i, i ^ mask) for i in range(lax.axis_size("seq"))])


def shifted(x, blocks):
    count = lax.axis_size("seq")
    route = [(i, i + 2 * blocks) for i in range(count) if 0 <= i + 2 * blocks < count]
    return lax.ppermute(x, "seq", route)


def gather_head(top, bottom):
    one_top = to_head(top, 1)
    two_bottom = to_head(bottom, 2)
    one_bottom = to_head(bottom, 1)
    two_top = to_head(top, 2)
    three_top = to_head(one_top, 2)
    three_bottom = to_head(two_bottom, 1)
    return top, bottom, one_top, one_bottom, two_top, two_bottom, three_top, three_bottom


def gather_rows_low(x):
    half = x.shape[0] // 2
    return gather_head(low(x[:half]), low(x[half:]))


def pin(x, *deps):
    if len(deps) == 0:
        return x
    return lax.optimization_barrier((x,) + deps)[0]


def add_low(*terms):
    return low(sum((t.astype(f32) for t in terms[1:]), terms[0].astype(f32)))


def sum_head(row):
    wide = row.shape[1] // HEADS
    total = row
    for mask in range(1, HEADS):
        got = to_head(row, mask)
        total = total + jnp.concatenate(
            [got[:, wide * (k ^ mask) : wide * ((k ^ mask) + 1)] for k in range(HEADS)], axis=1
        )
    return total


def send_packs(packed, blocks, direction):
    return [shifted(packed, direction * k) for k in range(1, blocks)]


def gather_rows(shard):
    return lax.all_gather(shard, "seq", axis=0, tiled=False)


def scatter_rows(x):
    return lax.psum_scatter(x, "seq", scatter_dimension=0, tiled=False)


def in_order(pieces, index):
    bit = 1
    while bit < len(pieces):
        upper = (index & bit) != 0
        pieces = [jnp.where(upper, pieces[j ^ bit], pieces[j]) for j in range(len(pieces))]
        bit *= 2
    return pieces


def ordered_rows(x, head_index):
    parts = [
        lax.dynamic_index_in_dim(x, head_index ^ j, 1, keepdims=False) for j in range(HEADS)
    ]
    return jnp.stack(parts).reshape(-1, x.shape[-1])


def scatter_direct(x, core, block):
    blocks = x.shape[0] // 2
    x = x.reshape((blocks, 2) + x.shape[1:])
    pick = lambda c: lax.dynamic_index_in_dim(x, c, 1, keepdims=False)
    x = add_low(pick(core), to_seq(pick(1 - core), 1))
    parts = [lax.dynamic_index_in_dim(x, block, 0, keepdims=False)]
    for k in range(1, blocks):
        part = lax.dynamic_index_in_dim(x, block ^ k, 0, keepdims=False)
        parts.append(to_seq(part, 2 * k))
    return parts


LATE = QD + 2 * HD
EARLY_AT = LATE + 128
FF_AT = EARLY_AT + CH + QUERY_AT


def merge_columns(place, late, early, ff):
    shard, ff_wide = ff.shape[1:]
    columns = FF_AT + ff_wide
    count = len(late)

    def kernel(place, *refs):
        late, early, ff, outs = refs[:count], refs[count], refs[count + 1], refs[count + 2 :]
        for m in range(HEADS):
            j = place[0] ^ m
            out = outs[m]
            blocks = [part[j].astype(f32) for part in late]
            out[:, :LATE] = low(sum(part[:, :LATE] for part in blocks))
            small = in_order([part[:, LATE:] for part in blocks], place[2])
            out[:, LATE:EARLY_AT] = low(sum(small))
            out[:, EARLY_AT:FF_AT] = early[j]
            out[:, FF_AT:] = ff[j]

    return whole_call(
        kernel,
        place,
        [*late, early, ff],
        [like((shard, columns), bf16)] * HEADS,
        [],
        16,
        2,
        (),
        "merge_columns",
    )


def finish_columns(place, pieces, weights, gains, conv_shard):
    shard = pieces[0].shape[0]
    ff = weights[6].shape[1] // HEADS
    spans = -(-MH // shard)
    at_state = EARLY_AT + CH
    at_step = EARLY_AT + STEP_AT
    at_gate = EARLY_AT + QUERY_AT

    def fold(weight, grad):
        product = weight.astype(f32) * grad
        tiles = [product[:, 128 * i : 128 * (i + 1)] for i in range(product.shape[1] // 128)]
        return sum(tiles[1:], tiles[0])

    def kernel(place, *refs):
        pieces = refs[:HEADS]
        inputs_w, state_w, step_w, query_w, gate_w, pair_w, ff_w, up_w = refs[4:12]
        gain_in, gain_two = refs[12:14]
        inputs, states, steps, query, gate, pair, ff_gate, ff_up = refs[14:22]
        grad_in, grad_two, taps, *heads = refs[22:]
        owners = [place[0] ^ m for m in range(HEADS)]

        def spread(out, weight, start, wide):
            total = jnp.zeros((shard, 128), f32)
            for m in range(HEADS):
                here = pl.ds(pl.multiple_of(owners[m] * wide, 128), wide)
                grad = pieces[m][:, start : start + wide].astype(f32)
                out[:, here] = grad
                total = total + fold(weight[:, here], grad)
            return total

        first = spread(inputs, inputs_w, EARLY_AT, CH) + spread(query, query_w, 0, QD)
        first = first + spread(gate, gate_w, at_gate, CH)
        second = spread(ff_gate, ff_w, FF_AT, ff) + spread(ff_up, up_w, FF_AT + ff, ff)
        grad = sum(p[:, at_state : at_state + 2 * NS].astype(f32) for p in pieces)
        states[...] = grad
        first = first + fold(state_w[...], grad)
        for i in range(KVH):
            for kind in range(2):
                start = QD + HD * kind
                grad = jnp.zeros((shard, HD), f32)
                for m in range(HEADS):
                    mine = (owners[m] // (HEADS // KVH)) == i
                    part = pieces[m][:, start : start + HD].astype(f32)
                    grad = grad + jnp.where(mine, part, 0.0)
                lanes = slice(HD * (KVH * kind + i), HD * (KVH * kind + i + 1))
                pair[:, lanes] = grad
                first = first + fold(pair_w[:, lanes], grad)
        grad = jnp.zeros((shard, 128), f32)
        source, target = iota((128, 128), 0), iota((128, 128), 1)
        for m in range(HEADS):
            moved = low((target == source + owners[m] * MIX) & (source < MIX))
            grad = grad + mul(pieces[m][:, at_step : at_step + 128], moved)
        steps[...] = grad[:, :MH]
        step_sum = jnp.sum(step_w[...].astype(f32) * grad[:, :MH], axis=1, keepdims=True)

        def turned(x):
            return jnp.concatenate([x, jnp.zeros((128 - shard, 128), f32)], axis=0).T

        def row(total, extra):
            column = jnp.sum(total, axis=1, keepdims=True) + extra
            return turned(jnp.broadcast_to(column, (shard, 128)))[0:1, :shard]

        grad_in[...] = row(first, step_sum) / gain_in[...].astype(f32)
        grad_two[...] = row(second, 0.0) / gain_two[...].astype(f32)
        small = in_order([p[:, LATE:EARLY_AT].astype(f32) for p in pieces], place[0])
        small = sum(small[1:], small[0])
        taps[0:shard, :] = small[:, 0:4]
        taps[shard:conv_shard, :] = small[0 : conv_shard - shard, 4:8]
        rows = turned(small)
        for i in range(3):
            for j in range(spans):
                wide = min(shard, MH - j * shard)
                at = 8 + i * spans + j
                heads[i][:, j * shard : j * shard + wide] = rows[at : at + 1, :wide]

    return whole_call(
        kernel,
        place,
        [*pieces, *weights, *gains],
        [like(w.shape, f32) for w in weights]
        + [like((1, shard), f32)] * 2
        + [like((conv_shard, 4), f32)]
        + [like((1, MH), f32)] * 3,
        [],
        24,
        4,
        (),
        "finish_columns",
    )


def split_columns(x):
    return x.reshape(x.shape[0], HEADS, -1).swapaxes(0, 1)


def body(
    hidden_in,
    lengths,
    cotangent,
    input_gain,
    mixer_gate,
    mixer_inputs,
    state_weights,
    conv_weight,
    step_weight,
    decay_log,
    step_bias,
    skip_gain,
    query_weight,
    key_value_weight,
    mixer_gain,
    mixer_output,
    attention_out,
    second_gain,
    gate_weight,
    up_weight,
    down_weight,
):
    seq_count = lax.axis_size("seq")
    head_index = lax.axis_index("head")
    seq_index = lax.axis_index("seq")
    block = seq_index // 2
    core = seq_index % 2
    blocks = seq_count // 2
    own_rows, features = hidden_in.shape[2], hidden_in.shape[3]
    rows = 2 * own_rows * HEADS
    shard = input_gain.shape[0]
    ff = gate_weight.shape[1] // HEADS
    mix_shard, down_shard = mixer_output.shape[0], down_weight.shape[0]
    conv_shard = conv_weight.shape[0]
    device = head_index * seq_count + seq_index

    def in_columns(x):
        x = x.reshape(x.shape[0], -1)
        rest = jnp.pad(x[shard:], ((0, 2 * shard - x.shape[0]), (0, 0)))
        return [x[:shard], rest]

    small = [input_gain[:, None], second_gain[:, None]]
    small = small + in_columns(mixer_gain) + in_columns(conv_weight)
    small = jnp.concatenate(small, axis=1)
    small = jnp.pad(small, ((0, 0), (0, 128 - GAIN_LANE - small.shape[1])))
    steps = jnp.pad(split_columns(step_weight), ((0, 0), (0, 0), (0, GAIN_LANE - MIX)))
    steps = jnp.concatenate([steps, jnp.broadcast_to(small[None], (HEADS,) + small.shape)], axis=2)
    end_row = ((head_index ^ (HEADS - 1)) * 2 + (1 ^ core)) * TILE + TILE - 16
    place = jnp.stack([head_index, core, block, end_row // 16]).astype(jnp.int32)
    packs = pack_weights(
        place, state_weights, steps, [mixer_inputs, query_weight, mixer_gate], key_value_weight,
        [gate_weight, up_weight],
    )
    wide = packs[0].shape[1] - 2 * ff
    pieces = [packs[0]] + [to_head(packs[m], m) for m in range(1, HEADS)]

    both = jnp.stack([hidden_in[:, 0], cotangent[:, 0]], axis=1)
    keep = lax.dynamic_index_in_dim(both, core, 0, keepdims=False)
    give = lax.dynamic_index_in_dim(both, 1 - core, 0, keepdims=False)
    got = to_seq(give, 1)
    hidden = jnp.concatenate([keep[0], got[0]], axis=0).astype(f32)
    cot = jnp.concatenate([keep[1], got[1]], axis=0)
    first_own = pin(pieces[0], got)
    weights_in = gather_rows(
        jnp.stack([first_own[:, :wide]] + [p[:, :wide] for p in pieces[1:]])
    )
    tokens = 2 * own_rows
    block_rows = own_rows * HEADS
    spot = jnp.arange(tokens)
    positions = (
        (2 * block + ((spot // own_rows) ^ core)) * block_rows
        + head_index * own_rows
        + spot % own_rows
    )
    length = lax.dynamic_index_in_dim(lengths, core, 0, keepdims=False)
    valid = (positions < length).astype(f32)[:, None]
    grad_result_own = cot.astype(f32) * valid
    grad_low = low(grad_result_own)
    both_all = gather_head(
        jnp.stack([keep[0], grad_low[:own_rows]]), jnp.stack([got[0], grad_low[own_rows:]])
    )

    out_pack = jnp.concatenate([mixer_output, attention_out], axis=0)
    out_all = gather_rows(pin(out_pack, *pieces))
    ff_pack = jnp.concatenate([p[:, wide:] for p in pieces] + [down_weight], axis=0)

    def sources(channels, size):
        owner, offset = channels // size, channels % size
        main = jnp.where(offset < shard, owner * shard + offset, -1)
        return jnp.stack([main, jnp.where(offset < shard, -1, owner * shard + offset - shard)])

    spread = jnp.arange(CONV)
    spread = jnp.where(spread < CH, spread + head_index * CH, spread + (MH * MP - CH))
    spots = jnp.concatenate(
        [sources(spread, conv_shard), sources(jnp.arange(CH) + head_index * CH, mix_shard)], axis=1
    )
    spots = jnp.pad(spots, ((0, 6), (0, 0))).astype(jnp.int32)
    (normed, mix_in, query, z, own_pair, small, taps, gain_mix) = project_all(
        place, both_all, weights_in, spots, deps=(ff_pack, out_pack)
    )
    tail = shifted(lax.dynamic_slice(mix_in, (end_row, 0), (16, CONV)), 1)
    gain_in, gain_two = small[0:1], small[1:2]
    scale_in = lax.rsqrt(jnp.mean(hidden * hidden, axis=-1, keepdims=True) + norm_eps)
    unit_in = hidden * scale_in

    pair = [own_pair, shifted(pin(own_pair, tail), 1)]

    decay_part = lax.dynamic_slice_in_dim(-jnp.exp(decay_log), head_index * MIX, MIX)
    bias_part = lax.dynamic_slice_in_dim(step_bias, head_index * MIX, MIX)
    skip_part = lax.dynamic_slice_in_dim(skip_gain, head_index * MIX, MIX)
    heads = jnp.pad(jnp.stack([decay_part, bias_part]), ((0, 6), (0, 128 - MIX)))
    skip = jnp.broadcast_to(jnp.repeat(skip_part, MP)[None], (8, CH))
    y0, reads, cums, starts, runs, packed = mixer_forward(
        place, mix_in, tail, taps, heads, skip
    )
    packs = send_packs(packed, blocks, 1)
    running = attend(place, query, pair[0], 0, None, blocks == 1, deps=(packed,))
    pair.append(shifted(pin(pair[1], running[1], *packs), 1))
    out_all = pin(out_all, packed)
    weights_out = jnp.concatenate(
        [
            out_all[:, :mix_shard].reshape(CH, features),
            out_all[:, mix_shard:].reshape(QD, features),
        ],
        axis=0,
    )
    for k in range(1, blocks):
        running = attend(
            place, query, pair[k], k, running, k == blocks - 1,
            deps=(packed,) if k == 1 else (scale_mix,),
        )
        if k == 1:
            mixed, squares, incoming = mix_tokens(
                y0, cums, reads, packs, z, deps=(running[1], weights_out)
            )
            for j in range(3, blocks):
                pair.append(shifted(pin(pair[-1], squares), 1))
            scale_mix = lax.rsqrt(sum_head(squares) / (MH * MP) + norm_eps)
        if k == blocks - 2:
            ff_all = gather_rows(pin(ff_pack, running[1], pair[-1]))
    attended, logs = running
    ff_all = pin(ff_all, attended)
    weights_ff = ordered_rows(
        ff_all[:, : HEADS * shard].reshape(seq_count, HEADS, shard, 2 * ff), head_index
    )
    weights_down = ff_all[:, HEADS * shard :].reshape(ff, features)
    gated, parts = branch_out(mixed, z, scale_mix, gain_mix, attended, weights_out)
    resid = hidden + scatter_parts(parts)

    scale_two = lax.rsqrt(jnp.mean(resid * resid, axis=-1, keepdims=True) + norm_eps)
    norm_two = resid * scale_two
    normed_two, grad_result, acted, grad_inner, parts = feed_forward(
        gather_rows_low(norm_two * gain_two), both_all, weights_ff, weights_down
    )
    grad_down = low(mul(acted, grad_result, TN)).reshape(seq_count, down_shard, features)
    ff_rows = jnp.concatenate(
        [weight_rows(normed_two, [grad_inner], seq_count), grad_down], axis=1
    )
    ff_sum = scatter_rows(ff_rows)

    down_parts = scattered_product(acted, weights_down)
    grad_two = scatter_parts(parts, (ff_rows, grad_down, down_parts[0]))
    grad_two = grad_two * gain_two
    grad_resid = grad_result_own + scale_two * (
        grad_two - norm_two * jnp.mean(grad_two * norm_two, axis=-1, keepdims=True)
    )

    grad_branch, grad_attended, terms, grad_gated, sums_mix = branch_back(
        gather_rows_low(grad_resid), weights_out, attended, mixed, z, scale_mix, gain_mix,
    )
    mean_mix = sum_head(sums_mix) / (MH * MP)
    down_parts = [pin(p, terms) for p in down_parts]

    out_rows = jnp.concatenate(
        [
            low(mul(gated, grad_branch, TN)).reshape(seq_count, mix_shard, features),
            low(mul(attended, grad_branch, TN)).reshape(seq_count, shard, features),
        ],
        axis=1,
    )
    out_sum = scatter_rows(out_rows)

    def back_step(k, grad_query, deps):
        return attend_back(
            place, query, grad_attended, logs, terms, pair[k], grad_query, k, deps=deps
        )

    grad_query, kept = back_step(blocks - 1, None, ())
    chain = shifted(kept, -1)
    grad_mixed, grad_z, leaving = gate_back(
        grad_gated, mixed, z, scale_mix, mean_mix, gain_mix, cums, reads, packed,
        deps=(grad_query,),
    )
    back_packs = send_packs(leaving, blocks, -1)
    for k in range(blocks - 2, 1, -1):
        grad_query, kept = back_step(k, grad_query, (leaving, out_rows))
        if k > 2:
            chain = shifted(add_low(kept, chain), -1)
    grad_pre, first, grad_taps, sums, grad_skip = mixer_backward(
        place, mix_in, tail, taps, heads, skip, starts, runs, incoming, grad_mixed, back_packs,
        deps=(grad_query, chain),
    )
    from_next = shifted(first, -1)
    chain = shifted(add_low(kept, pin(chain, from_next)), -1)
    grad_query, kept = back_step(1, grad_query, (sums,))
    grad_pre = fix_ends(place, grad_pre, from_next, taps)
    early_rows = weight_rows(normed, [grad_pre, grad_z], seq_count, deps=(grad_query,))
    early_sum = scatter_rows(early_rows)
    chain = shifted(add_low(kept, pin(chain, early_rows)), -1)
    grad_query, kept = back_step(0, grad_query, (early_rows,))
    chain = add_low(kept, chain)

    small_part = small_rows(
        place, grad_taps, sums, grad_skip, spots, shard, features, deps=(early_rows,)
    )
    late_rows = weight_rows(normed, [grad_query, chain], seq_count, extra=(small_part,))
    late_parts = scatter_direct(
        late_rows.reshape(seq_count, HEADS, shard, late_rows.shape[2]), core, block
    )
    parts = normed_back(
        place, grad_pre, grad_z, grad_query, chain, weights_in, deps=(late_rows,)
    )
    grad_normed = scatter_parts(parts) * gain_in
    result = (resid + scatter_parts(down_parts, (parts[0],))) * valid
    merged = merge_columns(
        place,
        late_parts,
        early_sum.reshape(HEADS, shard, -1),
        ff_sum.reshape(-1, shard, features),
    )
    pieces = [merged[0]] + [to_head(merged[m], m) for m in range(1, HEADS)]
    (
        grad_inputs, states, grad_steps, grad_queries, grad_gate, key_values, grad_ff_gate,
        grad_ff_up, grad_gain_in, grad_gain_two, grad_conv, *head_sums,
    ) = finish_columns(
        place, pieces,
        [
            mixer_inputs, state_weights, step_weight, query_weight, mixer_gate, key_value_weight,
            gate_weight, up_weight,
        ],
        [input_gain[None], second_gain[None]], conv_shard,
    )
    grad_hidden = grad_resid + scale_in * (
        grad_normed - unit_in * jnp.mean(grad_normed * unit_in, axis=-1, keepdims=True)
    )

    def back(x):
        x = x.reshape(2, own_rows, features)
        arrived = to_seq(x[1], 1)
        return jnp.stack(
            [jnp.where(core == 0, x[0], arrived), jnp.where(core == 0, arrived, x[0])]
        )[:, None]

    grad_mixer_output = out_sum[:mix_shard].astype(f32)

    grad_gain_mix = jnp.sum(mixer_output.astype(f32) * grad_mixer_output, axis=1)
    return (
        back(result),
        back(grad_hidden),
        grad_gain_in[0],
        grad_gate,
        grad_inputs,
        states,
        grad_conv,
        grad_steps,
        head_sums[0][0],
        head_sums[1][0],
        head_sums[2][0],
        grad_queries,
        key_values,
        grad_gain_mix / mixer_gain.astype(f32),
        grad_mixer_output,
        out_sum[mix_shard:].astype(f32),
        grad_gain_two[0],
        grad_ff_gate,
        grad_ff_up,
        ff_sum[HEADS * shard :].astype(f32),
    )


def solution(mesh):
    tokens = P(None, "seq", "head", None)
    split = P(("head", "seq"), None)
    line = P(("head", "seq"))
    whole = P()
    in_specs = (
        tokens, whole, tokens, line, split, split, split, split, split, whole, whole, whole,
        split, split, line, split, split, line, split, split, split,
    )
    out_specs = (
        tokens, tokens, line, split, split, split, split, split, whole, whole, whole, split,
        split, line, split, split, line, split, split, split,
    )
    return jax.shard_map(body, mesh=mesh, in_specs=in_specs, out_specs=out_specs, check_vma=False)
```

```python
import functools

import jax
import jax.numpy as jnp
from jax import lax
from jax.experimental import pallas as pl
from jax.experimental.pallas import tpu as pltpu
from jax.sharding import PartitionSpec as P

QH = 8
KVH = 2
HD = 128
MH = 24
MP = 64
NS = 128
HEADS = 4
MIX = MH // HEADS
CH = MIX * MP
QD = QH // HEADS * HD
CONV = CH + 2 * NS
STEP_AT = CONV
QUERY_AT = STEP_AT + 128
GATE_AT = QUERY_AT + QD
KEY_AT = GATE_AT + CH
TILE = 128
GAIN_LANE = 8
PAIRS = MIX // 2

norm_eps = 1e-05
score_scale = HD ** (-0.5)
exponent_scale = score_scale * 1.4426950408889634
highest = lax.Precision.HIGHEST
f32 = jnp.float32
bf16 = jnp.bfloat16
NN = ((1,), (0,))
NT = ((1,), (1,))
TN = ((0,), (0,))
BIG = 1e30
VMEM = 24


def low(x):
    return x.astype(bf16)


def mul(left, right, sides=NN, precision=None):
    return lax.dot_general(
        left, right, (sides, ((), ())), preferred_element_type=f32, precision=precision
    )


def params(megabytes, **more):
    return pltpu.CompilerParams(vmem_limit_bytes=megabytes * 1024 * 1024, **more)


def taking(micros):
    micros = micros * 0.25
    return pl.CostEstimate(
        flops=int(micros * 1.1e9), bytes_accessed=int(micros * 3.6e6), transcendentals=0
    )


def unread(deps):
    return [pl.BlockSpec(memory_space=pl.ANY)] * len(deps)


def iota(shape, dim):
    return lax.broadcasted_iota(jnp.int32, shape, dim)


def tile_of(g, place):
    blocks = TILE * HEADS // TILE
    return ((g % blocks) ^ place[0]) * 2 + ((g // blocks) ^ place[1])


def conv_sums(ext, taps):
    total = ext[5:133, :] * taps[0:1, :]
    for k in range(1, 4):
        total = total + ext[5 + k : 133 + k, :] * taps[k : k + 1, :]
    return total


def mul_exact(picks, values):
    high_part = low(values)
    low_part = low(values - high_part.astype(f32))
    return mul(picks, high_part) + mul(picks, low_part)


def step_sizes(raw, heads):
    rows = iota((TILE, TILE), 0)
    cols = iota((TILE, TILE), 1)
    lower = rows >= cols
    moved = raw + heads[1:2, :]
    delta = jnp.maximum(moved, 0.0) + jnp.log1p(jnp.exp(-jnp.abs(moved)))
    cum = mul_exact(low(lower), heads[0:1, :] * delta)
    return moved, delta, cum, lower


def head_terms(delta, cum, lower, left):
    cum_rows = cum.T
    decays, both, sizes = [], [], []
    for p in range(PAIRS):
        columns = []
        for h in (2 * p, 2 * p + 1):
            column = jnp.broadcast_to(cum[:, h : h + 1], (TILE, TILE))
            decays.append(jnp.exp(jnp.where(lower, column - cum_rows[h : h + 1, :], -BIG)))
            columns.append(column)
        both.append(jnp.where(left, columns[0], columns[1]))
        sizes.append(jnp.where(left, delta[:, 2 * p : 2 * p + 1], delta[:, 2 * p + 1 : 2 * p + 2]))
    return decays, jnp.concatenate(both, axis=1), jnp.concatenate(sizes, axis=1)


def head_rows(values, top):
    return jnp.concatenate([row_pair(values, p, top) for p in range(PAIRS)], axis=0)


def row_pair(values, p, top):
    return jnp.where(top, values[:, 2 * p : 2 * p + 1], values[:, 2 * p + 1 : 2 * p + 2])


def halves(x, left):
    none = jnp.zeros_like(x)
    return jnp.concatenate([jnp.where(left, x, none), jnp.where(left, none, x)], axis=0)


def tile_rows(g, place):
    return pl.ds(pl.multiple_of(tile_of(g, place) * TILE, TILE), TILE)


def pack_rows(state, total):
    high_part = low(total).astype(f32)
    rows = jnp.concatenate([high_part, total - high_part, jnp.zeros((14, 128), f32)], axis=0)
    return jnp.concatenate([low(state), low(rows)], axis=0)


def sum_packs(packs, out):
    top = iota((TILE, NS), 0) < MP
    out[...] = jnp.zeros_like(out)
    passed = jnp.zeros((1, 128), f32)
    for pack in packs:
        factor = jnp.exp(passed)
        for p in range(PAIRS):
            lanes = slice(TILE * p, TILE * (p + 1))
            out[lanes, :] = out[lanes, :] + row_pair(factor, p, top) * pack[lanes, :].astype(f32)
        ends = pack[CH : CH + 16, :].astype(f32)
        passed = passed + ends[0:1, :] + ends[1:2, :]


def mixer_forward_kernel(
    place, rest, tail, taps, heads, skip, y0, reads_out, cums, starts, runs, packed,
    ext, state, run,
):
    state[...] = jnp.zeros_like(state)
    run[...] = jnp.zeros_like(run)
    ext[0:8, :] = tail[...].astype(f32)[8:16, :]

    def one_tile(g, unused):
        here = tile_rows(g, place)
        pre = rest[here, :CONV].astype(f32)
        ext[8:136, :] = pre
        total = conv_sums(ext, taps)
        act = total * jax.nn.sigmoid(total)
        ext[0:8, :] = pre[120:128, :]
        writes = low(act[:, CH : CH + NS])
        reads = low(act[:, CH + NS :])
        reads_out[here, :] = reads
        starts[g] = low(state[...])
        runs[g] = run[...]
        _, delta, cum, lower = step_sizes(rest[here, STEP_AT:].astype(f32), heads)
        left = iota((TILE, TILE), 1) < MP
        top = iota((TILE, TILE), 0) < MP
        meet = mul(reads, writes, NT)
        cums[:, here] = (cum + run[0:1, :]).T[0:8, :]
        last_row = cum[127:128, :]
        decays, both, sizes = head_terms(delta, cum, lower, left)
        x = act[:, :CH]
        xd = x * sizes
        held = state[...]
        carried = jnp.exp(both) * mul(reads, low(held), NT)
        out = []
        for p in range(PAIRS):
            lanes = slice(TILE * p, TILE * (p + 1))
            mix = jnp.concatenate([low(meet * d) for d in decays[2 * p : 2 * p + 2]], axis=1)
            out.append(mul(mix, low(halves(xd[:, lanes], left))))
        y0[here, :] = jnp.concatenate(out, axis=1) + carried + skip[0:1, :] * x
        xw = low(jnp.exp(both[127:128, :] - both) * xd)
        state[...] = head_rows(jnp.exp(last_row), top) * held + mul(xw, writes, TN)
        run[...] = run[...] + last_row
        return unused

    lax.fori_loop(0, rest.shape[0] // TILE, one_tile, 0, unroll=2)
    packed[...] = pack_rows(state[...], run[0:1, :])


def skipping(kernel, before, count):
    def run(*refs):
        kernel(*refs[:before], *refs[before + count :])

    return run


def whole_block(*shape):
    return pl.BlockSpec(shape, lambda *i: (0,) * len(shape))


def whole_call(kernel, place, args, outs, scratch, megabytes, micros, deps, name):
    count = 0 if place is None else 1
    before = len(args) + count
    specs = [whole_block(*a.shape) if hasattr(a, "shape") else a[1] for a in args]
    args = [a if hasattr(a, "shape") else a[0] for a in args]
    return pl.pallas_call(
        skipping(kernel, before, len(deps)),
        grid_spec=pltpu.PrefetchScalarGridSpec(
            num_scalar_prefetch=count,
            grid=(1,),
            in_specs=specs + unread(deps),
            out_specs=[whole_block(*o.shape) for o in outs],
            scratch_shapes=scratch,
        ),
        out_shape=outs,
        compiler_params=params(megabytes),
        cost_estimate=taking(micros),
        name=name,
    )(*([] if place is None else [place]), *args, *deps)


def like(shape, kind):
    return jax.ShapeDtypeStruct(shape, kind)


def mixer_forward(place, rest, tail, taps, heads, skip, deps=()):
    rows = rest.shape[0]
    tiles = rows // TILE
    return whole_call(
        mixer_forward_kernel,
        place,
        [rest, tail, taps, heads, skip],
        [
            like((rows, CH), f32),
            like((rows, NS), bf16),
            like((8, rows), f32),
            like((tiles, CH, NS), bf16),
            like((tiles, 8, 128), f32),
            like((CH + 16, NS), bf16),
        ],
        [
            pltpu.VMEM((TILE + 8, CONV), f32),
            pltpu.VMEM((CH, NS), f32),
            pltpu.VMEM((8, 128), f32),
        ],
        20,
        6,
        deps,
        "mixer_forward",
    )


def mixer_backward_kernel(
    count, place, rest, tail, taps, heads, skip, starts, runs, incoming, grad_y, *refs
):
    packs = refs[:count]
    grad_pre, first, grad_taps, sums, grad_skip, ext, dext, grad_state = refs[count:]
    sum_packs(packs, grad_state)
    dext[128:136, :] = jnp.zeros((8, CONV), f32)
    grad_taps[...] = jnp.zeros_like(grad_taps)
    sums[...] = jnp.zeros_like(sums)
    grad_skip[...] = jnp.zeros_like(grad_skip)
    tiles = rest.shape[0] // TILE

    def one_tile(step, unused):
        g = tiles - 1 - step
        here = tile_rows(g, place)
        before = tile_of(jnp.maximum(g - 1, 0), place) * TILE + TILE - 16
        before = rest[pl.ds(pl.multiple_of(before, 16), 16), :CONV].astype(f32)
        ext[8:136, :] = rest[here, :CONV].astype(f32)
        ext[0:8, :] = jnp.where(g == 0, tail[...].astype(f32), before)[8:16, :]
        total = conv_sums(ext, taps)
        gate = jax.nn.sigmoid(total)
        act = total * gate
        writes = low(act[:, CH : CH + NS])
        reads = low(act[:, CH + NS :])
        moved, delta, cum, lower = step_sizes(rest[here, STEP_AT:].astype(f32), heads)
        rows = iota((TILE, TILE), 0)
        cols = iota((TILE, TILE), 1)
        left = cols < MP
        top = rows < MP
        meet = mul(reads, writes, NT)
        last_row = cum[127:128, :]
        shrink = jnp.exp(last_row)
        decays, both, sizes = head_terms(delta, cum, lower, left)
        x = act[:, :CH]
        xd = x * sizes
        xd_low = low(xd)
        dy_low = grad_y[here, :]
        dy = dy_low.astype(f32)
        held = starts[g].astype(f32) + head_rows(jnp.exp(runs[g][0:1, :]), top) * incoming[...]
        held_low = low(held)
        ds = grad_state[...]
        ds_low = low(ds)
        from_start = jnp.exp(both)
        to_end = jnp.exp(both[127:128, :] - both)
        carried = from_start * mul(reads, held_low, NT)
        kept = to_end * mul(writes, ds_low, NT)
        dy_start = low(dy * from_start)
        grad_reads = mul(dy_start, held_low)
        grad_writes = mul(low(xd * to_end), ds_low)
        grad_meet = jnp.zeros((TILE, TILE), f32)
        within, backs = [], []
        for p in range(PAIRS):
            lanes = slice(TILE * p, TILE * (p + 1))
            l0, l1 = decays[2 * p : 2 * p + 2]
            dy_two = halves(dy_low[:, lanes], left)
            m0, m1 = low(meet * l0), low(meet * l1)
            dm = mul(dy_two, xd_low[:, lanes], NT)
            grad_meet = grad_meet + dm[:TILE] * l0 + dm[TILE:] * l1
            mix = jnp.concatenate([m0, m1], axis=1)
            within.append(mul(mix, halves(xd_low[:, lanes], left)))
            backs.append(mul(jnp.concatenate([m0, m1], axis=0), dy_two, TN))
        within = jnp.concatenate(within, axis=1)
        backs = jnp.concatenate(backs, axis=1)
        dxd = backs + kept
        grad_x = dxd * sizes + skip[0:1, :] * dy
        kept_part = kept * xd
        along = dy * (within + carried) - kept_part - xd_low.astype(f32) * backs
        grad_skip[0:1, :] = grad_skip[0:1, :] + jnp.sum(dy * x, axis=0, keepdims=True)
        product = held * ds
        ends = [jnp.sum(kept_part, axis=0, keepdims=True)]
        head_of = iota((CH, 128), 0) // MP == iota((CH, 128), 1)
        pick = low(head_of)
        by_row = jnp.sum(product, axis=1, keepdims=True)
        state_part = jnp.sum(jnp.where(head_of, by_row, 0.0), axis=0, keepdims=True)
        grad_state[...] = head_rows(shrink, top) * ds + mul(dy_start, reads, TN)
        meet_low = low(grad_meet)
        grad_reads = grad_reads + mul(meet_low, writes)
        grad_writes = grad_writes + mul(meet_low, reads, TN)
        ends.append(jnp.zeros((7, CH), f32))
        stacked = jnp.concatenate([along, dxd * x] + ends, axis=0)
        high_part = low(stacked)
        low_part = low(stacked - high_part.astype(f32))
        by_head = mul(high_part, pick) + mul(low_part, pick)
        grad_cum = by_head[:TILE]
        grad_delta = by_head[TILE : 2 * TILE]
        last_add = state_part * shrink + by_head[2 * TILE : 2 * TILE + 1]
        grad_cum = grad_cum + jnp.where(rows == TILE - 1, last_add, 0.0)
        later = mul_exact(low(rows <= cols), grad_cum)
        grad_raw = (grad_delta + heads[0:1, :] * later) * jax.nn.sigmoid(moved)
        grad_raw = jnp.where(cols < MIX, grad_raw, 0.0)
        sums[0:1, :] = sums[0:1, :] + heads[0:1, :] * jnp.sum(delta * later, axis=0, keepdims=True)
        sums[1:2, :] = sums[1:2, :] + jnp.sum(grad_raw, axis=0, keepdims=True)
        grad_act = jnp.concatenate([grad_x, grad_writes, grad_reads], axis=1)
        grad_total = grad_act * (gate * (1.0 + total * (1.0 - gate)))
        dext[0:128, :] = grad_total
        out = dext[3:131, :] * taps[0:1, :]
        for k in range(1, 4):
            out = out + dext[3 - k : 131 - k, :] * taps[k : k + 1, :]
        for k in range(4):
            grad_taps[k : k + 1, :] = grad_taps[k : k + 1, :] + jnp.sum(
                grad_total * ext[5 + k : 133 + k, :], axis=0, keepdims=True
            )
        grad_pre[here, :CONV] = low(out)
        grad_pre[here, STEP_AT:] = low(grad_raw)
        dext[128:136, :] = grad_total[0:8, :]
        first[...] = grad_total[0:8, :]
        return unused

    lax.fori_loop(0, tiles, one_tile, 0, unroll=2)


def mixer_backward(
    place, rest, tail, taps, heads, skip, starts, runs, incoming, grad_y, packs, deps=()
):
    rows = rest.shape[0]
    return whole_call(
        functools.partial(mixer_backward_kernel, len(packs)),
        place,
        [rest, tail, taps, heads, skip, starts, runs, incoming, grad_y, *packs],
        [
            like((rows, QUERY_AT), bf16),
            like((8, CONV), f32),
            like((8, CONV), f32),
            like((8, 128), f32),
            like((8, CH), f32),
        ],
        [
            pltpu.VMEM((TILE + 8, CONV), f32),
            pltpu.VMEM((TILE + 8, CONV), f32),
            pltpu.VMEM((CH, NS), f32),
        ],
        24,
        13,
        deps,
        "mixer_backward",
    )


def fix_ends(place, grad_pre, from_next, taps):
    def kernel(place, grad_pre, from_next, taps, out):
        fixed = jnp.zeros((16, CONV), f32)
        rows = iota((16, CONV), 0)
        for d in range(3):
            part = from_next[0:1, :] * taps[d : d + 1, :]
            for k in range(d):
                part = part + from_next[d - k : d - k + 1, :] * taps[k : k + 1, :]
            fixed = fixed + jnp.where(rows == 13 + d, part, 0.0)
        out[:, :CONV] = low(grad_pre[:, :CONV].astype(f32) + fixed)
        out[:, CONV:] = grad_pre[:, CONV:]

    block = pl.BlockSpec((16, QUERY_AT), lambda i, s: (s[3], 0))
    return pl.pallas_call(
        kernel,
        grid_spec=pltpu.PrefetchScalarGridSpec(
            num_scalar_prefetch=1,
            grid=(1,),
            in_specs=[block, whole_block(8, CONV), whole_block(8, CONV)],
            out_specs=block,
        ),
        out_shape=like(grad_pre.shape, bf16),
        input_output_aliases={1: 0},
        compiler_params=params(8),
        cost_estimate=taking(1),
        name="fix_ends",
    )(place, grad_pre, from_next, taps)


def tile_number(stored, place):
    return ((stored % 2) ^ place[1]) * HEADS + ((stored // 2) ^ place[0])


def masked(scores, place, query_tile):
    reach = iota((TILE, TILE), 0) - iota((TILE, TILE), 1)
    rows = []
    for i in range(scores.shape[0] // TILE):
        cols = []
        for j in range(scores.shape[1] // TILE):
            gap = (tile_number(query_tile + j, place) - tile_number(i, place)) * TILE
            part = scores[TILE * i : TILE * (i + 1), TILE * j : TILE * (j + 1)]
            cols.append(jnp.where(reach <= gap, part, -BIG))
        rows.append(jnp.concatenate(cols, axis=1))
    return jnp.concatenate(rows, axis=0)


def attend_kernel(back, closing, count, place, *refs):
    diagonal = back == 0
    query, pair = refs[:2]
    refs = refs[2:]
    if not diagonal:
        acc_in, stat_in = refs[:2]
        refs = refs[2:]
    refs = refs[count:]
    if closing:
        attended, logs = refs
    else:
        acc_out, stat_out = refs
    wide = 256
    columns = query.shape[0]
    items = [
        (j, slice(wide * i, wide * (i + 1))) for i in range(columns // wide) for j in range(QD // HD)
    ]

    def put(j, cols, acc, new, total):
        if closing:
            attended[cols, HD * j : HD * (j + 1)] = low((acc / total).T)
            logs[j, :, cols] = new + jnp.log2(total)
        else:
            acc_out[j, :, cols] = acc
            stat_out[j, 0:1, cols] = new
            stat_out[j, 1:2, cols] = total

    def work():
        keys = pair[:, :HD]
        vals = pair[:, HD:]

        def start(j, cols):
            scores = mul(keys, query[cols, HD * j : HD * (j + 1)], NT)
            return masked(scores, place, cols.start // TILE) if diagonal else scores

        def weigh(scores, j, cols):
            new = jnp.max(scores, axis=0, keepdims=True) * exponent_scale
            if not diagonal:
                new = jnp.maximum(new, stat_in[j, 0:1, cols])
            probs = jnp.exp2(scores * exponent_scale - new)
            return low(probs), jnp.sum(probs, axis=0, keepdims=True), new

        def finish(probs, total, new, j, cols):
            acc = mul(vals, probs, TN)
            if not diagonal:
                fade = jnp.exp2(stat_in[j, 0:1, cols] - new)
                total = total + stat_in[j, 1:2, cols] * fade
                acc = acc + acc_in[j, :, cols] * fade
            put(j, cols, acc, new, total)

        scores = start(*items[0])
        pending = None
        for n, item in enumerate(items):
            following = start(*items[n + 1]) if n + 1 < len(items) else None
            weighed = weigh(scores, *item)
            if pending is not None:
                finish(*pending)
            pending = weighed + item
            scores = following
        finish(*pending)

    if diagonal:
        work()
    else:
        active = place[2] >= back
        pl.when(active)(work)

        @pl.when(jnp.logical_not(active))
        def _():
            for j, cols in items:
                put(j, cols, acc_in[j, :, cols], stat_in[j, 0:1, cols], stat_in[j, 1:2, cols])


def attend(place, query, pair, back, carried, closing, deps=()):
    diagonal = back == 0
    rows = query.shape[0]
    heads = QD // HD
    whole = lambda *shape: pl.BlockSpec(shape, lambda i, s: (0,) * len(shape))
    in_specs = [
        whole(rows, QD),
        whole(rows, 2 * HD),
    ]
    running = [whole(heads, HD, rows), whole(heads, 8, rows)]
    if not diagonal:
        in_specs += running
    if closing:
        out_specs = [whole(rows, QD), whole(heads, 1, rows)]
        out_shape = [
            jax.ShapeDtypeStruct((rows, QD), bf16),
            jax.ShapeDtypeStruct((heads, 1, rows), f32),
        ]
    else:
        out_specs = running
        out_shape = [
            jax.ShapeDtypeStruct((heads, HD, rows), f32),
            jax.ShapeDtypeStruct((heads, 8, rows), f32),
        ]
    return pl.pallas_call(
        functools.partial(attend_kernel, back, closing, len(deps)),
        grid_spec=pltpu.PrefetchScalarGridSpec(
            num_scalar_prefetch=1,
            grid=(1,),
            in_specs=in_specs + unread(deps),
            out_specs=out_specs,
        ),
        out_shape=out_shape,
        compiler_params=params(16),
        cost_estimate=taking(5),
        name="attend",
    )(place, query, pair, *(() if diagonal else carried), *deps)


def attend_back_kernel(back, opening, count, place, *refs):
    diagonal = back == 0
    query, grad_out, logs, terms, pair = refs[:5]
    refs = refs[5:]
    if not opening:
        grad_in = refs[0]
        refs = refs[1:]
    grad_query, grad_pair = refs[count:]
    wide = 512

    def work():
        keys = pair[:, :HD]
        vals = pair[:, HD:]
        keys_sum = None
        for i in range(query.shape[0] // wide):
            cols = slice(wide * i, wide * (i + 1))
            for j in range(QD // HD):
                lanes = slice(HD * j, HD * (j + 1))
                q = query[cols, lanes]
                do = grad_out[cols, lanes]
                scores = mul(keys, q, NT)
                if diagonal:
                    scores = masked(scores, place, cols.start // TILE)
                probs = jnp.exp2(scores * exponent_scale - logs[j, :, cols])
                grad_probs = mul(vals, do, NT)
                grad_scores = low(probs * (grad_probs - terms[j, :, cols]))
                vals_add = mul(low(probs), do)
                keys_add = mul(grad_scores, q)
                add = mul(keys, grad_scores, TN)
                if not opening:
                    add = add + grad_in[j, :, cols]
                if diagonal:
                    grad_query[cols, lanes] = low((add * score_scale).T)
                else:
                    grad_query[j, :, cols] = add
                if keys_sum is None:
                    keys_sum, vals_sum = keys_add, vals_add
                else:
                    keys_sum, vals_sum = keys_sum + keys_add, vals_sum + vals_add
        grad_pair[:, :HD] = low(keys_sum * score_scale)
        grad_pair[:, HD:] = low(vals_sum)

    if diagonal:
        work()
    else:
        active = place[2] >= back
        pl.when(active)(work)

        @pl.when(jnp.logical_not(active))
        def _():
            grad_query[...] = jnp.zeros_like(grad_query) if opening else grad_in[...]
            grad_pair[...] = jnp.zeros_like(grad_pair)


def attend_back(place, query, grad_out, logs, terms, pair, grad_query, back, deps=()):
    diagonal = back == 0
    rows = query.shape[0]
    heads = QD // HD
    whole = lambda *shape: pl.BlockSpec(shape, lambda i, s: (0,) * len(shape))
    in_specs = [
        whole(rows, QD),
        whole(rows, QD),
        whole(heads, 1, rows),
        whole(heads, 1, rows),
        whole(rows, 2 * HD),
    ]
    args = [place, query, grad_out, logs, terms, pair]
    opening = grad_query is None
    if not opening:
        in_specs.append(whole(heads, HD, rows))
        args.append(grad_query)
    if diagonal:
        query_spec = whole(rows, QD)
        query_shape = jax.ShapeDtypeStruct((rows, QD), bf16)
    else:
        query_spec = whole(heads, HD, rows)
        query_shape = jax.ShapeDtypeStruct((heads, HD, rows), f32)
    return pl.pallas_call(
        functools.partial(attend_back_kernel, back, opening, len(deps)),
        grid_spec=pltpu.PrefetchScalarGridSpec(
            num_scalar_prefetch=1,
            grid=(1,),
            in_specs=in_specs + unread(deps),
            out_specs=[query_spec, whole(rows, 2 * HD)],
        ),
        out_shape=[
            query_shape,
            jax.ShapeDtypeStruct((rows, 2 * HD), bf16),
        ],
        compiler_params=params(VMEM),
        cost_estimate=taking(7),
        name="attend_back",
    )(*args, *deps)


def ring(i):
    j = (i + 1) % HEADS
    return j ^ (j // 2)


def load_piece(i, pieces, held, which=None):
    half = pieces[0].shape[-2]
    if which is not None:
        pieces = [p.at[which] for p in pieces]
    for at, k in enumerate((1, 3, 2, 0)):

        @pl.when(i == at)
        def _(k=k):
            held[:half, :] = pieces[2 * k][...]
            held[half:, :] = pieces[2 * k + 1][...]

    return held[...]


def piece_specs(pieces):
    return [fixed_block(*p.shape) for p in pieces]


def put_scatter(i, value, refs):
    send_one, send_two, keep_one, keep_two, own = refs
    half = keep_one.shape[0]
    top, bottom = low(value[:half]), low(value[half:])

    @pl.when(i == 0)
    def _():
        send_one[0] = top
        keep_two[...] = bottom

    @pl.when(i == 1)
    def _():
        send_one[0] = top
        send_two[0] = bottom

    @pl.when(i == 2)
    def _():
        keep_one[...] = top
        send_two[0] = bottom

    @pl.when(i == 3)
    def _():
        own[...] = value


def scatter_outs(half, columns):
    specs = [
        pl.BlockSpec((1, half, columns), lambda i: (jnp.minimum(i, 1), 0, 0)),
        pl.BlockSpec((1, half, columns), lambda i: (jnp.clip(i - 1, 0, 1), 0, 0)),
        pl.BlockSpec((half, columns), lambda i: (0, 0)),
        pl.BlockSpec((half, columns), lambda i: (0, 0)),
        pl.BlockSpec((2 * half, columns), lambda i: (0, 0)),
    ]
    shapes = [
        jax.ShapeDtypeStruct((2, half, columns), bf16),
        jax.ShapeDtypeStruct((2, half, columns), bf16),
        jax.ShapeDtypeStruct((half, columns), bf16),
        jax.ShapeDtypeStruct((half, columns), bf16),
        jax.ShapeDtypeStruct((2 * half, columns), f32),
    ]
    return specs, shapes


def scatter_parts(parts, marks=()):
    send_one, send_two, keep_one, keep_two, own = parts
    first = pin(to_head(send_one, 1), *marks)
    second = pin(to_head(send_two, 2), *marks)
    top = to_head(add_low(keep_one, first[1]), 2)
    bottom = to_head(add_low(keep_two, second[0]), 1)
    half = keep_one.shape[0]
    return jnp.concatenate(
        [
            own[:half] + first[0].astype(f32) + top.astype(f32),
            own[half:] + second[1].astype(f32) + bottom.astype(f32),
        ],
        axis=0,
    )


def by_ring(*block):
    return pl.BlockSpec(block, lambda i: (ring(i), 0))


def row_sums(x):
    ones = jnp.ones((8, x.shape[1]), bf16)
    high_part = low(x)
    low_part = low(x - high_part.astype(f32))
    return (mul(ones, high_part, NT) + mul(ones, low_part, NT))[0:1, :]


def column_of(row, width):
    column = jnp.broadcast_to(row, (128, row.shape[1])).T
    return jnp.concatenate([column] * (width // 128), axis=1)


def fixed_block(*shape):
    return pl.BlockSpec(shape, lambda i: (0,) * len(shape), pipeline_mode=pl.Buffered(1))


def tiled_call(kernel, steps, in_specs, out_specs, out_shape, scratch, micros, deps, name):
    count = len(deps)
    ins = len(in_specs)

    def run(*refs):
        kernel(*refs[:ins], *refs[ins + count :])

    return pl.pallas_call(
        run,
        grid=(steps,),
        in_specs=in_specs + unread(deps),
        out_specs=out_specs,
        out_shape=out_shape,
        scratch_shapes=scratch,
        compiler_params=params(32 if name == "feed_forward" else VMEM),
        cost_estimate=taking(micros),
        name=name,
    )


def weight_rows(normed, grads, seq_count, extra=(), deps=()):
    rows, features = normed.shape
    wide = features // HEADS
    shard = wide // seq_count
    columns = sum(g.shape[1] for g in grads) + 128 * len(extra)

    def kernel(*refs):
        normed, grads, out = refs[0], refs[1 : 1 + len(grads_in)], refs[-1]
        at = 0
        for e in refs[1 + len(grads_in) : -1]:
            filled = jnp.concatenate(
                [e[...], jnp.zeros((128 - e.shape[0], wide), f32)], axis=0
            ).T
            out[:, :, :, columns - 128 :] = low(filled.reshape(seq_count, 1, shard, 128))
        for g in grads:
            value = mul(normed[...], g[...], TN).reshape(seq_count, 1, shard, g.shape[1])
            out[:, :, :, at : at + g.shape[1]] = low(value)
            at += g.shape[1]

    grads_in = grads
    out = tiled_call(
        kernel,
        HEADS,
        [pl.BlockSpec((rows, wide), lambda i: (0, i))]
        + [fixed_block(*g.shape) for g in grads]
        + [pl.BlockSpec((e.shape[0], wide), lambda i: (0, i)) for e in extra],
        [pl.BlockSpec((seq_count, 1, shard, columns), lambda i: (0, i, 0, 0))],
        [jax.ShapeDtypeStruct((seq_count, HEADS, shard, columns), bf16)],
        [],
        columns / 300,
        deps,
        "weight_rows",
    )(normed, *grads, *extra, *deps)[0]
    return out.reshape(seq_count, HEADS * shard, columns)


def fetch_weights(source, held, sems, place):
    return [
        pltpu.make_async_copy(source.at[:, place[0] ^ j], held.at[j], sems.at[j])
        for j in range(HEADS)
    ]


def project_all(place, tokens, weights, spots, deps=()):
    half, features = tokens[0].shape[1:]
    rows = 2 * half * HEADS
    seq_count, _, shard, columns = weights.shape
    widths = (features, QUERY_AT, QD, CH, 2 * HD)
    count = len(deps)

    def kernel(place, *refs):
        tokens, spots, source = refs[:8], refs[8], refs[9]
        refs = refs[10 + count :]
        outs, (small, taps, gain_mix) = refs[:5], refs[5:8]
        held, scaled, *stored, sems, out_sems = refs[8:]
        copies = fetch_weights(source, held, sems, place)
        for copy in copies:
            copy.start()
        for t in range(2 * HEADS):
            x = tokens[t][0].astype(f32)
            scale = lax.rsqrt(jnp.mean(x * x, axis=1, keepdims=True) + norm_eps)
            scaled[half * t : half * (t + 1), :] = x * scale
        sources = iota((features, spots.shape[1]), 0)
        main = low(sources == spots[0:1, :])
        rest = low(sources == spots[1:2, :])
        for copy in copies:
            copy.wait()

        def take(start, stop):
            part = held[:, :, :, start:stop]
            if shard % 16 != 0:
                part = part.astype(f32)
            return low(part.reshape(features, stop - start))

        def send(i):
            return pltpu.make_async_copy(stored[i], outs[i], out_sems.at[i])

        turned = take(STEP_AT, STEP_AT + 128).astype(f32).T
        small_rows = turned[GAIN_LANE : GAIN_LANE + 16, :]
        small[...] = small_rows
        stored[0][...] = low(scaled[...] * small_rows[0:1, :])
        send(0).start()
        x = stored[0][...]
        stored[4][...] = low(mul(x, take(KEY_AT, KEY_AT + 2 * HD)))
        send(4).start()
        stored[1][:, :CH] = low(mul(x, take(0, CH)))
        stored[1][:, CH:] = low(mul(x, take(CH, QUERY_AT)))
        send(1).start()
        stored[2][...] = low(mul(x, take(QUERY_AT, GATE_AT)))
        send(2).start()
        stored[3][...] = low(mul(x, take(GATE_AT, KEY_AT)))
        send(3).start()
        small_low = low(small_rows)
        mains, rests = mul(small_low, main), mul(small_low, rest)
        gain_mix[...] = mains[2:3, CONV:] + rests[3:4, CONV:]
        taps[0:4, :] = mains[4:8, :CONV] + rests[8:12, :CONV]
        taps[4:8, :] = jnp.zeros((4, CONV), f32)
        for i in range(5):
            send(i).wait()

    ANY = pl.BlockSpec(memory_space=pl.ANY)
    token_block = pl.BlockSpec((1, half, features), lambda *i: (0, 0, 0))
    return pl.pallas_call(
        kernel,
        grid_spec=pltpu.PrefetchScalarGridSpec(
            num_scalar_prefetch=1,
            grid=(1,),
            in_specs=[token_block] * 8 + [whole_block(*spots.shape), ANY] + unread(deps),
            out_specs=[ANY] * 5
            + [whole_block(16, features), whole_block(8, CONV), whole_block(1, CH)],
            scratch_shapes=[
                pltpu.VMEM((HEADS, seq_count, shard, columns), bf16),
                pltpu.VMEM((rows, features), f32),
                *[pltpu.VMEM((rows, wide), bf16) for wide in widths],
                pltpu.SemaphoreType.DMA((HEADS,)),
                pltpu.SemaphoreType.DMA((5,)),
            ],
        ),
        out_shape=[like((rows, wide), bf16) for wide in widths]
        + [like((16, features), f32), like((8, CONV), f32), like((1, CH), f32)],
        compiler_params=params(60),
        cost_estimate=taking(8),
        name="project_all",
    )(place, *tokens, spots, weights, *deps)


def exact(values, picks):
    high_part = low(values)
    low_part = low(values - high_part.astype(f32))
    return mul(high_part, picks) + mul(low_part, picks)


def small_rows(place, grad_taps, sums, grad_skip, spots, shard, features, deps=()):
    spans = -(-MH // shard)
    total = 8 + 3 * spans
    rows = -(-total // 16) * 16

    def kernel(place, grad_taps, sums, grad_skip, spots, out):
        places = iota((CONV, features), 1)
        turned = spots[...].T
        for half in range(2):
            picks = low(places == turned[:CONV, half : half + 1])
            out[4 * half : 4 * half + 4, :] = exact(grad_taps[...], picks)[0:4, :]
        by_head = low(iota((CH, 128), 0) // MP == iota((CH, 128), 1))
        skips = exact(grad_skip[...], by_head)[0:1, :]
        values = jnp.concatenate([sums[0:2, :], skips, jnp.zeros((5, 128), f32)], axis=0)
        within = iota((128, features), 1) % shard - place[0] * MIX
        head = iota((128, features), 0)
        for j in range(spans):
            spread = exact(values, low((head == within + shard * j) & (head < MIX)))
            for i in range(3):
                at = 8 + i * spans + j
                out[at : at + 1, :] = spread[i : i + 1, :]
        out[total:, :] = jnp.zeros((rows - total, features), f32)

    return whole_call(
        kernel,
        place,
        [grad_taps, sums, grad_skip, spots],
        [like((rows, features), f32)],
        [],
        16,
        2,
        deps,
        "small_rows",
    )[0]


def pack_weights(place, inputs, state, step, query, gate, pairs, ff_gate, ff_up, gains, conv):
    shard = state.shape[0]
    conv_shard, mix_shard = conv.shape[1], gains[2].shape[1]
    ff = ff_gate.shape[1] // HEADS
    columns = CONV + 128 + QD + CH + 2 * HD + 2 * ff
    group = HEADS // KVH

    def kernel(place, inputs, state, step, query, gate, pairs, ff_gate, ff_up, *refs):
        gain_in, gain_two, gain_mix, conv = refs[:4]
        outs, (rows, steps) = refs[4 : 4 + HEADS], refs[4 + HEADS :]
        rows[...] = jnp.zeros_like(rows)
        steps[...] = jnp.zeros_like(steps)
        at = GAIN_LANE
        rows[at : at + 1, :shard] = gain_in[...].astype(f32)
        rows[at + 1 : at + 2, :shard] = gain_two[...].astype(f32)
        rows[at + 2 : at + 3, :shard] = gain_mix[:, :shard].astype(f32)
        rows[at + 3 : at + 4, : mix_shard - shard] = gain_mix[:, shard:].astype(f32)
        taps = conv[...].astype(f32)
        rows[at + 4 : at + 8, :shard] = taps[:, :shard]
        rows[at + 8 : at + 12, : conv_shard - shard] = taps[:, shard:]
        steps[:MH, :shard] = step[...].astype(f32)
        base = rows[...].T[:shard, :]
        every = low(steps[...].T[:shard, :])
        source, target = iota((128, 128), 0), iota((128, 128), 1)
        for m in range(HEADS):
            j = place[0] ^ m

            def cut(ref, wide, at=0, spot=j):
                return ref[:, pl.ds(pl.multiple_of(at + spot * wide, 128), wide)]

            moved = low((source == target + j * MIX) & (target < MIX))
            both = j // group
            blocks = [
                cut(inputs, CH), state[...], low(base + mul(every, moved)), cut(query, QD),
                cut(gate, CH), cut(pairs, HD, 0, both), cut(pairs, HD, KVH * HD, both),
                cut(ff_gate, ff), cut(ff_up, ff),
            ]
            at = 0
            for block in blocks:
                outs[m][:, at : at + block.shape[1]] = block
                at += block.shape[1]

    return whole_call(
        kernel,
        place,
        [inputs, state, step, query, gate, pairs, ff_gate, ff_up, *gains, conv],
        [like((shard, columns), bf16)] * HEADS,
        [pltpu.VMEM((128, 128), f32), pltpu.VMEM((128, 128), f32)],
        60,
        2,
        (),
        "pack_weights",
    )


def gate_of(z_tile):
    z = z_tile.astype(f32)
    return z, jax.nn.sigmoid(z)


def lanes_of(rows, p):
    left = iota((rows.shape[1], TILE), 1) < MP
    first, second = rows[2 * p : 2 * p + 1, :], rows[2 * p + 1 : 2 * p + 2, :]
    return jnp.where(left, column_of(first, TILE), column_of(second, TILE))


def mix_tokens(y0, cums, reads, packs, z, deps=()):
    rows = y0.shape[0]
    wide = rows // HEADS
    count = len(packs)

    def kernel(y0, cums, reads, z, *refs):
        packs, (mixed_out, squares, incoming) = refs[:count], refs[count:]
        sum_packs(packs, incoming)
        for t in range(HEADS):
            here = slice(wide * t, wide * (t + 1))
            met = mul(reads[here, :], low(incoming[...]), NT)
            growth = jnp.exp(cums[:, here])
            grown = jnp.concatenate([lanes_of(growth, p) for p in range(PAIRS)], axis=1)
            mixed = low(y0[here, :] + grown * met)
            mixed_out[here, :] = mixed
            gate, sig = gate_of(z[here, :])
            inner = mixed.astype(f32) * gate * sig
            squares[:, here] = row_sums(inner * inner)

    return whole_call(
        kernel,
        None,
        [y0, cums, reads, z, *packs],
        [like((rows, CH), bf16), like((1, rows), f32), like((CH, NS), f32)],
        [],
        20,
        3,
        deps,
        "mix_tokens",
    )


def branch_out(mixed, z, scale, gain, attended, weights, deps=()):
    rows, features = mixed.shape[0], weights.shape[1]
    wide = rows // HEADS
    specs, shapes = scatter_outs(wide // 2, features)

    def kernel(mixed, z, scale, gain, attended, weights, gated_out, *parts):
        gate, sig = gate_of(z[...])
        inner = mixed[...].astype(f32) * gate * sig
        gated = low(inner * column_of(scale[...], CH) * gain[...])
        gated_out[...] = gated
        value = mul(gated, weights[:CH, :]) + mul(attended[...], weights[CH:, :])
        put_scatter(pl.program_id(0), value, parts)

    outs = tiled_call(
        kernel,
        HEADS,
        [
            by_ring(wide, CH),
            by_ring(wide, CH),
            pl.BlockSpec((1, wide), lambda i: (0, ring(i))),
            pl.BlockSpec((1, CH), lambda i: (0, 0)),
            by_ring(wide, QD),
            fixed_block(CH + QD, features),
        ],
        [by_ring(wide, CH)] + specs,
        [jax.ShapeDtypeStruct((rows, CH), bf16)] + shapes,
        [],
        3,
        deps,
        "branch_out",
    )(mixed, z, scale, gain, attended, weights, *deps)
    return outs[0], outs[1:]


def feed_forward(tokens, grads, weights, weights_down, deps=()):
    wide, features = 2 * tokens[0].shape[0], tokens[0].shape[1]
    rows = wide * HEADS
    ff = weights_down.shape[0]
    specs, shapes = scatter_outs(wide // 2, features)

    def kernel(*refs):
        tokens, grads = refs[:8], refs[8:16]
        weights, weights_down, tokens_out, grads_out, acted_out, inner_out = refs[16:22]
        parts, held, held_grads = refs[22:27], refs[27], refs[28]
        i = pl.program_id(0)
        x = load_piece(i, tokens, held)
        g = load_piece(i, grads, held_grads, 1)
        tokens_out[...] = x
        grads_out[...] = g
        inner = mul(x, weights[...])
        grad_acted = mul(g, weights_down[...], NT)
        gate, up = inner[:, :ff], inner[:, ff:]
        sig = jax.nn.sigmoid(gate)
        silu = gate * sig
        acted_out[...] = low(silu * up)
        grad_gate = low(grad_acted * up * (sig * (1.0 + gate * (1.0 - sig))))
        grad_inner = jnp.concatenate([grad_gate, low(grad_acted * silu)], axis=1)
        inner_out[...] = grad_inner
        put_scatter(i, mul(grad_inner, weights[...], NT), parts)

    outs = tiled_call(
        kernel,
        HEADS,
        piece_specs(tokens)
        + piece_specs(grads)
        + [
            fixed_block(features, 2 * ff),
            fixed_block(ff, features),
        ],
        [by_ring(wide, features), by_ring(wide, features), by_ring(wide, ff), by_ring(wide, 2 * ff)]
        + specs,
        [
            jax.ShapeDtypeStruct((rows, features), bf16),
            jax.ShapeDtypeStruct((rows, features), bf16),
            jax.ShapeDtypeStruct((rows, ff), bf16),
            jax.ShapeDtypeStruct((rows, 2 * ff), bf16),
        ]
        + shapes,
        [pltpu.VMEM((wide, features), bf16), pltpu.VMEM((wide, features), bf16)],
        7,
        deps,
        "feed_forward",
    )(*tokens, *grads, weights, weights_down, *deps)
    return outs[0], outs[1], outs[2], outs[3], outs[4:]


def scattered_product(left, weights, deps=()):
    rows, depth = left.shape
    features = weights.shape[1]
    wide = rows // HEADS
    specs, shapes = scatter_outs(wide // 2, features)

    def kernel(left, weights, *parts):
        put_scatter(pl.program_id(0), mul(left[...], weights[...]), parts)

    return tiled_call(
        kernel,
        HEADS,
        [by_ring(wide, depth), fixed_block(depth, features)],
        specs,
        shapes,
        [],
        2,
        deps,
        "scattered_product",
    )(left, weights, *deps)


def branch_back(grads, weights, attended, mixed, z, scale, gain, deps=()):
    wide, features = 2 * grads[0].shape[0], grads[0].shape[1]
    rows = wide * HEADS
    heads = QD // HD

    def kernel(*refs):
        grads = refs[:8]
        weights, attended, mixed, z, scale, gain = refs[8:14]
        grads_out, grad_att, terms, grad_gated, sums, held = refs[14:]
        i = pl.program_id(0)
        g = load_piece(i, grads, held)
        grads_out[...] = g
        both = mul(g, weights[...], NT)
        att = low(both[:, CH:])
        grad_att[...] = att
        product = att.astype(f32) * attended[...].astype(f32)
        for j in range(heads):
            terms[j] = row_sums(product[:, HD * j : HD * (j + 1)])
        gate, sig = gate_of(z[...])
        unit = mixed[...].astype(f32) * gate * sig * column_of(scale[...], CH)
        gated = both[:, :CH]
        grad_gated[...] = low(gated)
        scaled = gated * unit
        sums[...] = row_sums(scaled * gain[...])

    return tiled_call(
        kernel,
        HEADS,
        piece_specs(grads)
        + [
            fixed_block(CH + QD, features),
            by_ring(wide, QD),
            by_ring(wide, CH),
            by_ring(wide, CH),
            pl.BlockSpec((1, wide), lambda i: (0, ring(i))),
            pl.BlockSpec((1, CH), lambda i: (0, 0)),
        ],
        [
            by_ring(wide, features),
            by_ring(wide, QD),
            pl.BlockSpec((heads, 1, wide), lambda i: (0, 0, ring(i))),
            by_ring(wide, CH),
            pl.BlockSpec((1, wide), lambda i: (0, ring(i))),
        ],
        [
            jax.ShapeDtypeStruct((rows, features), bf16),
            jax.ShapeDtypeStruct((rows, QD), bf16),
            jax.ShapeDtypeStruct((heads, 1, rows), f32),
            jax.ShapeDtypeStruct((rows, CH), bf16),
            jax.ShapeDtypeStruct((1, rows), f32),
        ],
        [pltpu.VMEM((wide, features), bf16)],
        4,
        deps,
        "branch_back",
    )(*grads, weights, attended, mixed, z, scale, gain, *deps)


def gate_back(grad_gated, mixed, z, scale, mean, gain, cums, reads, packed, deps=()):
    rows = mixed.shape[0]
    wide = rows // HEADS

    def kernel(
        grad_gated, mixed, z, scale, mean, gain, cums, reads, packed, grad_mixed, grad_z, leaving
    ):
        total = None
        for t in range(HEADS):
            here = slice(wide * t, wide * (t + 1))
            gate, sig = gate_of(z[here, :])
            silu = gate * sig
            value = mixed[here, :].astype(f32)
            factor = column_of(scale[:, here], CH)
            unit = value * silu * factor
            inner = grad_gated[here, :].astype(f32) * gain[...]
            inner = (inner - unit * column_of(mean[:, here], CH)) * factor
            out = low(inner * silu)
            grad_mixed[here, :] = out
            grad_z[here, :] = low(inner * value * (sig * (1.0 + gate * (1.0 - sig))))
            growth = jnp.exp(cums[:, here])
            grown = jnp.concatenate([lanes_of(growth, p) for p in range(PAIRS)], axis=1)
            part = mul(low(out.astype(f32) * grown), reads[here, :], TN)
            total = part if total is None else total + part
        leaving[:CH, :] = low(total)
        leaving[CH:, :] = packed[CH:, :]

    return whole_call(
        kernel,
        None,
        [grad_gated, mixed, z, scale, mean, gain, cums, reads, packed],
        [like((rows, CH), bf16), like((rows, CH), bf16), like((CH + 16, NS), bf16)],
        [],
        20,
        3,
        deps,
        "gate_back",
    )


def normed_back(place, grad_pre, grad_z, grad_query, grad_pair, weights, deps=()):
    rows = grad_pre.shape[0]
    wide = rows // HEADS
    half = wide // 2
    seq_count, _, shard, columns = weights.shape
    features = HEADS * seq_count * shard
    ANY = pl.BlockSpec(memory_space=pl.ANY)

    def kernel(place, grad_pre, grad_query, grad_z, grad_pair, source, *refs):
        send_one, send_two, keep_one, keep_two, own, held, sems = refs
        copies = fetch_weights(source, held, sems, place)
        for copy in copies:
            copy.start()
        for copy in copies:
            copy.wait()
        for k in (1, 3, 2, 0):
            here = slice(wide * k, wide * (k + 1))
            grads = jnp.concatenate(
                [grad_pre[here, :], grad_query[here, :], grad_z[here, :], grad_pair[here, :]],
                axis=1,
            )
            parts = []
            for j in range(HEADS):
                part = held[j]
                if shard % 16 != 0:
                    part = part.astype(f32)
                parts.append(mul(grads, low(part.reshape(seq_count * shard, columns)), NT))
            value = jnp.concatenate(parts, axis=1)
            top, bottom = low(value[:half]), low(value[half:])
            if k == 1:
                send_one[0] = top
                keep_two[...] = bottom
            elif k == 3:
                send_one[1] = top
                send_two[0] = bottom
            elif k == 2:
                keep_one[...] = top
                send_two[1] = bottom
            else:
                own[...] = value

    shapes = scatter_outs(half, features)[1]
    return whole_call(
        kernel,
        place,
        [grad_pre, grad_query, grad_z, grad_pair, (weights, ANY)],
        shapes,
        [
            pltpu.VMEM((HEADS, seq_count, shard, columns), bf16),
            pltpu.SemaphoreType.DMA((HEADS,)),
        ],
        40,
        6,
        deps,
        "normed_back",
    )


def to_head(x, mask):
    return lax.ppermute(x, "head", [(i, i ^ mask) for i in range(HEADS)])


def to_seq(x, mask):
    return lax.ppermute(x, "seq", [(i, i ^ mask) for i in range(lax.axis_size("seq"))])


def shifted(x, blocks):
    count = lax.axis_size("seq")
    route = [(i, i + 2 * blocks) for i in range(count) if 0 <= i + 2 * blocks < count]
    return lax.ppermute(x, "seq", route)


def gather_head(top, bottom):
    one_top = to_head(top, 1)
    two_bottom = to_head(bottom, 2)
    one_bottom = to_head(bottom, 1)
    two_top = to_head(top, 2)
    three_top = to_head(one_top, 2)
    three_bottom = to_head(two_bottom, 1)
    return top, bottom, one_top, one_bottom, two_top, two_bottom, three_top, three_bottom


def gather_rows_low(x):
    half = x.shape[0] // 2
    return gather_head(low(x[:half]), low(x[half:]))


def pin(x, *deps):
    if len(deps) == 0:
        return x
    return lax.optimization_barrier((x,) + deps)[0]


def add_low(*terms):
    return low(sum((t.astype(f32) for t in terms[1:]), terms[0].astype(f32)))


def sum_head(row):
    wide = row.shape[1] // HEADS
    total = row
    for mask in range(1, HEADS):
        got = to_head(row, mask)
        total = total + jnp.concatenate(
            [got[:, wide * (k ^ mask) : wide * ((k ^ mask) + 1)] for k in range(HEADS)], axis=1
        )
    return total


def send_packs(packed, blocks, direction):
    return [shifted(packed, direction * k) for k in range(1, blocks)]


def gather_rows(shard):
    return lax.all_gather(shard, "seq", axis=0, tiled=False)


def scatter_rows(x):
    return lax.psum_scatter(x, "seq", scatter_dimension=0, tiled=False)


def in_order(pieces, index):
    bit = 1
    while bit < len(pieces):
        upper = (index & bit) != 0
        pieces = [jnp.where(upper, pieces[j ^ bit], pieces[j]) for j in range(len(pieces))]
        bit *= 2
    return pieces


def ordered_rows(x, head_index):
    parts = [
        lax.dynamic_index_in_dim(x, head_index ^ j, 1, keepdims=False) for j in range(HEADS)
    ]
    return jnp.stack(parts).reshape(-1, x.shape[-1])


def scatter_direct(x, core, block):
    blocks = x.shape[0] // 2
    x = x.reshape((blocks, 2) + x.shape[1:])
    pick = lambda c: lax.dynamic_index_in_dim(x, c, 1, keepdims=False)
    x = add_low(pick(core), to_seq(pick(1 - core), 1))
    parts = [lax.dynamic_index_in_dim(x, block, 0, keepdims=False)]
    for k in range(1, blocks):
        part = lax.dynamic_index_in_dim(x, block ^ k, 0, keepdims=False)
        parts.append(to_seq(part, 2 * k))
    return parts


LATE = QD + 2 * HD
EARLY_AT = LATE + 128
FF_AT = EARLY_AT + CH + QUERY_AT


def merge_columns(place, late, early, ff):
    shard, ff_wide = ff.shape[1:]
    columns = FF_AT + ff_wide
    count = len(late)

    def kernel(place, *refs):
        late, early, ff, outs = refs[:count], refs[count], refs[count + 1], refs[count + 2 :]
        for m in range(HEADS):
            j = place[0] ^ m
            out = outs[m]
            blocks = [part[j].astype(f32) for part in late]
            out[:, :LATE] = low(sum(part[:, :LATE] for part in blocks))
            small = in_order([part[:, LATE:] for part in blocks], place[2])
            out[:, LATE:EARLY_AT] = low(sum(small))
            out[:, EARLY_AT:FF_AT] = early[j]
            out[:, FF_AT:] = ff[j]

    return whole_call(
        kernel,
        place,
        [*late, early, ff],
        [like((shard, columns), bf16)] * HEADS,
        [],
        16,
        2,
        (),
        "merge_columns",
    )


def finish_columns(place, pieces, weights, gains, conv_shard):
    shard = pieces[0].shape[0]
    ff = weights[6].shape[1] // HEADS
    spans = -(-MH // shard)
    at_state = EARLY_AT + CH
    at_step = EARLY_AT + STEP_AT
    at_gate = EARLY_AT + QUERY_AT

    def fold(weight, grad):
        product = weight.astype(f32) * grad
        tiles = [product[:, 128 * i : 128 * (i + 1)] for i in range(product.shape[1] // 128)]
        return sum(tiles[1:], tiles[0])

    def kernel(place, *refs):
        pieces = refs[:HEADS]
        inputs_w, state_w, step_w, query_w, gate_w, pair_w, ff_w, up_w = refs[4:12]
        gain_in, gain_two = refs[12:14]
        inputs, states, steps, query, gate, pair, ff_gate, ff_up = refs[14:22]
        grad_in, grad_two, taps, *heads = refs[22:]
        owners = [place[0] ^ m for m in range(HEADS)]

        def spread(out, weight, start, wide):
            total = jnp.zeros((shard, 128), f32)
            for m in range(HEADS):
                here = pl.ds(pl.multiple_of(owners[m] * wide, 128), wide)
                grad = pieces[m][:, start : start + wide].astype(f32)
                out[:, here] = grad
                total = total + fold(weight[:, here], grad)
            return total

        first = spread(inputs, inputs_w, EARLY_AT, CH) + spread(query, query_w, 0, QD)
        first = first + spread(gate, gate_w, at_gate, CH)
        second = spread(ff_gate, ff_w, FF_AT, ff) + spread(ff_up, up_w, FF_AT + ff, ff)
        grad = sum(p[:, at_state : at_state + 2 * NS].astype(f32) for p in pieces)
        states[...] = grad
        first = first + fold(state_w[...], grad)
        for i in range(KVH):
            for kind in range(2):
                start = QD + HD * kind
                grad = jnp.zeros((shard, HD), f32)
                for m in range(HEADS):
                    mine = (owners[m] // (HEADS // KVH)) == i
                    part = pieces[m][:, start : start + HD].astype(f32)
                    grad = grad + jnp.where(mine, part, 0.0)
                lanes = slice(HD * (KVH * kind + i), HD * (KVH * kind + i + 1))
                pair[:, lanes] = grad
                first = first + fold(pair_w[:, lanes], grad)
        grad = jnp.zeros((shard, 128), f32)
        source, target = iota((128, 128), 0), iota((128, 128), 1)
        for m in range(HEADS):
            moved = low((target == source + owners[m] * MIX) & (source < MIX))
            grad = grad + mul(pieces[m][:, at_step : at_step + 128], moved)

        def turned(x):
            return jnp.concatenate([x, jnp.zeros((128 - shard, 128), f32)], axis=0).T

        grad = turned(grad)[:MH, :shard]
        steps[...] = grad
        step_sum = jnp.sum(step_w[...].astype(f32) * grad, axis=0, keepdims=True)

        def row(total):
            column = jnp.sum(total, axis=1, keepdims=True)
            return turned(jnp.broadcast_to(column, (shard, 128)))[0:1, :shard]

        grad_in[...] = (row(first) + step_sum) / gain_in[...].astype(f32)
        grad_two[...] = row(second) / gain_two[...].astype(f32)
        small = in_order([p[:, LATE:EARLY_AT].astype(f32) for p in pieces], place[0])
        small = sum(small[1:], small[0])
        rows = turned(small)
        taps[:, 0:shard] = rows[0:4, :shard]
        taps[:, shard:conv_shard] = rows[4:8, : conv_shard - shard]
        for i in range(3):
            for j in range(spans):
                wide = min(shard, MH - j * shard)
                at = 8 + i * spans + j
                heads[i][:, j * shard : j * shard + wide] = rows[at : at + 1, :wide]

    return whole_call(
        kernel,
        place,
        [*pieces, *weights, *gains],
        [like(w.shape, f32) for w in weights]
        + [like((1, shard), f32)] * 2
        + [like((4, conv_shard), f32)]
        + [like((1, MH), f32)] * 3,
        [],
        24,
        4,
        (),
        "finish_columns",
    )


def split_columns(x):
    return x.reshape(x.shape[0], HEADS, -1).swapaxes(0, 1)


def body(
    hidden_in,
    lengths,
    cotangent,
    input_gain,
    mixer_gate,
    mixer_inputs,
    state_weights,
    conv_weight,
    step_weight,
    decay_log,
    step_bias,
    skip_gain,
    query_weight,
    key_value_weight,
    mixer_gain,
    mixer_output,
    attention_out,
    second_gain,
    gate_weight,
    up_weight,
    down_weight,
):
    seq_count = lax.axis_size("seq")
    head_index = lax.axis_index("head")
    seq_index = lax.axis_index("seq")
    block = seq_index // 2
    core = seq_index % 2
    blocks = seq_count // 2
    own_rows, features = hidden_in.shape[2], hidden_in.shape[3]
    rows = 2 * own_rows * HEADS
    shard = input_gain.shape[0]
    ff = gate_weight.shape[1] // HEADS
    mix_shard, down_shard = mixer_output.shape[0], down_weight.shape[0]
    conv_shard = conv_weight.shape[0]
    device = head_index * seq_count + seq_index

    end_row = ((head_index ^ (HEADS - 1)) * 2 + (1 ^ core)) * TILE + TILE - 16
    place = jnp.stack([head_index, core, block, end_row // 16]).astype(jnp.int32)
    packs = pack_weights(
        place, mixer_inputs, state_weights, step_weight.T, query_weight, mixer_gate,
        key_value_weight, gate_weight, up_weight,
        [input_gain[None], second_gain[None], mixer_gain[None]], conv_weight.T,
    )
    wide = packs[0].shape[1] - 2 * ff
    pieces = [packs[0]] + [to_head(packs[m], m) for m in range(1, HEADS)]

    both = jnp.stack([hidden_in[:, 0], cotangent[:, 0]], axis=1)
    keep = lax.dynamic_index_in_dim(both, core, 0, keepdims=False)
    give = lax.dynamic_index_in_dim(both, 1 - core, 0, keepdims=False)
    got = to_seq(give, 1)
    hidden = jnp.concatenate([keep[0], got[0]], axis=0).astype(f32)
    cot = jnp.concatenate([keep[1], got[1]], axis=0)
    first_own = pin(pieces[0], got)
    weights_in = gather_rows(
        jnp.stack([first_own[:, :wide]] + [p[:, :wide] for p in pieces[1:]])
    )
    tokens = 2 * own_rows
    block_rows = own_rows * HEADS
    spot = jnp.arange(tokens)
    positions = (
        (2 * block + ((spot // own_rows) ^ core)) * block_rows
        + head_index * own_rows
        + spot % own_rows
    )
    length = lax.dynamic_index_in_dim(lengths, core, 0, keepdims=False)
    valid = (positions < length).astype(f32)[:, None]
    grad_result_own = cot.astype(f32) * valid
    grad_low = low(grad_result_own)
    both_all = gather_head(
        jnp.stack([keep[0], grad_low[:own_rows]]), jnp.stack([got[0], grad_low[own_rows:]])
    )

    out_pack = jnp.concatenate([mixer_output, attention_out], axis=0)
    out_all = gather_rows(pin(out_pack, *pieces))
    ff_pack = jnp.concatenate([p[:, wide:] for p in pieces] + [down_weight], axis=0)

    def sources(channels, size):
        owner, offset = channels // size, channels % size
        main = jnp.where(offset < shard, owner * shard + offset, -1)
        return jnp.stack([main, jnp.where(offset < shard, -1, owner * shard + offset - shard)])

    spread = jnp.arange(CONV)
    spread = jnp.where(spread < CH, spread + head_index * CH, spread + (MH * MP - CH))
    spots = jnp.concatenate(
        [sources(spread, conv_shard), sources(jnp.arange(CH) + head_index * CH, mix_shard)], axis=1
    )
    spots = jnp.pad(spots, ((0, 6), (0, 0))).astype(jnp.int32)
    (normed, mix_in, query, z, own_pair, small, taps, gain_mix) = project_all(
        place, both_all, weights_in, spots, deps=(ff_pack, out_pack)
    )
    tail = shifted(lax.dynamic_slice(mix_in, (end_row, 0), (16, CONV)), 1)
    gain_in, gain_two = small[0:1], small[1:2]
    scale_in = lax.rsqrt(jnp.mean(hidden * hidden, axis=-1, keepdims=True) + norm_eps)
    unit_in = hidden * scale_in

    pair = [own_pair, shifted(pin(own_pair, tail), 1)]

    decay_part = lax.dynamic_slice_in_dim(-jnp.exp(decay_log), head_index * MIX, MIX)
    bias_part = lax.dynamic_slice_in_dim(step_bias, head_index * MIX, MIX)
    skip_part = lax.dynamic_slice_in_dim(skip_gain, head_index * MIX, MIX)
    heads = jnp.pad(jnp.stack([decay_part, bias_part]), ((0, 6), (0, 128 - MIX)))
    skip = jnp.broadcast_to(jnp.repeat(skip_part, MP)[None], (8, CH))
    y0, reads, cums, starts, runs, packed = mixer_forward(
        place, mix_in, tail, taps, heads, skip
    )
    packs = send_packs(packed, blocks, 1)
    running = attend(place, query, pair[0], 0, None, blocks == 1, deps=(packed,))
    pair.append(shifted(pin(pair[1], running[1], *packs), 1))
    out_all = pin(out_all, packed)
    weights_out = jnp.concatenate(
        [
            out_all[:, :mix_shard].reshape(CH, features),
            out_all[:, mix_shard:].reshape(QD, features),
        ],
        axis=0,
    )
    for k in range(1, blocks):
        running = attend(
            place, query, pair[k], k, running, k == blocks - 1,
            deps=(packed,) if k == 1 else (scale_mix,),
        )
        if k == 1:
            mixed, squares, incoming = mix_tokens(
                y0, cums, reads, packs, z, deps=(running[1], weights_out)
            )
            for j in range(3, blocks):
                pair.append(shifted(pin(pair[-1], squares), 1))
            scale_mix = lax.rsqrt(sum_head(squares) / (MH * MP) + norm_eps)
        if k == blocks - 2:
            ff_all = gather_rows(pin(ff_pack, running[1], pair[-1]))
    attended, logs = running
    ff_all = pin(ff_all, attended)
    weights_ff = ordered_rows(
        ff_all[:, : HEADS * shard].reshape(seq_count, HEADS, shard, 2 * ff), head_index
    )
    weights_down = ff_all[:, HEADS * shard :].reshape(ff, features)
    gated, parts = branch_out(mixed, z, scale_mix, gain_mix, attended, weights_out)
    resid = hidden + scatter_parts(parts)

    scale_two = lax.rsqrt(jnp.mean(resid * resid, axis=-1, keepdims=True) + norm_eps)
    norm_two = resid * scale_two
    normed_two, grad_result, acted, grad_inner, parts = feed_forward(
        gather_rows_low(norm_two * gain_two), both_all, weights_ff, weights_down
    )
    grad_down = low(mul(acted, grad_result, TN)).reshape(seq_count, down_shard, features)
    ff_rows = jnp.concatenate(
        [weight_rows(normed_two, [grad_inner], seq_count), grad_down], axis=1
    )
    ff_sum = scatter_rows(ff_rows)

    down_parts = scattered_product(acted, weights_down)
    grad_two = scatter_parts(parts, (ff_rows, grad_down, down_parts[0]))
    grad_two = grad_two * gain_two
    grad_resid = grad_result_own + scale_two * (
        grad_two - norm_two * jnp.mean(grad_two * norm_two, axis=-1, keepdims=True)
    )

    grad_branch, grad_attended, terms, grad_gated, sums_mix = branch_back(
        gather_rows_low(grad_resid), weights_out, attended, mixed, z, scale_mix, gain_mix,
    )
    mean_mix = sum_head(sums_mix) / (MH * MP)
    down_parts = [pin(p, terms) for p in down_parts]

    out_rows = jnp.concatenate(
        [
            low(mul(gated, grad_branch, TN)).reshape(seq_count, mix_shard, features),
            low(mul(attended, grad_branch, TN)).reshape(seq_count, shard, features),
        ],
        axis=1,
    )
    out_sum = scatter_rows(out_rows)

    def back_step(k, grad_query, deps):
        return attend_back(
            place, query, grad_attended, logs, terms, pair[k], grad_query, k, deps=deps
        )

    grad_query, kept = back_step(blocks - 1, None, ())
    chain = shifted(kept, -1)
    grad_mixed, grad_z, leaving = gate_back(
        grad_gated, mixed, z, scale_mix, mean_mix, gain_mix, cums, reads, packed,
        deps=(grad_query,),
    )
    back_packs = send_packs(leaving, blocks, -1)
    for k in range(blocks - 2, 1, -1):
        grad_query, kept = back_step(k, grad_query, (leaving, out_rows))
        if k > 2:
            chain = shifted(add_low(kept, chain), -1)
    grad_pre, first, grad_taps, sums, grad_skip = mixer_backward(
        place, mix_in, tail, taps, heads, skip, starts, runs, incoming, grad_mixed, back_packs,
        deps=(grad_query, chain),
    )
    from_next = shifted(first, -1)
    chain = shifted(add_low(kept, pin(chain, from_next)), -1)
    grad_query, kept = back_step(1, grad_query, (sums,))
    grad_pre = fix_ends(place, grad_pre, from_next, taps)
    early_rows = weight_rows(normed, [grad_pre, grad_z], seq_count, deps=(grad_query,))
    early_sum = scatter_rows(early_rows)
    chain = shifted(add_low(kept, pin(chain, early_rows)), -1)
    grad_query, kept = back_step(0, grad_query, (early_rows,))
    chain = add_low(kept, chain)

    small_part = small_rows(
        place, grad_taps, sums, grad_skip, spots, shard, features, deps=(early_rows,)
    )
    late_rows = weight_rows(normed, [grad_query, chain], seq_count, extra=(small_part,))
    late_parts = scatter_direct(
        late_rows.reshape(seq_count, HEADS, shard, late_rows.shape[2]), core, block
    )
    parts = normed_back(
        place, grad_pre, grad_z, grad_query, chain, weights_in, deps=(late_rows,)
    )
    grad_normed = scatter_parts(parts) * gain_in
    result = (resid + scatter_parts(down_parts, (parts[0],))) * valid
    merged = merge_columns(
        place,
        late_parts,
        early_sum.reshape(HEADS, shard, -1),
        ff_sum.reshape(-1, shard, features),
    )
    pieces = [merged[0]] + [to_head(merged[m], m) for m in range(1, HEADS)]
    (
        grad_inputs, states, grad_steps, grad_queries, grad_gate, key_values, grad_ff_gate,
        grad_ff_up, grad_gain_in, grad_gain_two, grad_conv, *head_sums,
    ) = finish_columns(
        place, pieces,
        [
            mixer_inputs, state_weights, step_weight.T, query_weight, mixer_gate,
            key_value_weight, gate_weight, up_weight,
        ],
        [input_gain[None], second_gain[None]], conv_shard,
    )
    grad_hidden = grad_resid + scale_in * (
        grad_normed - unit_in * jnp.mean(grad_normed * unit_in, axis=-1, keepdims=True)
    )

    def back(x):
        x = x.reshape(2, own_rows, features)
        arrived = to_seq(x[1], 1)
        return jnp.stack(
            [jnp.where(core == 0, x[0], arrived), jnp.where(core == 0, arrived, x[0])]
        )[:, None]

    grad_mixer_output = out_sum[:mix_shard].astype(f32)

    grad_gain_mix = jnp.sum(mixer_output.astype(f32) * grad_mixer_output, axis=1)
    return (
        back(result),
        back(grad_hidden),
        grad_gain_in[0],
        grad_gate,
        grad_inputs,
        states,
        grad_conv.T,
        grad_steps.T,
        head_sums[0][0],
        head_sums[1][0],
        head_sums[2][0],
        grad_queries,
        key_values,
        grad_gain_mix / mixer_gain.astype(f32),
        grad_mixer_output,
        out_sum[mix_shard:].astype(f32),
        grad_gain_two[0],
        grad_ff_gate,
        grad_ff_up,
        ff_sum[HEADS * shard :].astype(f32),
    )


def solution(mesh):
    tokens = P(None, "seq", "head", None)
    split = P(("head", "seq"), None)
    line = P(("head", "seq"))
    whole = P()
    in_specs = (
        tokens, whole, tokens, line, split, split, split, split, split, whole, whole, whole,
        split, split, line, split, split, line, split, split, split,
    )
    out_specs = (
        tokens, tokens, line, split, split, split, split, split, whole, whole, whole, split,
        split, line, split, split, line, split, split, split,
    )
    return jax.shard_map(body, mesh=mesh, in_specs=in_specs, out_specs=out_specs, check_vma=False)
```

```python
import functools

import jax
import jax.numpy as jnp
from jax import lax
from jax.experimental import pallas as pl
from jax.experimental.pallas import tpu as pltpu
from jax.sharding import PartitionSpec as P

QH = 8
KVH = 2
HD = 128
MH = 24
MP = 64
NS = 128
HEADS = 4
MIX = MH // HEADS
CH = MIX * MP
QD = QH // HEADS * HD
CONV = CH + 2 * NS
STEP_AT = CONV
QUERY_AT = STEP_AT + 128
GATE_AT = QUERY_AT + QD
KEY_AT = GATE_AT + CH
TILE = 128
GAIN_LANE = 8
PAIRS = MIX // 2

norm_eps = 1e-05
score_scale = HD ** (-0.5)
exponent_scale = score_scale * 1.4426950408889634
highest = lax.Precision.HIGHEST
f32 = jnp.float32
bf16 = jnp.bfloat16
NN = ((1,), (0,))
NT = ((1,), (1,))
TN = ((0,), (0,))
BIG = 1e30
VMEM = 24


def low(x):
    return x.astype(bf16)


def mul(left, right, sides=NN, precision=None):
    return lax.dot_general(
        left, right, (sides, ((), ())), preferred_element_type=f32, precision=precision
    )


def params(megabytes, **more):
    return pltpu.CompilerParams(vmem_limit_bytes=megabytes * 1024 * 1024, **more)


def taking(micros):
    micros = micros * 0.25
    return pl.CostEstimate(
        flops=int(micros * 1.1e9), bytes_accessed=int(micros * 3.6e6), transcendentals=0
    )


def unread(deps):
    return [pl.BlockSpec(memory_space=pl.ANY)] * len(deps)


def iota(shape, dim):
    return lax.broadcasted_iota(jnp.int32, shape, dim)


def tile_of(g, place):
    blocks = TILE * HEADS // TILE
    return ((g % blocks) ^ place[0]) * 2 + ((g // blocks) ^ place[1])


def conv_sums(ext, taps):
    total = ext[5:133, :] * taps[0:1, :]
    for k in range(1, 4):
        total = total + ext[5 + k : 133 + k, :] * taps[k : k + 1, :]
    return total


def mul_exact(picks, values):
    high_part = low(values)
    low_part = low(values - high_part.astype(f32))
    return mul(picks, high_part) + mul(picks, low_part)


def step_sizes(raw, heads):
    rows = iota((TILE, TILE), 0)
    cols = iota((TILE, TILE), 1)
    lower = rows >= cols
    moved = raw + heads[1:2, :]
    delta = jnp.maximum(moved, 0.0) + jnp.log1p(jnp.exp(-jnp.abs(moved)))
    cum = mul_exact(low(lower), heads[0:1, :] * delta)
    return moved, delta, cum, lower


def head_terms(delta, cum, lower, left):
    cum_rows = cum.T
    decays, both, sizes = [], [], []
    for p in range(PAIRS):
        columns = []
        for h in (2 * p, 2 * p + 1):
            column = jnp.broadcast_to(cum[:, h : h + 1], (TILE, TILE))
            decays.append(jnp.exp(jnp.where(lower, column - cum_rows[h : h + 1, :], -BIG)))
            columns.append(column)
        both.append(jnp.where(left, columns[0], columns[1]))
        sizes.append(jnp.where(left, delta[:, 2 * p : 2 * p + 1], delta[:, 2 * p + 1 : 2 * p + 2]))
    return decays, jnp.concatenate(both, axis=1), jnp.concatenate(sizes, axis=1)


def head_rows(values, top):
    return jnp.concatenate([row_pair(values, p, top) for p in range(PAIRS)], axis=0)


def row_pair(values, p, top):
    return jnp.where(top, values[:, 2 * p : 2 * p + 1], values[:, 2 * p + 1 : 2 * p + 2])


def halves(x, left):
    none = jnp.zeros_like(x)
    return jnp.concatenate([jnp.where(left, x, none), jnp.where(left, none, x)], axis=0)


def tile_rows(g, place):
    return pl.ds(pl.multiple_of(tile_of(g, place) * TILE, TILE), TILE)


def pack_rows(state, total):
    high_part = low(total).astype(f32)
    rows = jnp.concatenate([high_part, total - high_part, jnp.zeros((14, 128), f32)], axis=0)
    return jnp.concatenate([low(state), low(rows)], axis=0)


def sum_packs(packs, out):
    top = iota((TILE, NS), 0) < MP
    out[...] = jnp.zeros_like(out)
    passed = jnp.zeros((1, 128), f32)
    for pack in packs:
        factor = jnp.exp(passed)
        for p in range(PAIRS):
            lanes = slice(TILE * p, TILE * (p + 1))
            out[lanes, :] = out[lanes, :] + row_pair(factor, p, top) * pack[lanes, :].astype(f32)
        ends = pack[CH : CH + 16, :].astype(f32)
        passed = passed + ends[0:1, :] + ends[1:2, :]


def mixer_forward_kernel(
    place, rest, tail, taps, heads, skip, y0, reads_out, cums, starts, runs, packed,
    ext, state, run,
):
    state[...] = jnp.zeros_like(state)
    run[...] = jnp.zeros_like(run)
    ext[0:8, :] = tail[...].astype(f32)[8:16, :]

    def one_tile(g, unused):
        here = tile_rows(g, place)
        pre = rest[here, :CONV].astype(f32)
        ext[8:136, :] = pre
        total = conv_sums(ext, taps)
        act = total * jax.nn.sigmoid(total)
        ext[0:8, :] = pre[120:128, :]
        writes = low(act[:, CH : CH + NS])
        reads = low(act[:, CH + NS :])
        reads_out[here, :] = reads
        starts[g] = low(state[...])
        runs[g] = run[...]
        _, delta, cum, lower = step_sizes(rest[here, STEP_AT:].astype(f32), heads)
        left = iota((TILE, TILE), 1) < MP
        top = iota((TILE, TILE), 0) < MP
        meet = mul(reads, writes, NT)
        cums[:, here] = (cum + run[0:1, :]).T[0:8, :]
        last_row = cum[127:128, :]
        decays, both, sizes = head_terms(delta, cum, lower, left)
        x = act[:, :CH]
        xd = x * sizes
        held = state[...]
        carried = jnp.exp(both) * mul(reads, low(held), NT)
        out = []
        for p in range(PAIRS):
            lanes = slice(TILE * p, TILE * (p + 1))
            mix = jnp.concatenate([low(meet * d) for d in decays[2 * p : 2 * p + 2]], axis=1)
            out.append(mul(mix, low(halves(xd[:, lanes], left))))
        y0[here, :] = jnp.concatenate(out, axis=1) + carried + skip[0:1, :] * x
        xw = low(jnp.exp(both[127:128, :] - both) * xd)
        state[...] = head_rows(jnp.exp(last_row), top) * held + mul(xw, writes, TN)
        run[...] = run[...] + last_row
        return unused

    lax.fori_loop(0, rest.shape[0] // TILE, one_tile, 0, unroll=2)
    packed[...] = pack_rows(state[...], run[0:1, :])


def skipping(kernel, before, count):
    def run(*refs):
        kernel(*refs[:before], *refs[before + count :])

    return run


def whole_block(*shape):
    return pl.BlockSpec(shape, lambda *i: (0,) * len(shape))


def whole_call(kernel, place, args, outs, scratch, megabytes, micros, deps, name):
    count = 0 if place is None else 1
    before = len(args) + count
    specs = [whole_block(*a.shape) if hasattr(a, "shape") else a[1] for a in args]
    args = [a if hasattr(a, "shape") else a[0] for a in args]
    return pl.pallas_call(
        skipping(kernel, before, len(deps)),
        grid_spec=pltpu.PrefetchScalarGridSpec(
            num_scalar_prefetch=count,
            grid=(1,),
            in_specs=specs + unread(deps),
            out_specs=[whole_block(*o.shape) for o in outs],
            scratch_shapes=scratch,
        ),
        out_shape=outs,
        compiler_params=params(megabytes),
        cost_estimate=taking(micros),
        name=name,
    )(*([] if place is None else [place]), *args, *deps)


def like(shape, kind):
    return jax.ShapeDtypeStruct(shape, kind)


def mixer_forward(place, rest, tail, taps, heads, skip, deps=()):
    rows = rest.shape[0]
    tiles = rows // TILE
    return whole_call(
        mixer_forward_kernel,
        place,
        [rest, tail, taps, heads, skip],
        [
            like((rows, CH), f32),
            like((rows, NS), bf16),
            like((8, rows), f32),
            like((tiles, CH, NS), bf16),
            like((tiles, 8, 128), f32),
            like((CH + 16, NS), bf16),
        ],
        [
            pltpu.VMEM((TILE + 8, CONV), f32),
            pltpu.VMEM((CH, NS), f32),
            pltpu.VMEM((8, 128), f32),
        ],
        20,
        6,
        deps,
        "mixer_forward",
    )


def mixer_backward_kernel(
    count, place, rest, tail, taps, heads, skip, starts, runs, incoming, grad_y, *refs
):
    packs = refs[:count]
    grad_pre, first, grad_taps, sums, grad_skip, ext, dext, grad_state = refs[count:]
    sum_packs(packs, grad_state)
    dext[128:136, :] = jnp.zeros((8, CONV), f32)
    grad_taps[...] = jnp.zeros_like(grad_taps)
    sums[...] = jnp.zeros_like(sums)
    grad_skip[...] = jnp.zeros_like(grad_skip)
    tiles = rest.shape[0] // TILE

    def one_tile(step, unused):
        g = tiles - 1 - step
        here = tile_rows(g, place)
        before = tile_of(jnp.maximum(g - 1, 0), place) * TILE + TILE - 16
        before = rest[pl.ds(pl.multiple_of(before, 16), 16), :CONV].astype(f32)
        ext[8:136, :] = rest[here, :CONV].astype(f32)
        ext[0:8, :] = jnp.where(g == 0, tail[...].astype(f32), before)[8:16, :]
        total = conv_sums(ext, taps)
        gate = jax.nn.sigmoid(total)
        act = total * gate
        writes = low(act[:, CH : CH + NS])
        reads = low(act[:, CH + NS :])
        moved, delta, cum, lower = step_sizes(rest[here, STEP_AT:].astype(f32), heads)
        rows = iota((TILE, TILE), 0)
        cols = iota((TILE, TILE), 1)
        left = cols < MP
        top = rows < MP
        meet = mul(reads, writes, NT)
        last_row = cum[127:128, :]
        shrink = jnp.exp(last_row)
        decays, both, sizes = head_terms(delta, cum, lower, left)
        x = act[:, :CH]
        xd = x * sizes
        xd_low = low(xd)
        dy_low = grad_y[here, :]
        dy = dy_low.astype(f32)
        held = starts[g].astype(f32) + head_rows(jnp.exp(runs[g][0:1, :]), top) * incoming[...]
        held_low = low(held)
        ds = grad_state[...]
        ds_low = low(ds)
        from_start = jnp.exp(both)
        to_end = jnp.exp(both[127:128, :] - both)
        carried = from_start * mul(reads, held_low, NT)
        kept = to_end * mul(writes, ds_low, NT)
        dy_start = low(dy * from_start)
        grad_reads = mul(dy_start, held_low)
        grad_writes = mul(low(xd * to_end), ds_low)
        grad_meet = jnp.zeros((TILE, TILE), f32)
        within, backs = [], []
        for p in range(PAIRS):
            lanes = slice(TILE * p, TILE * (p + 1))
            l0, l1 = decays[2 * p : 2 * p + 2]
            dy_two = halves(dy_low[:, lanes], left)
            m0, m1 = low(meet * l0), low(meet * l1)
            dm = mul(dy_two, xd_low[:, lanes], NT)
            grad_meet = grad_meet + dm[:TILE] * l0 + dm[TILE:] * l1
            mix = jnp.concatenate([m0, m1], axis=1)
            within.append(mul(mix, halves(xd_low[:, lanes], left)))
            backs.append(mul(jnp.concatenate([m0, m1], axis=0), dy_two, TN))
        within = jnp.concatenate(within, axis=1)
        backs = jnp.concatenate(backs, axis=1)
        dxd = backs + kept
        grad_x = dxd * sizes + skip[0:1, :] * dy
        kept_part = kept * xd
        along = dy * (within + carried) - kept_part - xd_low.astype(f32) * backs
        grad_skip[0:1, :] = grad_skip[0:1, :] + jnp.sum(dy * x, axis=0, keepdims=True)
        product = held * ds
        ends = [jnp.sum(kept_part, axis=0, keepdims=True)]
        head_of = iota((CH, 128), 0) // MP == iota((CH, 128), 1)
        pick = low(head_of)
        by_row = jnp.sum(product, axis=1, keepdims=True)
        state_part = jnp.sum(jnp.where(head_of, by_row, 0.0), axis=0, keepdims=True)
        grad_state[...] = head_rows(shrink, top) * ds + mul(dy_start, reads, TN)
        meet_low = low(grad_meet)
        grad_reads = grad_reads + mul(meet_low, writes)
        grad_writes = grad_writes + mul(meet_low, reads, TN)
        ends.append(jnp.zeros((7, CH), f32))
        stacked = jnp.concatenate([along, dxd * x] + ends, axis=0)
        high_part = low(stacked)
        low_part = low(stacked - high_part.astype(f32))
        by_head = mul(high_part, pick) + mul(low_part, pick)
        grad_cum = by_head[:TILE]
        grad_delta = by_head[TILE : 2 * TILE]
        last_add = state_part * shrink + by_head[2 * TILE : 2 * TILE + 1]
        grad_cum = grad_cum + jnp.where(rows == TILE - 1, last_add, 0.0)
        later = mul_exact(low(rows <= cols), grad_cum)
        grad_raw = (grad_delta + heads[0:1, :] * later) * jax.nn.sigmoid(moved)
        grad_raw = jnp.where(cols < MIX, grad_raw, 0.0)
        sums[0:1, :] = sums[0:1, :] + heads[0:1, :] * jnp.sum(delta * later, axis=0, keepdims=True)
        sums[1:2, :] = sums[1:2, :] + jnp.sum(grad_raw, axis=0, keepdims=True)
        grad_act = jnp.concatenate([grad_x, grad_writes, grad_reads], axis=1)
        grad_total = grad_act * (gate * (1.0 + total * (1.0 - gate)))
        dext[0:128, :] = grad_total
        out = dext[3:131, :] * taps[0:1, :]
        for k in range(1, 4):
            out = out + dext[3 - k : 131 - k, :] * taps[k : k + 1, :]
        for k in range(4):
            grad_taps[k : k + 1, :] = grad_taps[k : k + 1, :] + jnp.sum(
                grad_total * ext[5 + k : 133 + k, :], axis=0, keepdims=True
            )
        grad_pre[here, :CONV] = low(out)
        grad_pre[here, STEP_AT:] = low(grad_raw)
        dext[128:136, :] = grad_total[0:8, :]
        first[...] = grad_total[0:8, :]
        return unused

    lax.fori_loop(0, tiles, one_tile, 0, unroll=2)


def mixer_backward(
    place, rest, tail, taps, heads, skip, starts, runs, incoming, grad_y, packs, deps=()
):
    rows = rest.shape[0]
    return whole_call(
        functools.partial(mixer_backward_kernel, len(packs)),
        place,
        [rest, tail, taps, heads, skip, starts, runs, incoming, grad_y, *packs],
        [
            like((rows, QUERY_AT), bf16),
            like((8, CONV), f32),
            like((8, CONV), f32),
            like((8, 128), f32),
            like((8, CH), f32),
        ],
        [
            pltpu.VMEM((TILE + 8, CONV), f32),
            pltpu.VMEM((TILE + 8, CONV), f32),
            pltpu.VMEM((CH, NS), f32),
        ],
        24,
        13,
        deps,
        "mixer_backward",
    )


def fix_ends(place, grad_pre, from_next, taps):
    def kernel(place, grad_pre, from_next, taps, out):
        fixed = jnp.zeros((16, CONV), f32)
        rows = iota((16, CONV), 0)
        for d in range(3):
            part = from_next[0:1, :] * taps[d : d + 1, :]
            for k in range(d):
                part = part + from_next[d - k : d - k + 1, :] * taps[k : k + 1, :]
            fixed = fixed + jnp.where(rows == 13 + d, part, 0.0)
        out[:, :CONV] = low(grad_pre[:, :CONV].astype(f32) + fixed)
        out[:, CONV:] = grad_pre[:, CONV:]

    block = pl.BlockSpec((16, QUERY_AT), lambda i, s: (s[3], 0))
    return pl.pallas_call(
        kernel,
        grid_spec=pltpu.PrefetchScalarGridSpec(
            num_scalar_prefetch=1,
            grid=(1,),
            in_specs=[block, whole_block(8, CONV), whole_block(8, CONV)],
            out_specs=block,
        ),
        out_shape=like(grad_pre.shape, bf16),
        input_output_aliases={1: 0},
        compiler_params=params(8),
        cost_estimate=taking(1),
        name="fix_ends",
    )(place, grad_pre, from_next, taps)


def tile_number(stored, place):
    return ((stored % 2) ^ place[1]) * HEADS + ((stored // 2) ^ place[0])


def masked(scores, place, query_tile):
    reach = iota((TILE, TILE), 0) - iota((TILE, TILE), 1)
    rows = []
    for i in range(scores.shape[0] // TILE):
        cols = []
        for j in range(scores.shape[1] // TILE):
            gap = (tile_number(query_tile + j, place) - tile_number(i, place)) * TILE
            part = scores[TILE * i : TILE * (i + 1), TILE * j : TILE * (j + 1)]
            cols.append(jnp.where(reach <= gap, part, -BIG))
        rows.append(jnp.concatenate(cols, axis=1))
    return jnp.concatenate(rows, axis=0)


def attend_kernel(back, closing, count, place, *refs):
    diagonal = back == 0
    query, pair = refs[:2]
    refs = refs[2:]
    if not diagonal:
        acc_in, stat_in = refs[:2]
        refs = refs[2:]
    refs = refs[count:]
    if closing:
        attended, logs = refs
    else:
        acc_out, stat_out = refs
    wide = 256
    columns = query.shape[0]
    items = [
        (j, slice(wide * i, wide * (i + 1))) for i in range(columns // wide) for j in range(QD // HD)
    ]

    def put(j, cols, acc, new, total):
        if closing:
            attended[cols, HD * j : HD * (j + 1)] = low((acc / total).T)
            logs[j, :, cols] = new + jnp.log2(total)
        else:
            acc_out[j, :, cols] = acc
            stat_out[j, 0:1, cols] = new
            stat_out[j, 1:2, cols] = total

    def work():
        keys = pair[:, :HD]
        vals = pair[:, HD:]

        def start(j, cols):
            scores = mul(keys, query[cols, HD * j : HD * (j + 1)], NT)
            return masked(scores, place, cols.start // TILE) if diagonal else scores

        def weigh(scores, j, cols):
            new = jnp.max(scores, axis=0, keepdims=True) * exponent_scale
            if not diagonal:
                new = jnp.maximum(new, stat_in[j, 0:1, cols])
            probs = jnp.exp2(scores * exponent_scale - new)
            return low(probs), jnp.sum(probs, axis=0, keepdims=True), new

        def finish(probs, total, new, j, cols):
            acc = mul(vals, probs, TN)
            if not diagonal:
                fade = jnp.exp2(stat_in[j, 0:1, cols] - new)
                total = total + stat_in[j, 1:2, cols] * fade
                acc = acc + acc_in[j, :, cols] * fade
            put(j, cols, acc, new, total)

        scores = start(*items[0])
        pending = None
        for n, item in enumerate(items):
            following = start(*items[n + 1]) if n + 1 < len(items) else None
            weighed = weigh(scores, *item)
            if pending is not None:
                finish(*pending)
            pending = weighed + item
            scores = following
        finish(*pending)

    if diagonal:
        work()
    else:
        active = place[2] >= back
        pl.when(active)(work)

        @pl.when(jnp.logical_not(active))
        def _():
            for j, cols in items:
                put(j, cols, acc_in[j, :, cols], stat_in[j, 0:1, cols], stat_in[j, 1:2, cols])


def attend(place, query, pair, back, carried, closing, deps=()):
    diagonal = back == 0
    rows = query.shape[0]
    heads = QD // HD
    whole = lambda *shape: pl.BlockSpec(shape, lambda i, s: (0,) * len(shape))
    in_specs = [
        whole(rows, QD),
        whole(rows, 2 * HD),
    ]
    running = [whole(heads, HD, rows), whole(heads, 8, rows)]
    if not diagonal:
        in_specs += running
    if closing:
        out_specs = [whole(rows, QD), whole(heads, 1, rows)]
        out_shape = [
            jax.ShapeDtypeStruct((rows, QD), bf16),
            jax.ShapeDtypeStruct((heads, 1, rows), f32),
        ]
    else:
        out_specs = running
        out_shape = [
            jax.ShapeDtypeStruct((heads, HD, rows), f32),
            jax.ShapeDtypeStruct((heads, 8, rows), f32),
        ]
    return pl.pallas_call(
        functools.partial(attend_kernel, back, closing, len(deps)),
        grid_spec=pltpu.PrefetchScalarGridSpec(
            num_scalar_prefetch=1,
            grid=(1,),
            in_specs=in_specs + unread(deps),
            out_specs=out_specs,
        ),
        out_shape=out_shape,
        compiler_params=params(60 if closing else 16),
        cost_estimate=taking(5),
        name="attend",
    )(place, query, pair, *(() if diagonal else carried), *deps)


def attend_back_kernel(back, opening, count, place, *refs):
    diagonal = back == 0
    query, grad_out, logs, terms, pair = refs[:5]
    refs = refs[5:]
    if not opening:
        grad_in = refs[0]
        refs = refs[1:]
    grad_query, grad_pair = refs[count:]
    wide = 512

    def work():
        keys = pair[:, :HD]
        vals = pair[:, HD:]
        keys_sum = None
        for i in range(query.shape[0] // wide):
            cols = slice(wide * i, wide * (i + 1))
            for j in range(QD // HD):
                lanes = slice(HD * j, HD * (j + 1))
                q = query[cols, lanes]
                do = grad_out[cols, lanes]
                scores = mul(keys, q, NT)
                if diagonal:
                    scores = masked(scores, place, cols.start // TILE)
                probs = jnp.exp2(scores * exponent_scale - logs[j, :, cols])
                grad_probs = mul(vals, do, NT)
                grad_scores = low(probs * (grad_probs - terms[j, :, cols]))
                vals_add = mul(low(probs), do)
                keys_add = mul(grad_scores, q)
                add = mul(keys, grad_scores, TN)
                if not opening:
                    add = add + grad_in[j, :, cols]
                if diagonal:
                    grad_query[cols, lanes] = low((add * score_scale).T)
                else:
                    grad_query[j, :, cols] = add
                if keys_sum is None:
                    keys_sum, vals_sum = keys_add, vals_add
                else:
                    keys_sum, vals_sum = keys_sum + keys_add, vals_sum + vals_add
        grad_pair[:, :HD] = low(keys_sum * score_scale)
        grad_pair[:, HD:] = low(vals_sum)

    if diagonal:
        work()
    else:
        active = place[2] >= back
        pl.when(active)(work)

        @pl.when(jnp.logical_not(active))
        def _():
            grad_query[...] = jnp.zeros_like(grad_query) if opening else grad_in[...]
            grad_pair[...] = jnp.zeros_like(grad_pair)


def attend_back(place, query, grad_out, logs, terms, pair, grad_query, back, deps=()):
    diagonal = back == 0
    rows = query.shape[0]
    heads = QD // HD
    whole = lambda *shape: pl.BlockSpec(shape, lambda i, s: (0,) * len(shape))
    in_specs = [
        whole(rows, QD),
        whole(rows, QD),
        whole(heads, 1, rows),
        whole(heads, 1, rows),
        whole(rows, 2 * HD),
    ]
    args = [place, query, grad_out, logs, terms, pair]
    opening = grad_query is None
    if not opening:
        in_specs.append(whole(heads, HD, rows))
        args.append(grad_query)
    if diagonal:
        query_spec = whole(rows, QD)
        query_shape = jax.ShapeDtypeStruct((rows, QD), bf16)
    else:
        query_spec = whole(heads, HD, rows)
        query_shape = jax.ShapeDtypeStruct((heads, HD, rows), f32)
    return pl.pallas_call(
        functools.partial(attend_back_kernel, back, opening, len(deps)),
        grid_spec=pltpu.PrefetchScalarGridSpec(
            num_scalar_prefetch=1,
            grid=(1,),
            in_specs=in_specs + unread(deps),
            out_specs=[query_spec, whole(rows, 2 * HD)],
        ),
        out_shape=[
            query_shape,
            jax.ShapeDtypeStruct((rows, 2 * HD), bf16),
        ],
        compiler_params=params(VMEM),
        cost_estimate=taking(7),
        name="attend_back",
    )(*args, *deps)


def ring(i):
    j = (i + 1) % HEADS
    return j ^ (j // 2)


def load_piece(i, pieces, held, which=None):
    half = pieces[0].shape[-2]
    if which is not None:
        pieces = [p.at[which] for p in pieces]
    for at, k in enumerate((1, 3, 2, 0)):

        @pl.when(i == at)
        def _(k=k):
            held[:half, :] = pieces[2 * k][...]
            held[half:, :] = pieces[2 * k + 1][...]

    return held[...]


def piece_specs(pieces):
    return [fixed_block(*p.shape) for p in pieces]


def put_scatter(i, value, refs):
    send_one, send_two, keep_one, keep_two, own = refs
    half = keep_one.shape[0]
    top, bottom = low(value[:half]), low(value[half:])

    @pl.when(i == 0)
    def _():
        send_one[0] = top
        keep_two[...] = bottom

    @pl.when(i == 1)
    def _():
        send_one[0] = top
        send_two[0] = bottom

    @pl.when(i == 2)
    def _():
        keep_one[...] = top
        send_two[0] = bottom

    @pl.when(i == 3)
    def _():
        own[...] = value


def scatter_outs(half, columns):
    specs = [
        pl.BlockSpec((1, half, columns), lambda i: (jnp.minimum(i, 1), 0, 0)),
        pl.BlockSpec((1, half, columns), lambda i: (jnp.clip(i - 1, 0, 1), 0, 0)),
        pl.BlockSpec((half, columns), lambda i: (0, 0)),
        pl.BlockSpec((half, columns), lambda i: (0, 0)),
        pl.BlockSpec((2 * half, columns), lambda i: (0, 0)),
    ]
    shapes = [
        jax.ShapeDtypeStruct((2, half, columns), bf16),
        jax.ShapeDtypeStruct((2, half, columns), bf16),
        jax.ShapeDtypeStruct((half, columns), bf16),
        jax.ShapeDtypeStruct((half, columns), bf16),
        jax.ShapeDtypeStruct((2 * half, columns), f32),
    ]
    return specs, shapes


def scatter_parts(parts, marks=()):
    send_one, send_two, keep_one, keep_two, own = parts
    first = pin(to_head(send_one, 1), *marks)
    second = pin(to_head(send_two, 2), *marks)
    top = to_head(add_low(keep_one, first[1]), 2)
    bottom = to_head(add_low(keep_two, second[0]), 1)
    half = keep_one.shape[0]
    return jnp.concatenate(
        [
            own[:half] + first[0].astype(f32) + top.astype(f32),
            own[half:] + second[1].astype(f32) + bottom.astype(f32),
        ],
        axis=0,
    )


def by_ring(*block):
    return pl.BlockSpec(block, lambda i: (ring(i), 0))


def row_sums(x):
    ones = jnp.ones((8, x.shape[1]), bf16)
    high_part = low(x)
    low_part = low(x - high_part.astype(f32))
    return (mul(ones, high_part, NT) + mul(ones, low_part, NT))[0:1, :]


def column_of(row, width):
    column = jnp.broadcast_to(row, (128, row.shape[1])).T
    return jnp.concatenate([column] * (width // 128), axis=1)


def fixed_block(*shape):
    return pl.BlockSpec(shape, lambda i: (0,) * len(shape), pipeline_mode=pl.Buffered(1))


def tiled_call(kernel, steps, in_specs, out_specs, out_shape, scratch, micros, deps, name):
    count = len(deps)
    ins = len(in_specs)

    def run(*refs):
        kernel(*refs[:ins], *refs[ins + count :])

    return pl.pallas_call(
        run,
        grid=(steps,),
        in_specs=in_specs + unread(deps),
        out_specs=out_specs,
        out_shape=out_shape,
        scratch_shapes=scratch,
        compiler_params=params(32 if name == "feed_forward" else VMEM),
        cost_estimate=taking(micros),
        name=name,
    )


def weight_rows(normed, grads, seq_count, extra=(), deps=()):
    rows, features = normed.shape
    wide = features // HEADS
    shard = wide // seq_count
    columns = sum(g.shape[1] for g in grads) + 128 * len(extra)

    def kernel(*refs):
        normed, grads, out = refs[0], refs[1 : 1 + len(grads_in)], refs[-1]
        at = 0
        for e in refs[1 + len(grads_in) : -1]:
            filled = jnp.concatenate(
                [e[...], jnp.zeros((128 - e.shape[0], wide), f32)], axis=0
            ).T
            out[:, :, :, columns - 128 :] = low(filled.reshape(seq_count, 1, shard, 128))
        for g in grads:
            value = mul(normed[...], g[...], TN).reshape(seq_count, 1, shard, g.shape[1])
            out[:, :, :, at : at + g.shape[1]] = low(value)
            at += g.shape[1]

    grads_in = grads
    out = tiled_call(
        kernel,
        HEADS,
        [pl.BlockSpec((rows, wide), lambda i: (0, i))]
        + [fixed_block(*g.shape) for g in grads]
        + [pl.BlockSpec((e.shape[0], wide), lambda i: (0, i)) for e in extra],
        [pl.BlockSpec((seq_count, 1, shard, columns), lambda i: (0, i, 0, 0))],
        [jax.ShapeDtypeStruct((seq_count, HEADS, shard, columns), bf16)],
        [],
        columns / 300,
        deps,
        "weight_rows",
    )(normed, *grads, *extra, *deps)[0]
    return out.reshape(seq_count, HEADS * shard, columns)


def fetch_weights(source, held, sems, place):
    return [
        pltpu.make_async_copy(source.at[:, place[0] ^ j], held.at[j], sems.at[j])
        for j in range(HEADS)
    ]


def project_all(place, tokens, weights, spots, deps=()):
    half, features = tokens[0].shape[1:]
    rows = 2 * half * HEADS
    seq_count, _, shard, columns = weights.shape
    widths = (features, QUERY_AT, QD, CH, 2 * HD)
    count = len(deps)

    def kernel(place, *refs):
        tokens, spots, source = refs[:8], refs[8], refs[9]
        refs = refs[10 + count :]
        outs, (small, taps, gain_mix) = refs[:5], refs[5:8]
        held, scaled, *stored, sems, out_sems = refs[8:]
        copies = fetch_weights(source, held, sems, place)
        for copy in copies:
            copy.start()
        for t in range(2 * HEADS):
            x = tokens[t][0].astype(f32)
            scale = lax.rsqrt(jnp.mean(x * x, axis=1, keepdims=True) + norm_eps)
            scaled[half * t : half * (t + 1), :] = x * scale
        sources = iota((features, spots.shape[1]), 0)
        main = low(sources == spots[0:1, :])
        rest = low(sources == spots[1:2, :])
        for copy in copies:
            copy.wait()

        def take(start, stop):
            part = held[:, :, :, start:stop]
            if shard % 16 != 0:
                part = part.astype(f32)
            return low(part.reshape(features, stop - start))

        def send(i):
            return pltpu.make_async_copy(stored[i], outs[i], out_sems.at[i])

        turned = take(STEP_AT, STEP_AT + 128).astype(f32).T
        small_rows = turned[GAIN_LANE : GAIN_LANE + 16, :]
        small[...] = small_rows
        stored[0][...] = low(scaled[...] * small_rows[0:1, :])
        send(0).start()
        x = stored[0][...]
        stored[4][...] = low(mul(x, take(KEY_AT, KEY_AT + 2 * HD)))
        send(4).start()
        stored[1][:, :CH] = low(mul(x, take(0, CH)))
        stored[1][:, CH:] = low(mul(x, take(CH, QUERY_AT)))
        send(1).start()
        stored[2][...] = low(mul(x, take(QUERY_AT, GATE_AT)))
        send(2).start()
        stored[3][...] = low(mul(x, take(GATE_AT, KEY_AT)))
        send(3).start()
        small_low = low(small_rows)
        mains, rests = mul(small_low, main), mul(small_low, rest)
        gain_mix[...] = mains[2:3, CONV:] + rests[3:4, CONV:]
        taps[0:4, :] = mains[4:8, :CONV] + rests[8:12, :CONV]
        taps[4:8, :] = jnp.zeros((4, CONV), f32)
        for i in range(5):
            send(i).wait()

    ANY = pl.BlockSpec(memory_space=pl.ANY)
    token_block = pl.BlockSpec((1, half, features), lambda *i: (0, 0, 0))
    return pl.pallas_call(
        kernel,
        grid_spec=pltpu.PrefetchScalarGridSpec(
            num_scalar_prefetch=1,
            grid=(1,),
            in_specs=[token_block] * 8 + [whole_block(*spots.shape), ANY] + unread(deps),
            out_specs=[ANY] * 5
            + [whole_block(16, features), whole_block(8, CONV), whole_block(1, CH)],
            scratch_shapes=[
                pltpu.VMEM((HEADS, seq_count, shard, columns), bf16),
                pltpu.VMEM((rows, features), f32),
                *[pltpu.VMEM((rows, wide), bf16) for wide in widths],
                pltpu.SemaphoreType.DMA((HEADS,)),
                pltpu.SemaphoreType.DMA((5,)),
            ],
        ),
        out_shape=[like((rows, wide), bf16) for wide in widths]
        + [like((16, features), f32), like((8, CONV), f32), like((1, CH), f32)],
        compiler_params=params(60),
        cost_estimate=taking(8),
        name="project_all",
    )(place, *tokens, spots, weights, *deps)


def exact(values, picks):
    high_part = low(values)
    low_part = low(values - high_part.astype(f32))
    return mul(high_part, picks) + mul(low_part, picks)


def small_rows(place, grad_taps, sums, grad_skip, spots, shard, features, deps=()):
    spans = -(-MH // shard)
    total = 8 + 3 * spans
    rows = -(-total // 16) * 16

    def kernel(place, grad_taps, sums, grad_skip, spots, out):
        places = iota((CONV, features), 1)
        turned = spots[...].T
        for half in range(2):
            picks = low(places == turned[:CONV, half : half + 1])
            out[4 * half : 4 * half + 4, :] = exact(grad_taps[...], picks)[0:4, :]
        by_head = low(iota((CH, 128), 0) // MP == iota((CH, 128), 1))
        skips = exact(grad_skip[...], by_head)[0:1, :]
        values = jnp.concatenate([sums[0:2, :], skips, jnp.zeros((5, 128), f32)], axis=0)
        within = iota((128, features), 1) % shard - place[0] * MIX
        head = iota((128, features), 0)
        for j in range(spans):
            spread = exact(values, low((head == within + shard * j) & (head < MIX)))
            for i in range(3):
                at = 8 + i * spans + j
                out[at : at + 1, :] = spread[i : i + 1, :]
        out[total:, :] = jnp.zeros((rows - total, features), f32)

    return whole_call(
        kernel,
        place,
        [grad_taps, sums, grad_skip, spots],
        [like((rows, features), f32)],
        [],
        16,
        2,
        deps,
        "small_rows",
    )[0]


def pack_weights(place, inputs, state, step, query, gate, pairs, ff_gate, ff_up, gains, conv):
    shard = state.shape[0]
    conv_shard, mix_shard = conv.shape[1], gains[2].shape[1]
    ff = ff_gate.shape[1] // HEADS
    columns = CONV + 128 + QD + CH + 2 * HD + 2 * ff
    group = HEADS // KVH

    def kernel(place, inputs, state, step, query, gate, pairs, ff_gate, ff_up, *refs):
        gain_in, gain_two, gain_mix, conv = refs[:4]
        outs, (rows, steps) = refs[4 : 4 + HEADS], refs[4 + HEADS :]
        rows[...] = jnp.zeros_like(rows)
        steps[...] = jnp.zeros_like(steps)
        at = GAIN_LANE
        rows[at : at + 1, :shard] = gain_in[...].astype(f32)
        rows[at + 1 : at + 2, :shard] = gain_two[...].astype(f32)
        rows[at + 2 : at + 3, :shard] = gain_mix[:, :shard].astype(f32)
        rows[at + 3 : at + 4, : mix_shard - shard] = gain_mix[:, shard:].astype(f32)
        taps = conv[...].astype(f32)
        rows[at + 4 : at + 8, :shard] = taps[:, :shard]
        rows[at + 8 : at + 12, : conv_shard - shard] = taps[:, shard:]
        steps[:MH, :shard] = step[...].astype(f32)
        base = rows[...].T[:shard, :]
        every = low(steps[...].T[:shard, :])
        source, target = iota((128, 128), 0), iota((128, 128), 1)
        for m in range(HEADS):
            j = place[0] ^ m

            def cut(ref, wide, at=0, spot=j):
                return ref[:, pl.ds(pl.multiple_of(at + spot * wide, 128), wide)]

            moved = low((source == target + j * MIX) & (target < MIX))
            both = j // group
            blocks = [
                cut(inputs, CH), state[...], low(base + mul(every, moved)), cut(query, QD),
                cut(gate, CH), cut(pairs, HD, 0, both), cut(pairs, HD, KVH * HD, both),
                cut(ff_gate, ff), cut(ff_up, ff),
            ]
            at = 0
            for block in blocks:
                outs[m][:, at : at + block.shape[1]] = block
                at += block.shape[1]

    return whole_call(
        kernel,
        place,
        [inputs, state, step, query, gate, pairs, ff_gate, ff_up, *gains, conv],
        [like((shard, columns), bf16)] * HEADS,
        [pltpu.VMEM((128, 128), f32), pltpu.VMEM((128, 128), f32)],
        60,
        2,
        (),
        "pack_weights",
    )


def gate_of(z_tile):
    z = z_tile.astype(f32)
    return z, jax.nn.sigmoid(z)


def lanes_of(rows, p):
    left = iota((rows.shape[1], TILE), 1) < MP
    first, second = rows[2 * p : 2 * p + 1, :], rows[2 * p + 1 : 2 * p + 2, :]
    return jnp.where(left, column_of(first, TILE), column_of(second, TILE))


def mix_tokens(y0, cums, reads, packs, z, deps=()):
    rows = y0.shape[0]
    wide = rows // HEADS
    count = len(packs)

    def kernel(y0, cums, reads, z, *refs):
        packs, (mixed_out, squares, incoming) = refs[:count], refs[count:]
        sum_packs(packs, incoming)
        for t in range(HEADS):
            here = slice(wide * t, wide * (t + 1))
            met = mul(reads[here, :], low(incoming[...]), NT)
            growth = jnp.exp(cums[:, here])
            grown = jnp.concatenate([lanes_of(growth, p) for p in range(PAIRS)], axis=1)
            mixed = low(y0[here, :] + grown * met)
            mixed_out[here, :] = mixed
            gate, sig = gate_of(z[here, :])
            inner = mixed.astype(f32) * gate * sig
            squares[:, here] = row_sums(inner * inner)

    return whole_call(
        kernel,
        None,
        [y0, cums, reads, z, *packs],
        [like((rows, CH), bf16), like((1, rows), f32), like((CH, NS), f32)],
        [],
        20,
        3,
        deps,
        "mix_tokens",
    )


def branch_out(mixed, z, scale, gain, attended, weights, deps=()):
    rows, features = mixed.shape[0], weights.shape[1]
    wide = rows // HEADS
    specs, shapes = scatter_outs(wide // 2, features)

    def kernel(mixed, z, scale, gain, attended, weights, gated_out, *parts):
        gate, sig = gate_of(z[...])
        inner = mixed[...].astype(f32) * gate * sig
        gated = low(inner * column_of(scale[...], CH) * gain[...])
        gated_out[...] = gated
        value = mul(gated, weights[:CH, :]) + mul(attended[...], weights[CH:, :])
        put_scatter(pl.program_id(0), value, parts)

    outs = tiled_call(
        kernel,
        HEADS,
        [
            by_ring(wide, CH),
            by_ring(wide, CH),
            pl.BlockSpec((1, wide), lambda i: (0, ring(i))),
            pl.BlockSpec((1, CH), lambda i: (0, 0)),
            by_ring(wide, QD),
            fixed_block(CH + QD, features),
        ],
        [by_ring(wide, CH)] + specs,
        [jax.ShapeDtypeStruct((rows, CH), bf16)] + shapes,
        [],
        3,
        deps,
        "branch_out",
    )(mixed, z, scale, gain, attended, weights, *deps)
    return outs[0], outs[1:]


def feed_forward(tokens, grads, weights, weights_down, deps=()):
    wide, features = 2 * tokens[0].shape[0], tokens[0].shape[1]
    rows = wide * HEADS
    ff = weights_down.shape[0]
    specs, shapes = scatter_outs(wide // 2, features)

    def kernel(*refs):
        tokens, grads = refs[:8], refs[8:16]
        weights, weights_down, tokens_out, grads_out, acted_out, inner_out = refs[16:22]
        parts, held, held_grads = refs[22:27], refs[27], refs[28]
        i = pl.program_id(0)
        x = load_piece(i, tokens, held)
        g = load_piece(i, grads, held_grads, 0)
        tokens_out[...] = x
        grads_out[...] = g
        inner = mul(x, weights[...])
        grad_acted = mul(g, weights_down[...], NT)
        gate, up = inner[:, :ff], inner[:, ff:]
        sig = jax.nn.sigmoid(gate)
        silu = gate * sig
        acted_out[...] = low(silu * up)
        grad_gate = low(grad_acted * up * (sig * (1.0 + gate * (1.0 - sig))))
        grad_inner = jnp.concatenate([grad_gate, low(grad_acted * silu)], axis=1)
        inner_out[...] = grad_inner
        put_scatter(i, mul(grad_inner, weights[...], NT), parts)

    outs = tiled_call(
        kernel,
        HEADS,
        piece_specs(tokens)
        + [
            pl.BlockSpec((1,) + g.shape[1:], lambda i: (1, 0, 0), pipeline_mode=pl.Buffered(1))
            for g in grads
        ]
        + [
            fixed_block(features, 2 * ff),
            fixed_block(ff, features),
        ],
        [by_ring(wide, features), by_ring(wide, features), by_ring(wide, ff), by_ring(wide, 2 * ff)]
        + specs,
        [
            jax.ShapeDtypeStruct((rows, features), bf16),
            jax.ShapeDtypeStruct((rows, features), bf16),
            jax.ShapeDtypeStruct((rows, ff), bf16),
            jax.ShapeDtypeStruct((rows, 2 * ff), bf16),
        ]
        + shapes,
        [pltpu.VMEM((wide, features), bf16), pltpu.VMEM((wide, features), bf16)],
        7,
        deps,
        "feed_forward",
    )(*tokens, *grads, weights, weights_down, *deps)
    return outs[0], outs[1], outs[2], outs[3], outs[4:]


def scattered_product(left, weights, deps=()):
    rows, depth = left.shape
    features = weights.shape[1]
    wide = rows // HEADS
    specs, shapes = scatter_outs(wide // 2, features)

    def kernel(left, weights, *parts):
        put_scatter(pl.program_id(0), mul(left[...], weights[...]), parts)

    return tiled_call(
        kernel,
        HEADS,
        [by_ring(wide, depth), fixed_block(depth, features)],
        specs,
        shapes,
        [],
        2,
        deps,
        "scattered_product",
    )(left, weights, *deps)


def branch_back(grads, weights, attended, mixed, z, scale, gain, deps=()):
    wide, features = 2 * grads[0].shape[0], grads[0].shape[1]
    rows = wide * HEADS
    heads = QD // HD

    def kernel(*refs):
        grads = refs[:8]
        weights, attended, mixed, z, scale, gain = refs[8:14]
        grads_out, grad_att, terms, grad_gated, sums, held = refs[14:]
        i = pl.program_id(0)
        g = load_piece(i, grads, held)
        grads_out[...] = g
        both = mul(g, weights[...], NT)
        att = low(both[:, CH:])
        grad_att[...] = att
        product = att.astype(f32) * attended[...].astype(f32)
        for j in range(heads):
            terms[j] = row_sums(product[:, HD * j : HD * (j + 1)])
        gate, sig = gate_of(z[...])
        unit = mixed[...].astype(f32) * gate * sig * column_of(scale[...], CH)
        gated = both[:, :CH]
        grad_gated[...] = low(gated)
        scaled = gated * unit
        sums[...] = row_sums(scaled * gain[...])

    return tiled_call(
        kernel,
        HEADS,
        piece_specs(grads)
        + [
            fixed_block(CH + QD, features),
            by_ring(wide, QD),
            by_ring(wide, CH),
            by_ring(wide, CH),
            pl.BlockSpec((1, wide), lambda i: (0, ring(i))),
            pl.BlockSpec((1, CH), lambda i: (0, 0)),
        ],
        [
            by_ring(wide, features),
            by_ring(wide, QD),
            pl.BlockSpec((heads, 1, wide), lambda i: (0, 0, ring(i))),
            by_ring(wide, CH),
            pl.BlockSpec((1, wide), lambda i: (0, ring(i))),
        ],
        [
            jax.ShapeDtypeStruct((rows, features), bf16),
            jax.ShapeDtypeStruct((rows, QD), bf16),
            jax.ShapeDtypeStruct((heads, 1, rows), f32),
            jax.ShapeDtypeStruct((rows, CH), bf16),
            jax.ShapeDtypeStruct((1, rows), f32),
        ],
        [pltpu.VMEM((wide, features), bf16)],
        4,
        deps,
        "branch_back",
    )(*grads, weights, attended, mixed, z, scale, gain, *deps)


def gate_back(grad_gated, mixed, z, scale, mean, gain, cums, reads, packed, deps=()):
    rows = mixed.shape[0]
    wide = rows // HEADS

    def kernel(
        grad_gated, mixed, z, scale, mean, gain, cums, reads, packed, grad_mixed, grad_z, leaving
    ):
        total = None
        for t in range(HEADS):
            here = slice(wide * t, wide * (t + 1))
            gate, sig = gate_of(z[here, :])
            silu = gate * sig
            value = mixed[here, :].astype(f32)
            factor = column_of(scale[:, here], CH)
            unit = value * silu * factor
            inner = grad_gated[here, :].astype(f32) * gain[...]
            inner = (inner - unit * column_of(mean[:, here], CH)) * factor
            out = low(inner * silu)
            grad_mixed[here, :] = out
            grad_z[here, :] = low(inner * value * (sig * (1.0 + gate * (1.0 - sig))))
            growth = jnp.exp(cums[:, here])
            grown = jnp.concatenate([lanes_of(growth, p) for p in range(PAIRS)], axis=1)
            part = mul(low(out.astype(f32) * grown), reads[here, :], TN)
            total = part if total is None else total + part
        leaving[:CH, :] = low(total)
        leaving[CH:, :] = packed[CH:, :]

    return whole_call(
        kernel,
        None,
        [grad_gated, mixed, z, scale, mean, gain, cums, reads, packed],
        [like((rows, CH), bf16), like((rows, CH), bf16), like((CH + 16, NS), bf16)],
        [],
        20,
        3,
        deps,
        "gate_back",
    )


def normed_back(place, grad_pre, grad_z, grad_query, grad_pair, weights, deps=()):
    rows = grad_pre.shape[0]
    wide = rows // HEADS
    half = wide // 2
    seq_count, _, shard, columns = weights.shape
    features = HEADS * seq_count * shard
    ANY = pl.BlockSpec(memory_space=pl.ANY)

    def kernel(place, grad_pre, grad_query, grad_z, grad_pair, source, *refs):
        send_one, send_two, keep_one, keep_two, own, held, sems = refs
        copies = fetch_weights(source, held, sems, place)
        for copy in copies:
            copy.start()
        for copy in copies:
            copy.wait()
        for k in (1, 3, 2, 0):
            here = slice(wide * k, wide * (k + 1))
            grads = jnp.concatenate(
                [grad_pre[here, :], grad_query[here, :], grad_z[here, :], grad_pair[here, :]],
                axis=1,
            )
            parts = []
            for j in range(HEADS):
                part = held[j]
                if shard % 16 != 0:
                    part = part.astype(f32)
                parts.append(mul(grads, low(part.reshape(seq_count * shard, columns)), NT))
            value = jnp.concatenate(parts, axis=1)
            top, bottom = low(value[:half]), low(value[half:])
            if k == 1:
                send_one[0] = top
                keep_two[...] = bottom
            elif k == 3:
                send_one[1] = top
                send_two[0] = bottom
            elif k == 2:
                keep_one[...] = top
                send_two[1] = bottom
            else:
                own[...] = value

    shapes = scatter_outs(half, features)[1]
    return whole_call(
        kernel,
        place,
        [grad_pre, grad_query, grad_z, grad_pair, (weights, ANY)],
        shapes,
        [
            pltpu.VMEM((HEADS, seq_count, shard, columns), bf16),
            pltpu.SemaphoreType.DMA((HEADS,)),
        ],
        40,
        6,
        deps,
        "normed_back",
    )


def to_head(x, mask):
    return lax.ppermute(x, "head", [(i, i ^ mask) for i in range(HEADS)])


def to_seq(x, mask):
    return lax.ppermute(x, "seq", [(i, i ^ mask) for i in range(lax.axis_size("seq"))])


def shifted(x, blocks):
    count = lax.axis_size("seq")
    route = [(i, i + 2 * blocks) for i in range(count) if 0 <= i + 2 * blocks < count]
    return lax.ppermute(x, "seq", route)


def gather_head(top, bottom):
    one_top = to_head(top, 1)
    two_bottom = to_head(bottom, 2)
    one_bottom = to_head(bottom, 1)
    two_top = to_head(top, 2)
    three_top = to_head(one_top, 2)
    three_bottom = to_head(two_bottom, 1)
    return top, bottom, one_top, one_bottom, two_top, two_bottom, three_top, three_bottom


def gather_rows_low(x):
    half = x.shape[0] // 2
    return gather_head(low(x[:half]), low(x[half:]))


def pin(x, *deps):
    if len(deps) == 0:
        return x
    return lax.optimization_barrier((x,) + deps)[0]


def add_low(*terms):
    return low(sum((t.astype(f32) for t in terms[1:]), terms[0].astype(f32)))


def sum_head(row):
    wide = row.shape[1] // HEADS
    total = row
    for mask in range(1, HEADS):
        got = to_head(row, mask)
        total = total + jnp.concatenate(
            [got[:, wide * (k ^ mask) : wide * ((k ^ mask) + 1)] for k in range(HEADS)], axis=1
        )
    return total


def send_packs(packed, blocks, direction):
    return [shifted(packed, direction * k) for k in range(1, blocks)]


def gather_rows(shard):
    return lax.all_gather(shard, "seq", axis=0, tiled=False)


def scatter_rows(x):
    return lax.psum_scatter(x, "seq", scatter_dimension=0, tiled=False)


def in_order(pieces, index):
    bit = 1
    while bit < len(pieces):
        upper = (index & bit) != 0
        pieces = [jnp.where(upper, pieces[j ^ bit], pieces[j]) for j in range(len(pieces))]
        bit *= 2
    return pieces


def ordered_rows(x, head_index):
    parts = [
        lax.dynamic_index_in_dim(x, head_index ^ j, 1, keepdims=False) for j in range(HEADS)
    ]
    return jnp.stack(parts).reshape(-1, x.shape[-1])


def scatter_direct(x, core, block):
    blocks = x.shape[0] // 2
    x = x.reshape((blocks, 2) + x.shape[1:])
    pick = lambda c: lax.dynamic_index_in_dim(x, c, 1, keepdims=False)
    x = add_low(pick(core), to_seq(pick(1 - core), 1))
    parts = [lax.dynamic_index_in_dim(x, block, 0, keepdims=False)]
    for k in range(1, blocks):
        part = lax.dynamic_index_in_dim(x, block ^ k, 0, keepdims=False)
        parts.append(to_seq(part, 2 * k))
    return parts


LATE = QD + 2 * HD
EARLY_AT = LATE + 128
FF_AT = EARLY_AT + CH + QUERY_AT


def merge_columns(place, late, early, ff):
    shard, ff_wide = ff.shape[1:]
    columns = FF_AT + ff_wide
    count = len(late)

    def kernel(place, *refs):
        late, early, ff, outs = refs[:count], refs[count], refs[count + 1], refs[count + 2 :]
        for m in range(HEADS):
            j = place[0] ^ m
            out = outs[m]
            blocks = [part[j].astype(f32) for part in late]
            out[:, :LATE] = low(sum(part[:, :LATE] for part in blocks))
            small = in_order([part[:, LATE:] for part in blocks], place[2])
            out[:, LATE:EARLY_AT] = low(sum(small))
            out[:, EARLY_AT:FF_AT] = early[j]
            out[:, FF_AT:] = ff[j]

    return whole_call(
        kernel,
        place,
        [*late, early, ff],
        [like((shard, columns), bf16)] * HEADS,
        [],
        16,
        2,
        (),
        "merge_columns",
    )


def finish_columns(place, pieces, weights, gains, conv_shard):
    shard = pieces[0].shape[0]
    ff = weights[6].shape[1] // HEADS
    spans = -(-MH // shard)
    at_state = EARLY_AT + CH
    at_step = EARLY_AT + STEP_AT
    at_gate = EARLY_AT + QUERY_AT

    def fold(weight, grad):
        product = weight.astype(f32) * grad
        tiles = [product[:, 128 * i : 128 * (i + 1)] for i in range(product.shape[1] // 128)]
        return sum(tiles[1:], tiles[0])

    def kernel(place, *refs):
        pieces = refs[:HEADS]
        inputs_w, state_w, step_w, query_w, gate_w, pair_w, ff_w, up_w = refs[4:12]
        gain_in, gain_two = refs[12:14]
        inputs, states, steps, query, gate, pair, ff_gate, ff_up = refs[14:22]
        grad_in, grad_two, taps, *heads = refs[22:]
        owners = [place[0] ^ m for m in range(HEADS)]

        def spread(out, weight, start, wide):
            total = jnp.zeros((shard, 128), f32)
            for m in range(HEADS):
                here = pl.ds(pl.multiple_of(owners[m] * wide, 128), wide)
                grad = pieces[m][:, start : start + wide].astype(f32)
                out[:, here] = grad
                total = total + fold(weight[:, here], grad)
            return total

        first = spread(inputs, inputs_w, EARLY_AT, CH) + spread(query, query_w, 0, QD)
        first = first + spread(gate, gate_w, at_gate, CH)
        second = spread(ff_gate, ff_w, FF_AT, ff) + spread(ff_up, up_w, FF_AT + ff, ff)
        grad = sum(p[:, at_state : at_state + 2 * NS].astype(f32) for p in pieces)
        states[...] = grad
        first = first + fold(state_w[...], grad)
        for i in range(KVH):
            for kind in range(2):
                start = QD + HD * kind
                grad = jnp.zeros((shard, HD), f32)
                for m in range(HEADS):
                    mine = (owners[m] // (HEADS // KVH)) == i
                    part = pieces[m][:, start : start + HD].astype(f32)
                    grad = grad + jnp.where(mine, part, 0.0)
                lanes = slice(HD * (KVH * kind + i), HD * (KVH * kind + i + 1))
                pair[:, lanes] = grad
                first = first + fold(pair_w[:, lanes], grad)
        grad = jnp.zeros((shard, 128), f32)
        source, target = iota((128, 128), 0), iota((128, 128), 1)
        for m in range(HEADS):
            moved = low((target == source + owners[m] * MIX) & (source < MIX))
            grad = grad + mul(pieces[m][:, at_step : at_step + 128], moved)

        def turned(x):
            return jnp.concatenate([x, jnp.zeros((128 - shard, 128), f32)], axis=0).T

        grad = turned(grad)[:MH, :shard]
        steps[...] = grad
        step_sum = jnp.sum(step_w[...].astype(f32) * grad, axis=0, keepdims=True)

        def row(total):
            column = jnp.sum(total, axis=1, keepdims=True)
            return turned(jnp.broadcast_to(column, (shard, 128)))[0:1, :shard]

        grad_in[...] = (row(first) + step_sum) / gain_in[...].astype(f32)
        grad_two[...] = row(second) / gain_two[...].astype(f32)
        small = in_order([p[:, LATE:EARLY_AT].astype(f32) for p in pieces], place[0])
        small = sum(small[1:], small[0])
        rows = turned(small)
        taps[:, 0:shard] = rows[0:4, :shard]
        taps[:, shard:conv_shard] = rows[4:8, : conv_shard - shard]
        for i in range(3):
            for j in range(spans):
                wide = min(shard, MH - j * shard)
                at = 8 + i * spans + j
                heads[i][:, j * shard : j * shard + wide] = rows[at : at + 1, :wide]

    return whole_call(
        kernel,
        place,
        [*pieces, *weights, *gains],
        [like(w.shape, f32) for w in weights]
        + [like((1, shard), f32)] * 2
        + [like((4, conv_shard), f32)]
        + [like((1, MH), f32)] * 3,
        [],
        24,
        4,
        (),
        "finish_columns",
    )


def split_columns(x):
    return x.reshape(x.shape[0], HEADS, -1).swapaxes(0, 1)


def body(
    hidden_in,
    lengths,
    cotangent,
    input_gain,
    mixer_gate,
    mixer_inputs,
    state_weights,
    conv_weight,
    step_weight,
    decay_log,
    step_bias,
    skip_gain,
    query_weight,
    key_value_weight,
    mixer_gain,
    mixer_output,
    attention_out,
    second_gain,
    gate_weight,
    up_weight,
    down_weight,
):
    seq_count = lax.axis_size("seq")
    head_index = lax.axis_index("head")
    seq_index = lax.axis_index("seq")
    block = seq_index // 2
    core = seq_index % 2
    blocks = seq_count // 2
    own_rows, features = hidden_in.shape[2], hidden_in.shape[3]
    rows = 2 * own_rows * HEADS
    shard = input_gain.shape[0]
    ff = gate_weight.shape[1] // HEADS
    mix_shard, down_shard = mixer_output.shape[0], down_weight.shape[0]
    conv_shard = conv_weight.shape[0]
    device = head_index * seq_count + seq_index

    end_row = ((head_index ^ (HEADS - 1)) * 2 + (1 ^ core)) * TILE + TILE - 16
    place = jnp.stack([head_index, core, block, end_row // 16]).astype(jnp.int32)
    packs = pack_weights(
        place, mixer_inputs, state_weights, step_weight.T, query_weight, mixer_gate,
        key_value_weight, gate_weight, up_weight,
        [input_gain[None], second_gain[None], mixer_gain[None]], conv_weight.T,
    )
    wide = packs[0].shape[1] - 2 * ff
    pieces = [packs[0]] + [to_head(packs[m], m) for m in range(1, HEADS)]

    both = jnp.stack([hidden_in[:, 0], cotangent[:, 0]], axis=1)
    keep = lax.dynamic_index_in_dim(both, core, 0, keepdims=False)
    give = lax.dynamic_index_in_dim(both, 1 - core, 0, keepdims=False)
    got = to_seq(give, 1)
    hidden = jnp.concatenate([keep[0], got[0]], axis=0).astype(f32)
    cot = jnp.concatenate([keep[1], got[1]], axis=0)
    first_own = pin(pieces[0], got)
    weights_in = gather_rows(
        jnp.stack([first_own[:, :wide]] + [p[:, :wide] for p in pieces[1:]])
    )
    tokens = 2 * own_rows
    block_rows = own_rows * HEADS
    spot = jnp.arange(tokens)
    positions = (
        (2 * block + ((spot // own_rows) ^ core)) * block_rows
        + head_index * own_rows
        + spot % own_rows
    )
    length = lax.dynamic_index_in_dim(lengths, core, 0, keepdims=False)
    valid = (positions < length).astype(f32)[:, None]
    grad_result_own = cot.astype(f32) * valid
    grad_low = low(grad_result_own)
    both_all = gather_head(
        jnp.stack([keep[0], grad_low[:own_rows]]), jnp.stack([got[0], grad_low[own_rows:]])
    )

    out_pack = jnp.concatenate([mixer_output, attention_out], axis=0)
    out_all = gather_rows(pin(out_pack, *pieces))
    ff_pack = jnp.concatenate([p[:, wide:] for p in pieces] + [down_weight], axis=0)

    def sources(channels, size):
        owner, offset = channels // size, channels % size
        main = jnp.where(offset < shard, owner * shard + offset, -1)
        return jnp.stack([main, jnp.where(offset < shard, -1, owner * shard + offset - shard)])

    spread = jnp.arange(CONV)
    spread = jnp.where(spread < CH, spread + head_index * CH, spread + (MH * MP - CH))
    spots = jnp.concatenate(
        [sources(spread, conv_shard), sources(jnp.arange(CH) + head_index * CH, mix_shard)], axis=1
    )
    spots = jnp.pad(spots, ((0, 6), (0, 0))).astype(jnp.int32)
    (normed, mix_in, query, z, own_pair, small, taps, gain_mix) = project_all(
        place, both_all, weights_in, spots, deps=(ff_pack, out_pack)
    )
    tail = shifted(lax.dynamic_slice(mix_in, (end_row, 0), (16, CONV)), 1)
    gain_in, gain_two = small[0:1], small[1:2]
    scale_in = lax.rsqrt(jnp.mean(hidden * hidden, axis=-1, keepdims=True) + norm_eps)
    unit_in = hidden * scale_in

    pair = [own_pair, shifted(pin(own_pair, tail), 1)]

    decay_part = lax.dynamic_slice_in_dim(-jnp.exp(decay_log), head_index * MIX, MIX)
    bias_part = lax.dynamic_slice_in_dim(step_bias, head_index * MIX, MIX)
    skip_part = lax.dynamic_slice_in_dim(skip_gain, head_index * MIX, MIX)
    heads = jnp.pad(jnp.stack([decay_part, bias_part]), ((0, 6), (0, 128 - MIX)))
    skip = jnp.broadcast_to(jnp.repeat(skip_part, MP)[None], (8, CH))
    y0, reads, cums, starts, runs, packed = mixer_forward(
        place, mix_in, tail, taps, heads, skip
    )
    packs = send_packs(packed, blocks, 1)
    running = attend(place, query, pair[0], 0, None, blocks == 1, deps=(packed,))
    pair.append(shifted(pin(pair[1], running[1], *packs), 1))
    out_all = pin(out_all, packed)
    weights_out = jnp.concatenate(
        [
            out_all[:, :mix_shard].reshape(CH, features),
            out_all[:, mix_shard:].reshape(QD, features),
        ],
        axis=0,
    )
    for k in range(1, blocks):
        running = attend(
            place, query, pair[k], k, running, k == blocks - 1,
            deps=(packed,) if k == 1 else (scale_mix,),
        )
        if k == 1:
            mixed, squares, incoming = mix_tokens(
                y0, cums, reads, packs, z, deps=(running[1], weights_out)
            )
            for j in range(3, blocks):
                pair.append(shifted(pin(pair[-1], squares), 1))
            scale_mix = lax.rsqrt(sum_head(squares) / (MH * MP) + norm_eps)
        if k == blocks - 2:
            ff_all = gather_rows(pin(ff_pack, running[1], pair[-1]))
    attended, logs = running
    ff_all = pin(ff_all, attended)
    weights_ff = ordered_rows(
        ff_all[:, : HEADS * shard].reshape(seq_count, HEADS, shard, 2 * ff), head_index
    )
    weights_down = ff_all[:, HEADS * shard :].reshape(ff, features)
    gated, parts = branch_out(mixed, z, scale_mix, gain_mix, attended, weights_out)
    resid = hidden + scatter_parts(parts)

    scale_two = lax.rsqrt(jnp.mean(resid * resid, axis=-1, keepdims=True) + norm_eps)
    norm_two = resid * scale_two
    normed_two, grad_result, acted, grad_inner, parts = feed_forward(
        gather_rows_low(norm_two * gain_two), both_all, weights_ff, weights_down
    )
    grad_down = low(mul(acted, grad_result, TN)).reshape(seq_count, down_shard, features)
    ff_rows = jnp.concatenate(
        [weight_rows(normed_two, [grad_inner], seq_count), grad_down], axis=1
    )
    ff_sum = scatter_rows(ff_rows)

    down_parts = scattered_product(acted, weights_down)
    grad_two = scatter_parts(parts, (ff_rows, grad_down, down_parts[0]))
    grad_two = grad_two * gain_two
    grad_resid = grad_result_own + scale_two * (
        grad_two - norm_two * jnp.mean(grad_two * norm_two, axis=-1, keepdims=True)
    )

    grad_branch, grad_attended, terms, grad_gated, sums_mix = branch_back(
        gather_rows_low(grad_resid), weights_out, attended, mixed, z, scale_mix, gain_mix,
    )
    mean_mix = sum_head(sums_mix) / (MH * MP)
    down_parts = [pin(p, terms) for p in down_parts]

    out_rows = jnp.concatenate(
        [
            low(mul(gated, grad_branch, TN)).reshape(seq_count, mix_shard, features),
            low(mul(attended, grad_branch, TN)).reshape(seq_count, shard, features),
        ],
        axis=1,
    )
    out_sum = scatter_rows(out_rows)

    def back_step(k, grad_query, deps):
        return attend_back(
            place, query, grad_attended, logs, terms, pair[k], grad_query, k, deps=deps
        )

    grad_query, kept = back_step(blocks - 1, None, ())
    chain = shifted(kept, -1)
    grad_mixed, grad_z, leaving = gate_back(
        grad_gated, mixed, z, scale_mix, mean_mix, gain_mix, cums, reads, packed,
        deps=(grad_query,),
    )
    back_packs = send_packs(leaving, blocks, -1)
    for k in range(blocks - 2, 1, -1):
        grad_query, kept = back_step(k, grad_query, (leaving, out_rows))
        if k > 2:
            chain = shifted(add_low(kept, chain), -1)
    grad_pre, first, grad_taps, sums, grad_skip = mixer_backward(
        place, mix_in, tail, taps, heads, skip, starts, runs, incoming, grad_mixed, back_packs,
        deps=(grad_query, chain),
    )
    from_next = shifted(first, -1)
    chain = shifted(add_low(kept, pin(chain, from_next)), -1)
    grad_query, kept = back_step(1, grad_query, (sums,))
    grad_pre = fix_ends(place, grad_pre, from_next, taps)
    early_rows = weight_rows(normed, [grad_pre, grad_z], seq_count, deps=(grad_query,))
    early_sum = scatter_rows(early_rows)
    chain = shifted(add_low(kept, pin(chain, early_rows)), -1)
    grad_query, kept = back_step(0, grad_query, (early_rows,))
    chain = add_low(kept, chain)

    small_part = small_rows(
        place, grad_taps, sums, grad_skip, spots, shard, features, deps=(early_rows,)
    )
    late_rows = weight_rows(normed, [grad_query, chain], seq_count, extra=(small_part,))
    late_parts = scatter_direct(
        late_rows.reshape(seq_count, HEADS, shard, late_rows.shape[2]), core, block
    )
    parts = normed_back(
        place, grad_pre, grad_z, grad_query, chain, weights_in, deps=(late_rows,)
    )
    grad_normed = scatter_parts(parts) * gain_in
    result = (resid + scatter_parts(down_parts, (parts[0],))) * valid
    merged = merge_columns(
        place,
        late_parts,
        early_sum.reshape(HEADS, shard, -1),
        ff_sum.reshape(-1, shard, features),
    )
    pieces = [merged[0]] + [to_head(merged[m], m) for m in range(1, HEADS)]
    (
        grad_inputs, states, grad_steps, grad_queries, grad_gate, key_values, grad_ff_gate,
        grad_ff_up, grad_gain_in, grad_gain_two, grad_conv, *head_sums,
    ) = finish_columns(
        place, pieces,
        [
            mixer_inputs, state_weights, step_weight.T, query_weight, mixer_gate,
            key_value_weight, gate_weight, up_weight,
        ],
        [input_gain[None], second_gain[None]], conv_shard,
    )
    grad_hidden = grad_resid + scale_in * (
        grad_normed - unit_in * jnp.mean(grad_normed * unit_in, axis=-1, keepdims=True)
    )

    def back(x):
        x = x.reshape(2, own_rows, features)
        arrived = to_seq(x[1], 1)
        return jnp.stack(
            [jnp.where(core == 0, x[0], arrived), jnp.where(core == 0, arrived, x[0])]
        )[:, None]

    grad_mixer_output = out_sum[:mix_shard].astype(f32)

    grad_gain_mix = jnp.sum(mixer_output.astype(f32) * grad_mixer_output, axis=1)
    return (
        back(result),
        back(grad_hidden),
        grad_gain_in[0],
        grad_gate,
        grad_inputs,
        states,
        grad_conv.T,
        grad_steps.T,
        head_sums[0][0],
        head_sums[1][0],
        head_sums[2][0],
        grad_queries,
        key_values,
        grad_gain_mix / mixer_gain.astype(f32),
        grad_mixer_output,
        out_sum[mix_shard:].astype(f32),
        grad_gain_two[0],
        grad_ff_gate,
        grad_ff_up,
        ff_sum[HEADS * shard :].astype(f32),
    )


def solution(mesh):
    tokens = P(None, "seq", "head", None)
    split = P(("head", "seq"), None)
    line = P(("head", "seq"))
    whole = P()
    in_specs = (
        tokens, whole, tokens, line, split, split, split, split, split, whole, whole, whole,
        split, split, line, split, split, line, split, split, split,
    )
    out_specs = (
        tokens, tokens, line, split, split, split, split, split, whole, whole, whole, split,
        split, line, split, split, line, split, split, split,
    )
    return jax.shard_map(body, mesh=mesh, in_specs=in_specs, out_specs=out_specs, check_vma=False)
```
